128 devices in a mesh: ctx: 32 (over y_lo, z, x), shard: 4 (over y_hi, core).
Axes of the slice: x: 4, y: 4 (y_hi: 2, y_lo: 2; y = y_hi * 2 + y_lo), z: 4, core: 2. Of those that a mesh axis runs over, the one named last changes fastest.
Arguments:
- inputs: bfloat16 [8, 2048, 1024], P('shard', 'ctx'), may hold values from -6 to 6
- cotangent: bfloat16 [8, 2048, 1024], P('shard', 'ctx'), may hold values from -6 to 6
- w_qkv: bfloat16 [1024, 3072], P('shard'), may hold values from -0.1875 to 0.1875
- bias_qv: bfloat16 [2, 1024], P(None, 'shard'), may hold values from -3 to 3
- w_out: bfloat16 [1024, 1024], P('shard'), may hold values from -4 to 4
- bias_out: bfloat16 [1024], P('shard'), may hold values from -3 to 3
- ln1_gain: bfloat16 [1024], P('shard'), may hold values from 0.099609375 to 1.8984375
- ln1_bias: bfloat16 [1024], P('shard'), may hold values from -3 to 3
- w_in: bfloat16 [1024, 4096], P('shard'), may hold values from -0.1875 to 0.1875
- bias_in: bfloat16 [4096], P('shard'), may hold values from -3 to 3
- w_ff_out: bfloat16 [4096, 1024], P('shard'), may hold values from -0.09375 to 0.09375
- bias_ff_out: bfloat16 [1024], P('shard'), may hold values from -3 to 3
- ln2_gain: bfloat16 [1024], P('shard'), may hold values from 0.099609375 to 1.8984375
- ln2_bias: bfloat16 [1024], P('shard'), may hold values from -3 to 3
Outputs:
- result: bfloat16 [8, 2048, 1024], P('shard', 'ctx')
- grad_inputs: float32 [8, 2048, 1024], P('shard', 'ctx')
- grad_w_qkv: float32 [1024, 3072], P('shard')
- grad_bias_qv: float32 [2, 1024], P(None, 'shard')
- grad_w_out: float32 [1024, 1024], P('shard')
- grad_bias_out: float32 [1024], P('shard')
- grad_ln1_gain: float32 [1024], P('shard')
- grad_ln1_bias: float32 [1024], P('shard')
- grad_w_in: float32 [1024, 4096], P('shard')
- grad_bias_in: float32 [4096], P('shard')
- grad_w_ff_out: float32 [4096, 1024], P('shard')
- grad_bias_ff_out: float32 [1024], P('shard')
- grad_ln2_gain: float32 [1024], P('shard')
- grad_ln2_bias: float32 [1024], P('shard')
The draws below stay inside these ranges and needn't reach their ends.
All inputs are finite; a program needn't handle non-finite values.
Results may differ from the reference program's by a relative error of at most 0.03.
Values may be sent and summed in bfloat16 or wider, within the bound.
A program may use at most 192 MiB of HBM per device.

```python
import jax
import jax.numpy as jnp
from jax import lax

D = 1024
H = 16
DH = 64
FF = 4096
SEQ = 2048
SEQS = 8


def level_of(rng, extent, pieces, low, largest):
    factor_of, own = 1.0, jax.random.fold_in(rng, 6)
    for axis_at, blocks in pieces:
        heights = jnp.exp(jax.random.uniform(jax.random.fold_in(own, axis_at), (blocks,), jnp.float32, low / len(pieces), largest / len(pieces)))
        factor_of = factor_of * jnp.repeat(heights, extent[axis_at] // blocks).reshape([-1 if axis == axis_at else 1 for axis in range(len(extent))])
    return factor_of


def centred(stream_key, dims, deviation, most, split=(), kind=jnp.bfloat16):
    factor_of = level_of(stream_key, dims, split, -0.22, 0.18) if split else 1.0
    drawn = jax.random.normal(stream_key, dims, jnp.float32) * deviation * factor_of
    return jnp.minimum(jnp.maximum(drawn, -most), most).astype(kind)


def setup_inputs(seed: int = 0) -> dict:
    keys = jax.random.split(jax.random.key(seed), 15)
    return {
        "inputs": centred(keys[0], (SEQS, SEQ, D), 1.0, 6.0, ((0, 4), (1, 32))),
        "cotangent": centred(keys[1], (SEQS, SEQ, D), 1.0, 6.0, ((0, 4), (1, 32))),
        "w_qkv": centred(keys[2], (D, 3 * D), D ** -0.5, 0.1875, ((0, 4),)),
        "bias_qv": centred(keys[3], (2, D), 0.5, 3.0, ((1, 4),)),
        "w_out": centred(keys[4], (D, D), (max(1, 4 * D // SEQ)) ** -0.5, 4.0, ((0, 4),)),
        "bias_out": centred(keys[5], (D,), 0.5, 3.0, ((0, 4),)),
        "ln1_gain": jnp.clip(1.0 + 0.18 * jax.random.normal(keys[6], (D,), jnp.float32), 0.099609375, 1.8984375).astype(jnp.bfloat16),
        "ln1_bias": centred(keys[7], (D,), 0.5, 3.0, ((0, 4),)),
        "w_in": centred(keys[8], (D, FF), D ** -0.5, 0.1875, ((0, 4),)),
        "bias_in": centred(keys[9], (FF,), 0.5, 3.0, ((0, 4),)),
        "w_ff_out": centred(keys[10], (FF, D), FF ** -0.5, 0.09375, ((0, 4),)),
        "bias_ff_out": centred(keys[11], (D,), 0.5, 3.0, ((0, 4),)),
        "ln2_gain": jnp.clip(1.0 + 0.18 * jax.random.normal(keys[12], (D,), jnp.float32), 0.099609375, 1.8984375).astype(jnp.bfloat16),
        "ln2_bias": centred(keys[13], (D,), 0.5, 3.0, ((0, 4),)),
    }


NORM_EPS = 1e-05

@jax.custom_vjp
def low(v):
    return lax.optimization_barrier(v.astype(jnp.bfloat16)).astype(jnp.float32)

@jax.custom_vjp
def low_back(v):
    return v

def low_keep(v):
    return (low(v), None)

def low_pass(kept, grad):
    return (grad,)

def back_keep(v):
    return (v, None)

def back_low(kept, grad):
    return (low(grad),)
low.defvjp(low_keep, low_pass)
low_back.defvjp(back_keep, back_low)

def matmul(left, right):
    return jnp.dot(left, right, precision=lax.Precision.HIGHEST)

def layer_norm(values, norm_gain, norm_shift):
    row_mean = lax.optimization_barrier(jnp.mean(values, axis=-1, keepdims=True))
    centered = values - row_mean
    row_var = lax.optimization_barrier(jnp.mean(centered * centered, axis=-1, keepdims=True))
    return centered * lax.rsqrt(row_var + NORM_EPS) * norm_gain + norm_shift

def gelu_exact(values):
    return 0.5 * values * (1.0 + lax.erf(values * 0.7071067811865476))

def attend_rows(query_rows, key_rows, value_rows):
    scores = jnp.einsum('qhd,khd->qhk', query_rows, key_rows, precision=lax.Precision.HIGHEST)
    scores = low_back(scores * DH ** (-0.5))
    row_max = lax.optimization_barrier(jnp.max(scores, axis=-1, keepdims=True))
    expo = jnp.exp(scores - row_max)
    probs = low(expo / lax.optimization_barrier(jnp.sum(expo, axis=-1, keepdims=True)))
    return jnp.einsum('qhk,khd->qhd', probs, value_rows, precision=lax.Precision.HIGHEST)

def one_sequence(params, tokens_in):
    w_qkv, bias_qv, w_out, bias_out, gain_one, shift_one, w_in, bias_in, w_ff_out, bias_ff_out, gain_two, shift_two = params
    bias_full = jnp.concatenate([bias_qv[0], jnp.zeros((D,), jnp.float32), bias_qv[1]])
    projected = low_back(low(matmul(tokens_in, w_qkv) + bias_full))
    queries = projected[:, :D].reshape(SEQ, H, DH)
    key_rows = projected[:, D:2 * D].reshape(SEQ, H, DH)
    value_rows = projected[:, 2 * D:].reshape(SEQ, H, DH)
    block_rows = min(512, SEQ)
    query_blocks = queries.reshape(SEQ // block_rows, block_rows, H, DH)
    attend_block = jax.checkpoint(lambda rows_in: attend_rows(rows_in, key_rows, value_rows))
    context = lax.map(attend_block, query_blocks).reshape(SEQ, D)
    context = low_back(low(context))
    attended = low_back(matmul(context, w_out) + bias_out)
    hidden = layer_norm(tokens_in + attended, gain_one, shift_one)
    pre_act = low_back(matmul(low(hidden), w_in) + bias_in)
    act_low = low(gelu_exact(pre_act))
    branch = low_back(matmul(act_low, w_ff_out) + bias_ff_out)
    return layer_norm(hidden + branch, gain_two, shift_two)

def reference(inputs, cotangent, w_qkv, bias_qv, w_out, bias_out, ln1_gain, ln1_bias, w_in, bias_in, w_ff_out, bias_ff_out, ln2_gain, ln2_bias):
    params = (w_qkv.astype(jnp.float32), bias_qv.astype(jnp.float32), w_out.astype(jnp.float32), bias_out.astype(jnp.float32), ln1_gain.astype(jnp.float32), ln1_bias.astype(jnp.float32), w_in.astype(jnp.float32), bias_in.astype(jnp.float32), w_ff_out.astype(jnp.float32), bias_ff_out.astype(jnp.float32), ln2_gain.astype(jnp.float32), ln2_bias.astype(jnp.float32))
    inputs_f = inputs.astype(jnp.float32)
    upstream = cotangent.astype(jnp.float32)

    def forward(weights_all, sequences):

        def step_seq(carried, tokens_in):
            return (carried, one_sequence(weights_all, tokens_in))
        unused_carry, outputs = lax.scan(step_seq, jnp.zeros((), jnp.float32), sequences)
        return outputs
    outputs, pull_back = jax.vjp(forward, params, inputs_f)
    grads, grad_inputs = pull_back(upstream)
    return (outputs.astype(jnp.bfloat16), grad_inputs, grads[0], grads[1], grads[2], grads[3], grads[4], grads[5], grads[6], grads[7], grads[8], grads[9], grads[10], grads[11])
```

```python
import functools

import jax
import jax.numpy as jnp
from jax import lax
from jax.experimental import pallas as pl
from jax.experimental.pallas import tpu as pltpu
from jax.sharding import PartitionSpec as P

D = 1024
H = 16
DH = 64
FF = 4096
NC = 32
SCALE = DH ** (-0.5)
MESH = pl.DeviceIdType.MESH
NORM_EPS = 1e-05
VMEM_LIMIT = 56 * 1024 * 1024
VM = pl.BlockSpec(memory_space=pltpu.VMEM)
ANY = pl.BlockSpec(memory_space=pl.ANY)


def layer_norm(values, norm_gain, norm_shift):
    row_mean = jnp.mean(values, axis=-1, keepdims=True)
    centered = values - row_mean
    row_var = jnp.mean(centered * centered, axis=-1, keepdims=True)
    return centered * lax.rsqrt(row_var + NORM_EPS) * norm_gain + norm_shift


def gelu_exact(values):
    return 0.5 * values * (1.0 + lax.erf(values * 0.7071067811865476))


def outer_sum(left, right):
    return lax.dot_general(
        left, right, (((0,), (0,)), ((), ())), preferred_element_type=jnp.float32
    )


def times_transposed(left, right):
    return lax.dot_general(
        left, right, (((1,), (1,)), ((), ())), preferred_element_type=jnp.float32
    )


def pack_tokens(src, send, parts):
    def step(hp, carry):
        for g in range(2):
            for part in range(parts):
                cols = pl.ds(pl.multiple_of(part * D + hp * 128, 128), 128)
                a = src[pl.ds(g * 64, 32), cols]
                b = src[pl.ds(g * 64 + 32, 32), cols]
                rows = pl.ds(part * 32, 32)
                send[g * 16 + 2 * hp, rows, :] = jnp.concatenate([a[:, :64], b[:, :64]], axis=1)
                send[g * 16 + 2 * hp + 1, rows, :] = jnp.concatenate(
                    [a[:, 64:], b[:, 64:]], axis=1
                )
        return carry

    lax.fori_loop(0, H // 2, step, 0)


def unpack_tokens(recv, dst, parts):
    def step(hp, carry):
        for g in range(2):
            for part in range(parts):
                cols = pl.ds(pl.multiple_of(part * D + hp * 128, 128), 128)
                rows = pl.ds(part * 32, 32)
                even = recv[g * 16 + 2 * hp, rows, :]
                odd = recv[g * 16 + 2 * hp + 1, rows, :]
                dst[pl.ds(g * 64, 32), cols] = jnp.concatenate([even[:, :64], odd[:, :64]], axis=1)
                dst[pl.ds(g * 64 + 32, 32), cols] = jnp.concatenate(
                    [even[:, 64:], odd[:, 64:]], axis=1
                )
        return carry

    lax.fori_loop(0, H // 2, step, 0)


def a2a_start(send, recv, ssem, rsem, me):
    def step(k, carry):
        dest = lax.rem(me + k, NC)
        pltpu.make_async_remote_copy(
            src_ref=send.at[dest],
            dst_ref=recv.at[me],
            send_sem=ssem.at[k],
            recv_sem=rsem.at[k],
            device_id={"ctx": dest},
            device_id_type=MESH,
        ).start()
        return carry

    lax.fori_loop(1, NC, step, 0)


def a2a_wait(send, recv, ssem, rsem, me):
    def step(k, carry):
        source = lax.rem(me + NC - k, NC)
        copy = pltpu.make_async_remote_copy(
            src_ref=send.at[source],
            dst_ref=recv.at[source],
            send_sem=ssem.at[k],
            recv_sem=rsem.at[k],
            device_id={"ctx": source},
            device_id_type=MESH,
        )
        copy.wait_send()
        copy.wait_recv()
        return carry

    lax.fori_loop(1, NC, step, 0)


def signal_ctx_peers(barrier, me):
    def step(k, carry):
        pl.semaphore_signal(
            barrier, inc=1, device_id={"ctx": lax.rem(me + k, NC)}, device_id_type=MESH
        )
        return carry

    lax.fori_loop(1, NC, step, 0)


def halves(packed):
    return jnp.concatenate([packed[:, :64], packed[:, 64:]], axis=0)


def dot_nt(a, b):
    return lax.dot_general(a, b, (((1,), (1,)), ((), ())), preferred_element_type=jnp.float32)


def dot_nn(a, b):
    return jnp.dot(a, b, preferred_element_type=jnp.float32)


QB = 256


def attn_fwd_kernel(
    proj, ctx_out, qkv_out, o_out, lse_out, send, recv, send2, recv2, keys, vt, ssem, rsem, ssem2, rsem2
):
    me = lax.axis_index("ctx")
    barrier = pltpu.get_barrier_semaphore()
    signal_ctx_peers(barrier, me)
    pack_tokens(proj, send, 3)
    pl.semaphore_wait(barrier, NC - 1)
    a2a_start(send, recv, ssem, rsem, me)
    recv[me] = send[me]
    a2a_wait(send, recv, ssem, rsem, me)
    qkv_out[...] = recv[...]
    keys[...] = halves(recv[:, 32:64, :].reshape(1024, 128))
    vp = recv[:, 64:96, :].reshape(1024, 128).astype(jnp.float32).T.astype(jnp.bfloat16)
    vt[...] = jnp.concatenate([vp[:64], vp[64:]], axis=1)

    def step(i, carry):
        qp = recv[pl.ds(i * 8, 8), 0:32, :].reshape(QB, 128) * jnp.bfloat16(SCALE)
        s = dot_nt(keys[...], halves(qp))
        m = jnp.max(s, axis=0, keepdims=True)
        p = jnp.exp(s - m)
        total = jnp.sum(p, axis=0, keepdims=True)
        ot = dot_nn(vt[...], p.astype(jnp.bfloat16)) / total
        o = jnp.concatenate([ot[:, :QB], ot[:, QB:]], axis=0).T
        o_out[pl.ds(pl.multiple_of(i * QB, QB), QB), :] = o
        lse_out[i] = m + jnp.log(total)
        send2[pl.ds(i * 8, 8)] = o.astype(jnp.bfloat16).reshape(8, 32, 128)
        return carry

    lax.fori_loop(0, 4, step, 0)
    a2a_start(send2, recv2, ssem2, rsem2, me)
    recv2[me] = send2[me]
    a2a_wait(send2, recv2, ssem2, rsem2, me)
    unpack_tokens(recv2, ctx_out, 1)


def attn_fwd(projected):
    return pl.pallas_call(
        attn_fwd_kernel,
        out_shape=(
            jax.ShapeDtypeStruct((128, D), jnp.bfloat16),
            jax.ShapeDtypeStruct((NC, 96, 128), jnp.bfloat16),
            jax.ShapeDtypeStruct((1024, 128), jnp.float32),
            jax.ShapeDtypeStruct((4, 1, 2 * QB), jnp.float32),
        ),
        in_specs=[VM],
        out_specs=(VM, VM, VM, VM),
        scratch_shapes=[
            pltpu.VMEM((NC, 96, 128), jnp.bfloat16),
            pltpu.VMEM((NC, 96, 128), jnp.bfloat16),
            pltpu.VMEM((NC, 32, 128), jnp.bfloat16),
            pltpu.VMEM((NC, 32, 128), jnp.bfloat16),
            pltpu.VMEM((2048, DH), jnp.bfloat16),
            pltpu.VMEM((DH, 2048), jnp.bfloat16),
            pltpu.SemaphoreType.DMA((NC,)),
            pltpu.SemaphoreType.DMA((NC,)),
            pltpu.SemaphoreType.DMA((NC,)),
            pltpu.SemaphoreType.DMA((NC,)),
        ],
        compiler_params=pltpu.CompilerParams(
            collective_id=0, has_side_effects=True, vmem_limit_bytes=VMEM_LIMIT
        ),
    )(projected)


def group_ids():
    c = lax.axis_index("ctx")
    s = lax.axis_index("shard")
    core = lax.rem(s, 2)
    other = 2 - 2 * lax.div(s, 2)
    sibling = s + 1 - 2 * core
    cross_c = lax.rem(c + NC // 2, NC)
    return ((c, sibling), (cross_c, other + core), (cross_c, other + 1 - core))


def mesh_id(pair):
    return {"ctx": pair[0], "shard": pair[1]}


def attn_bwd_kernel(
    dctx, qkv, o_in, lse_in, act, dpre, datt, hid, dbr, ctx, xin,
    dproj_out, dproj_g, act_g, dpre_g, datt_g, hid_g, dbr_g, ctx_g, x_g,
    send, recv, send2, recv2, keys, kt, vals, dk, dv, dproj,
    ssem, rsem, ssem2, rsem2, xs, xr, fs, fr, ls, ps, pr, pls,
):
    me = lax.axis_index("ctx")
    shard = lax.axis_index("shard")
    peers = group_ids()
    barrier = pltpu.get_barrier_semaphore()
    signal_ctx_peers(barrier, me)
    for peer in peers:
        pl.semaphore_signal(barrier, inc=1, device_id=mesh_id(peer), device_id_type=MESH)
    pack_tokens(dctx, send, 1)
    pl.semaphore_wait(barrier, NC + 2)
    a2a_start(send, recv, ssem, rsem, me)

    def remote(src, dst, ssem_, rsem_, peer):
        copy = pltpu.make_async_remote_copy(
            src_ref=src, dst_ref=dst, send_sem=ssem_, recv_sem=rsem_,
            device_id=mesh_id(peer), device_id_type=MESH,
        )
        copy.start()
        return copy

    slices = ((act, act_g, 1024), (dpre, dpre_g, 1024), (datt, datt_g, 256))
    whole = ((hid, hid_g), (dbr, dbr_g), (ctx, ctx_g), (xin, x_g))
    pending, arriving = [], []
    for n, (src, dst) in enumerate(whole):
        pending.append(remote(src, dst.at[1], xs.at[n, 0], xr.at[n, 0], peers[0]))
        arriving.append(remote(src, dst.at[2], xs.at[n, 1], xr.at[n, 1], peers[1]))
        local = pltpu.make_async_copy(src, dst.at[0], ls.at[n])
        local.start()
        pending.append(local)
    for n, (src, dst, width) in enumerate(slices):
        for k, peer in enumerate(peers):
            cols = pl.ds(pl.multiple_of(peer[1] * width, width), width)
            pending.append(
                remote(src.at[:, cols], dst.at[k + 1], xs.at[4 + n, k], xr.at[4 + n, k], peer)
            )
        cols = pl.ds(pl.multiple_of(shard * width, width), width)
        local = pltpu.make_async_copy(src.at[:, cols], dst.at[0], ls.at[4 + n])
        local.start()
        pending.append(local)

    recv[me] = send[me]
    keys[...] = halves(qkv[:, 32:64, :].reshape(1024, 128))
    vals[...] = halves(qkv[:, 64:96, :].reshape(1024, 128))
    kp = qkv[:, 32:64, :].reshape(1024, 128).astype(jnp.float32).T.astype(jnp.bfloat16)
    kt[...] = jnp.concatenate([kp[:64], kp[64:]], axis=1)
    dk[...] = jnp.zeros_like(dk)
    dv[...] = jnp.zeros_like(dv)
    a2a_wait(send, recv, ssem, rsem, me)

    def step(i, carry):
        blocks = pl.ds(i * 8, 8)
        qb = halves(qkv[blocks, 0:32, :].reshape(QB, 128) * jnp.bfloat16(SCALE))
        dop = recv[blocks].reshape(QB, 128)
        o = o_in[pl.ds(pl.multiple_of(i * QB, QB), QB), :]
        prod = (dop.astype(jnp.float32) * o).T
        delta = jnp.concatenate(
            [
                jnp.sum(prod[:64], axis=0, keepdims=True),
                jnp.sum(prod[64:], axis=0, keepdims=True),
            ],
            axis=1,
        )
        dob = halves(dop)
        probs = jnp.exp(dot_nt(keys[...], qb) - lse_in[i])
        dv[...] += dot_nn(probs.astype(jnp.bfloat16), dob)
        ds = (probs * (dot_nt(vals[...], dob) - delta)).astype(jnp.bfloat16)
        dk[...] += dot_nn(ds, qb)
        dqt = dot_nn(kt[...], ds) * SCALE
        dq = jnp.concatenate([dqt[:, :QB], dqt[:, QB:]], axis=0).T
        send2[blocks, 0:32, :] = dq.astype(jnp.bfloat16).reshape(8, 32, 128)
        return carry

    lax.fori_loop(0, 4, step, 0)
    for n, total in enumerate((dk, dv)):
        packed = jnp.concatenate([total[0:1024, :], total[1024:2048, :]], axis=1)
        send2[:, 32 + 32 * n : 64 + 32 * n, :] = packed.astype(jnp.bfloat16).reshape(NC, 32, 128)
    a2a_start(send2, recv2, ssem2, rsem2, me)
    recv2[me] = send2[me]
    for n, (src, dst) in enumerate(whole):
        arriving[n].wait()
        pending.append(remote(dst.at[2], dst.at[3], fs.at[n], fr.at[n], peers[0]))
    a2a_wait(send2, recv2, ssem2, rsem2, me)
    unpack_tokens(recv2, dproj, 3)
    for k, peer in enumerate(peers):
        cols = pl.ds(pl.multiple_of(peer[1] * 768, 256), 768)
        pending.append(remote(dproj.at[:, cols], dproj_g.at[k + 1], ps.at[k], pr.at[k], peer))
    cols = pl.ds(pl.multiple_of(shard * 768, 256), 768)
    local = pltpu.make_async_copy(dproj.at[:, cols], dproj_g.at[0], pls.at[0])
    local.start()
    pending.append(local)
    local = pltpu.make_async_copy(dproj, dproj_out, pls.at[1])
    local.start()
    pending.append(local)
    for copy in pending:
        copy.wait()


def attn_bwd(dctx, qkv, o, lse, act, dpre, datt, hid, dbr, ctx, xin):
    bf = jnp.bfloat16
    sds = jax.ShapeDtypeStruct
    dma = pltpu.SemaphoreType.DMA
    return pl.pallas_call(
        attn_bwd_kernel,
        out_shape=(
            sds((128, 3 * D), bf), sds((4, 128, 768), bf), sds((4, 128, 1024), bf),
            sds((4, 128, 1024), bf), sds((4, 128, 256), bf), sds((4, 128, 1024), bf),
            sds((4, 128, 1024), bf), sds((4, 128, 1024), bf), sds((4, 128, 1024), bf),
        ),
        in_specs=[VM] * 4 + [ANY] * 7,
        out_specs=(ANY,) * 9,
        scratch_shapes=[
            pltpu.VMEM((NC, 32, 128), bf),
            pltpu.VMEM((NC, 32, 128), bf),
            pltpu.VMEM((NC, 96, 128), bf),
            pltpu.VMEM((NC, 96, 128), bf),
            pltpu.VMEM((2048, DH), bf),
            pltpu.VMEM((DH, 2048), bf),
            pltpu.VMEM((2048, DH), bf),
            pltpu.VMEM((2048, DH), jnp.float32),
            pltpu.VMEM((2048, DH), jnp.float32),
            pltpu.VMEM((128, 3 * D), bf),
            dma((NC,)), dma((NC,)), dma((NC,)), dma((NC,)),
            dma((7, 3)), dma((7, 3)), dma((4,)), dma((4,)), dma((7,)),
            dma((3,)), dma((3,)), dma((2,)),
        ],
        compiler_params=pltpu.CompilerParams(
            collective_id=1, has_side_effects=True, vmem_limit_bytes=VMEM_LIMIT
        ),
    )(dctx, qkv, o, lse, act, dpre, datt, hid, dbr, ctx, xin)


GW = (1024, 768, 256, 1024)
GO = (0, 1024, 1792, 2048)


def reduce_kernel(
    g_in, g_qkv, g_out, g_ff, cols_out, ff_out,
    recv0, recv1, recv2, recv3, red, redf, s0, r0, s1, r1, s2, r2, ls
):
    me = lax.axis_index("ctx")
    shard = lax.axis_index("shard")
    owner = lax.div(me, 8)
    barrier = pltpu.get_barrier_semaphore()
    signal_ctx_peers(barrier, me)

    def greet(k, carry):
        source_c = shard * 8 + lax.div(k, 3)
        source_s = lax.rem(shard + 1 + lax.rem(k, 3), 4)
        pl.semaphore_signal(
            barrier, inc=1, device_id={"ctx": source_c, "shard": source_s}, device_id_type=MESH
        )
        return carry

    lax.fori_loop(0, 24, greet, 0)
    pl.semaphore_wait(barrier, jnp.where(owner == shard, NC - 1, 2 * NC - 1))

    pieces = tuple(zip((g_in, g_qkv, g_out, g_ff), (recv0, recv1, recv2, recv3)))

    def rows_of(index, count=32):
        return pl.ds(pl.multiple_of(index * 32, 32), count)

    for n, (src, recv) in enumerate(pieces):

        def send(k, carry):
            dest = lax.rem(me + k, NC)
            pltpu.make_async_remote_copy(
                src_ref=src.at[rows_of(dest)], dst_ref=recv.at[me],
                send_sem=s0.at[n, k], recv_sem=r0.at[n, k],
                device_id={"ctx": dest}, device_id_type=MESH,
            ).start()
            return carry

        lax.fori_loop(1, NC, send, 0)
        pltpu.make_async_copy(src.at[rows_of(me)], recv.at[me], ls.at[n]).start()

    for n, (src, recv) in enumerate(pieces):
        pltpu.make_async_copy(src.at[rows_of(me)], recv.at[me], ls.at[n]).wait()

        def arrive(k, carry):
            source = lax.rem(me + NC - k, NC)
            copy = pltpu.make_async_remote_copy(
                src_ref=src.at[rows_of(source)], dst_ref=recv.at[source],
                send_sem=s0.at[n, k], recv_sem=r0.at[n, k],
                device_id={"ctx": source}, device_id_type=MESH,
            )
            copy.wait_send()
            copy.wait_recv()
            return carry

        lax.fori_loop(1, NC, arrive, 0)
        total = lax.fori_loop(
            0, NC, lambda k, acc: acc + recv[k].astype(jnp.float32),
            jnp.zeros((32, GW[n]), jnp.float32),
        )
        if n < 3:
            red[:, GO[n] : GO[n] + GW[n]] = total.astype(jnp.bfloat16)
        else:
            redf[...] = total.astype(jnp.bfloat16)
        if n == 2:
            place = cols_out.at[
                rows_of(lax.rem(me, 8)), pl.ds(pl.multiple_of(shard * 2048, 2048), 2048)
            ]
            index = lax.rem(me, 8) * 4 + shard

            def spread(k, carry):
                dest = lax.rem(me + k, NC)

                @pl.when(jnp.logical_or(k > 0, owner != shard))
                def _():
                    pltpu.make_async_remote_copy(
                        src_ref=red, dst_ref=place, send_sem=s1.at[k], recv_sem=r1.at[index],
                        device_id={"ctx": dest, "shard": owner}, device_id_type=MESH,
                    ).start()

                return carry

            lax.fori_loop(0, NC, spread, 0)

            @pl.when(owner == shard)
            def _():
                local = pltpu.make_async_copy(red, place, ls.at[4])
                local.start()
                local.wait()

    def spread_ff(k, carry):
        dest = lax.rem(me + k, NC)
        pltpu.make_async_remote_copy(
            src_ref=redf, dst_ref=ff_out.at[rows_of(me)], send_sem=s2.at[k], recv_sem=r2.at[k],
            device_id={"ctx": dest}, device_id_type=MESH,
        ).start()
        return carry

    lax.fori_loop(1, NC, spread_ff, 0)
    local = pltpu.make_async_copy(redf, ff_out.at[rows_of(me)], ls.at[5])
    local.start()
    local.wait()

    def finish(k, carry):
        source = lax.rem(me + NC - k, NC)
        copy = pltpu.make_async_remote_copy(
            src_ref=redf, dst_ref=ff_out.at[rows_of(source)], send_sem=s2.at[k], recv_sem=r2.at[k],
            device_id={"ctx": source}, device_id_type=MESH,
        )
        copy.wait_send()
        copy.wait_recv()
        return carry

    lax.fori_loop(1, NC, finish, 0)

    def finish_cols(k, carry):
        source_c = shard * 8 + lax.div(k, 4)
        source_s = lax.rem(k, 4)
        copy = pltpu.make_async_remote_copy(
            src_ref=red,
            dst_ref=cols_out.at[
                rows_of(lax.div(k, 4)), pl.ds(pl.multiple_of(source_s * 2048, 2048), 2048)
            ],
            send_sem=s1.at[k], recv_sem=r1.at[k],
            device_id={"ctx": source_c, "shard": source_s}, device_id_type=MESH,
        )

        @pl.when(jnp.logical_or(k > 0, owner != shard))
        def _():
            copy.wait_send()

        @pl.when(jnp.logical_or(source_c != me, source_s != shard))
        def _():
            copy.wait_recv()

        return carry

    lax.fori_loop(0, NC, finish_cols, 0)


def reduce_grads(g_in, g_qkv, g_out, g_ff):
    bf = jnp.bfloat16
    dma = pltpu.SemaphoreType.DMA
    return pl.pallas_call(
        reduce_kernel,
        out_shape=(
            jax.ShapeDtypeStruct((256, 4 * 2048), bf),
            jax.ShapeDtypeStruct((1024, 1024), bf),
        ),
        in_specs=[ANY] * 4,
        out_specs=(ANY, ANY),
        scratch_shapes=[pltpu.VMEM((NC, 32, w), bf) for w in GW]
        + [
            pltpu.VMEM((32, 2048), bf),
            pltpu.VMEM((32, 1024), bf),
            dma((4, NC)), dma((4, NC)), dma((NC,)), dma((NC,)), dma((NC,)), dma((NC,)), dma((6,)),
        ],
        compiler_params=pltpu.CompilerParams(
            collective_id=2, has_side_effects=True, vmem_limit_bytes=VMEM_LIMIT
        ),
    )(g_in, g_qkv, g_out, g_ff)


def local(
    inputs, cotangent, w_qkv, bias_qv, w_out, bias_out, ln1_gain, ln1_bias, w_in, bias_in,
    w_ff_out, bias_ff_out, ln2_gain, ln2_bias,
):
    bf, f32 = jnp.bfloat16, jnp.float32
    shard = lax.axis_index("shard")
    small = jnp.concatenate(
        [
            bias_qv.reshape(512), bias_out, ln1_gain, ln1_bias, bias_ff_out, ln2_gain, ln2_bias,
            bias_in,
        ]
    )
    small_all = lax.all_gather(small, "shard", axis=0).astype(f32)
    w_qkv_all = lax.all_gather(w_qkv, "shard", axis=0, tiled=True)
    w_out_all = lax.all_gather(w_out, "shard", axis=0, tiled=True)
    w_in_all = lax.all_gather(w_in, "shard", axis=0, tiled=True)
    w_ff_all = lax.all_gather(w_ff_out, "shard", axis=0, tiled=True)
    bias_q, bias_v, bias_o, gain_one, shift_one, bias_ff, gain_two, shift_two = (
        small_all[:, 256 * k : 256 * k + 256].reshape(D) for k in range(8)
    )
    bias_i = small_all[:, 2048:].reshape(FF)
    groups, rows_dev = inputs.shape[0], inputs.shape[1]
    token_count = groups * rows_dev
    tokens_in = inputs.reshape(token_count, D)
    bias_full = jnp.concatenate([bias_q, jnp.zeros((D,), f32), bias_v])
    projected = (jnp.dot(tokens_in, w_qkv_all, preferred_element_type=f32) + bias_full).astype(bf)
    flat_context, qkv, o, lse = attn_fwd(projected)
    attended = jnp.dot(flat_context, w_out_all, preferred_element_type=f32) + bias_o
    first_sum = tokens_in.astype(f32) + attended
    hidden = layer_norm(first_sum, gain_one, shift_one)
    hidden_low = hidden.astype(bf)
    pre_act = jnp.dot(hidden_low, w_in_all, preferred_element_type=f32) + bias_i
    act_low = gelu_exact(pre_act).astype(bf)
    branch = jnp.dot(act_low, w_ff_all, preferred_element_type=f32) + bias_ff
    second_sum = hidden + branch
    result_rows = layer_norm(second_sum, gain_two, shift_two)
    upstream = cotangent.reshape(token_count, D).astype(f32)
    unused_two, pull_two = jax.vjp(layer_norm, second_sum, gain_two, shift_two)
    d_second, d_gain_two, d_shift_two = pull_two(upstream)
    d_branch = d_second.astype(bf)
    grad_bias_ff = jnp.sum(d_branch.astype(f32), axis=0)
    d_act = times_transposed(d_branch, w_ff_all)
    unused_act, pull_gelu = jax.vjp(gelu_exact, pre_act)
    d_pre_act = pull_gelu(d_act)[0].astype(bf)
    grad_bias_in = jnp.sum(d_pre_act.astype(f32), axis=0)
    d_hidden = d_second + times_transposed(d_pre_act, w_in_all)
    unused_one, pull_one = jax.vjp(layer_norm, first_sum, gain_one, shift_one)
    d_first, d_gain_one, d_shift_one = pull_one(d_hidden)
    d_attended = d_first.astype(bf)
    grad_bias_out = jnp.sum(d_attended.astype(f32), axis=0)
    d_context = times_transposed(d_attended, w_out_all).astype(bf)
    sums = lax.psum(
        jnp.concatenate(
            [
                grad_bias_out, d_gain_one, d_shift_one, grad_bias_ff, d_gain_two, d_shift_two,
                grad_bias_in,
            ]
        ),
        ("ctx", "shard"),
    )
    d_projected, dproj_g, act_g, dpre_g, datt_g, hid_g, dbr_g, ctx_g, x_g = attn_bwd(
        d_context, qkv, o, lse, act_low, d_pre_act, d_attended, hidden_low, d_branch,
        flat_context, tokens_in,
    )
    column_sums = jnp.sum(d_projected.astype(f32), axis=0)
    sums_qv = lax.psum(
        jnp.concatenate([column_sums[:D], column_sums[2 * D :]]), ("ctx", "shard")
    )

    def flat(a):
        return a.reshape(512, a.shape[-1])

    g_in = outer_sum(flat(hid_g), flat(dpre_g)).astype(bf)
    g_ff = outer_sum(flat(act_g), flat(dbr_g)).astype(bf)
    g_out = outer_sum(flat(ctx_g), flat(datt_g)).astype(bf)
    g_qkv = outer_sum(flat(x_g), flat(dproj_g)).astype(bf)
    cols, own_ff = reduce_grads(g_in, g_qkv, g_out, g_ff)
    cols = cols.reshape(256, 4, 2048)
    own_in = cols[:, :, :1024].reshape(256, FF).astype(f32)
    own_qkv = cols[:, :, 1024:1792].reshape(256, 3 * D).astype(f32)
    own_out = cols[:, :, 1792:].reshape(256, D).astype(f32)
    d_inputs = d_first + times_transposed(d_projected, w_qkv_all)

    def own(k):
        return lax.dynamic_slice_in_dim(sums[k * D : (k + 1) * D], shard * 256, 256)

    own_bias_in = lax.dynamic_slice_in_dim(sums[6 * D :], shard * 1024, 1024)
    own_bias_qv = lax.dynamic_slice_in_dim(sums_qv.reshape(2, D), shard * 256, 256, 1)
    return (
        result_rows.astype(bf).reshape(groups, rows_dev, D),
        d_inputs.reshape(groups, rows_dev, D),
        own_qkv,
        own_bias_qv,
        own_out,
        own(0),
        own(1),
        own(2),
        own_in,
        own_bias_in,
        own_ff.astype(f32),
        own(3),
        own(4),
        own(5),
    )


def solution(mesh):
    specs = (
        P("shard", "ctx", None),
        P("shard", "ctx", None),
        P("shard", None),
        P(None, "shard"),
        P("shard", None),
        P("shard"),
        P("shard"),
        P("shard"),
        P("shard", None),
        P("shard"),
        P("shard", None),
        P("shard"),
        P("shard"),
        P("shard"),
    )
    return jax.shard_map(local, mesh=mesh, in_specs=specs, out_specs=specs, check_vma=False)
```

```python
import functools

import jax
import jax.numpy as jnp
from jax import lax
from jax.experimental import pallas as pl
from jax.experimental.pallas import tpu as pltpu
from jax.sharding import PartitionSpec as P

D = 1024
H = 16
DH = 64
FF = 4096
NC = 32
SCALE = DH ** (-0.5)
MESH = pl.DeviceIdType.MESH
NORM_EPS = 1e-05
VMEM_LIMIT = 56 * 1024 * 1024
VM = pl.BlockSpec(memory_space=pltpu.VMEM)
ANY = pl.BlockSpec(memory_space=pl.ANY)


def layer_norm(values, norm_gain, norm_shift):
    row_mean = jnp.mean(values, axis=-1, keepdims=True)
    centered = values - row_mean
    row_var = jnp.mean(centered * centered, axis=-1, keepdims=True)
    return centered * lax.rsqrt(row_var + NORM_EPS) * norm_gain + norm_shift


def gelu_exact(values):
    return 0.5 * values * (1.0 + lax.erf(values * 0.7071067811865476))


def outer_sum(left, right):
    return lax.dot_general(
        left, right, (((0,), (0,)), ((), ())), preferred_element_type=jnp.float32
    )


def times_transposed(left, right):
    return lax.dot_general(
        left, right, (((1,), (1,)), ((), ())), preferred_element_type=jnp.float32
    )


def pack_tokens(src, send, parts):
    def step(hp, carry):
        for g in range(2):
            for part in range(parts):
                cols = pl.ds(pl.multiple_of(part * D + hp * 128, 128), 128)
                a = src[pl.ds(g * 64, 32), cols]
                b = src[pl.ds(g * 64 + 32, 32), cols]
                rows = pl.ds(part * 32, 32)
                send[g * 16 + 2 * hp, rows, :] = jnp.concatenate([a[:, :64], b[:, :64]], axis=1)
                send[g * 16 + 2 * hp + 1, rows, :] = jnp.concatenate(
                    [a[:, 64:], b[:, 64:]], axis=1
                )
        return carry

    lax.fori_loop(0, H // 2, step, 0)


def unpack_tokens(recv, dst, parts):
    def step(hp, carry):
        for g in range(2):
            for part in range(parts):
                cols = pl.ds(pl.multiple_of(part * D + hp * 128, 128), 128)
                rows = pl.ds(part * 32, 32)
                even = recv[g * 16 + 2 * hp, rows, :]
                odd = recv[g * 16 + 2 * hp + 1, rows, :]
                dst[pl.ds(g * 64, 32), cols] = jnp.concatenate([even[:, :64], odd[:, :64]], axis=1)
                dst[pl.ds(g * 64 + 32, 32), cols] = jnp.concatenate(
                    [even[:, 64:], odd[:, 64:]], axis=1
                )
        return carry

    lax.fori_loop(0, H // 2, step, 0)


def a2a_start(send, recv, ssem, rsem, me):
    def step(k, carry):
        dest = lax.rem(me + k, NC)
        pltpu.make_async_remote_copy(
            src_ref=send.at[dest],
            dst_ref=recv.at[me],
            send_sem=ssem.at[k],
            recv_sem=rsem.at[k],
            device_id={"ctx": dest},
            device_id_type=MESH,
        ).start()
        return carry

    lax.fori_loop(1, NC, step, 0)


def a2a_wait(send, recv, ssem, rsem, me):
    def step(k, carry):
        source = lax.rem(me + NC - k, NC)
        copy = pltpu.make_async_remote_copy(
            src_ref=send.at[source],
            dst_ref=recv.at[source],
            send_sem=ssem.at[k],
            recv_sem=rsem.at[k],
            device_id={"ctx": source},
            device_id_type=MESH,
        )
        copy.wait_send()
        copy.wait_recv()
        return carry

    lax.fori_loop(1, NC, step, 0)


def signal_ctx_peers(barrier, me):
    def step(k, carry):
        pl.semaphore_signal(
            barrier, inc=1, device_id={"ctx": lax.rem(me + k, NC)}, device_id_type=MESH
        )
        return carry

    lax.fori_loop(1, NC, step, 0)


def halves(packed):
    return jnp.concatenate([packed[:, :64], packed[:, 64:]], axis=0)


def dot_nt(a, b):
    return lax.dot_general(a, b, (((1,), (1,)), ((), ())), preferred_element_type=jnp.float32)


def dot_nn(a, b):
    return jnp.dot(a, b, preferred_element_type=jnp.float32)


def place():
    c = lax.axis_index("ctx")
    return c, lax.axis_index("shard"), lax.div(c, 16), lax.rem(lax.div(c, 4), 4), lax.rem(c, 4)


def remote(src, dst, send_sem, recv_sem, peer):
    return pltpu.make_async_remote_copy(
        src_ref=src, dst_ref=dst, send_sem=send_sem, recv_sem=recv_sem,
        device_id=peer, device_id_type=MESH,
    )


def send(src, dst, send_sem, recv_sem, peer):
    copy = remote(src, dst, send_sem, recv_sem, peer)
    copy.start()
    return copy


def rings():
    c, unused_s, y, z, x = place()
    along_x = (
        x,
        {"ctx": c - x + lax.rem(x + 1, 4)},
        {"ctx": c - x + lax.rem(x + 3, 4)},
    )
    along_z = (
        z,
        {"ctx": y * 16 + lax.rem(z + 1, 4) * 4 + x},
        {"ctx": y * 16 + lax.rem(z + 3, 4) * 4 + x},
    )
    return along_x, along_z


class RingGather:
    def __init__(self, block, first, second, ring, ssem, rsem):
        self.block, self.first, self.second = block, first, second
        self.p, self.up, self.down = ring
        self.ssem, self.rsem = ssem, rsem

    def at(self, k):
        return lax.rem(self.p + k, 4)

    def start(self):
        own = self.block(self.p)
        self.sent = [
            send(own, own, self.ssem(0), self.rsem(0), self.up),
            send(own, own, self.ssem(1), self.rsem(1), self.down),
        ]

    def forward(self):
        from_down, from_up = self.block(self.at(3)), self.block(self.at(1))
        remote(from_down, from_down, self.ssem(0), self.rsem(0), self.up).wait_recv()
        part = self.first(self.at(3))
        self.sent.append(send(part, part, self.ssem(2), self.rsem(2), self.up))
        remote(from_up, from_up, self.ssem(1), self.rsem(1), self.down).wait_recv()
        part = self.second(self.at(1))
        self.sent.append(send(part, part, self.ssem(3), self.rsem(3), self.down))

    def finish(self):
        part = self.first(self.at(2))
        remote(part, part, self.ssem(2), self.rsem(2), self.up).wait_recv()
        part = self.second(self.at(2))
        remote(part, part, self.ssem(3), self.rsem(3), self.down).wait_recv()
        for copy in self.sent:
            copy.wait_send()


def sems(ref, *lead):
    return lambda k: ref.at[(*lead, k)]


def rows16(index):
    return pl.ds(pl.multiple_of(index * 16, 16), 16)


def rows64(index):
    return pl.ds(pl.multiple_of(index * 64, 64), 64)


class WeightGather:
    STEPS = 7

    def __init__(self, src, dst, n, ls, os, orr, cs, cr, gs, gr, fs, fr):
        c, s, y, z, x = place()
        sibling, cross, unused = group_ids()
        self.sibling, self.cross = mesh_id(sibling), mesh_id(cross)
        self.src, self.dst, self.s = src, dst, s
        self.far, self.far_sib = cross[1], unused[1]
        self.sib_shard = sibling[1]
        self.ls, self.os, self.orr = ls.at[n], os.at[n], orr.at[n]
        self.cs, self.cr, self.fs, self.fr = cs, cr, fs, fr
        self.n = n
        width = src.shape[-1]
        self.half, self.quarter = width // 2, width // 4
        along_x, along_z = rings()
        self.streams = []
        for h in range(2):
            one, two = (along_z, along_x) if h == 0 else (along_x, along_z)
            base = x if h == 0 else z
            cols = pl.ds(h * self.half, self.half)
            cols_a = pl.ds(h * self.half, self.quarter)
            cols_b = pl.ds(h * self.half + self.quarter, self.quarter)
            own = self.dst.at[self.far]

            def small_block(p, cols=cols, base=base, own=own):
                return own.at[:, rows16(base * 4 + p), cols]

            def big_block(p, cols=cols, own=own):
                return own.at[:, rows64(p), cols]

            def part_of(make, cols):
                return lambda p: make(p, cols=cols)

            ring1 = RingGather(
                small_block, part_of(small_block, cols_a), part_of(small_block, cols_b), one,
                sems(gs, n, h, 0), sems(gr, n, h, 0),
            )
            ring2 = RingGather(
                big_block, part_of(big_block, cols_a), part_of(big_block, cols_b), two,
                sems(gs, n, h, 1), sems(gr, n, h, 1),
            )
            row = base * 4 + one[0]
            self.streams.append((h, row, cols, cols_a, cols_b, ring1, ring2, two[0]))
        self.sent = []

    def step(self, k):
        if k == 0:
            for h, row, cols, *unused in self.streams:
                self.sent.append(
                    send(
                        self.src.at[:, rows16(row), cols],
                        self.dst.at[self.s].at[:, rows16(row), cols],
                        self.cs.at[self.n, h], self.cr.at[self.n, h], self.cross,
                    )
                )
            self.local = pltpu.make_async_copy(self.src, self.dst.at[self.s], self.ls)
            self.local.start()
            self.own = send(self.src, self.dst.at[self.s], self.os, self.orr, self.sibling)
        elif k == 1:
            for h, row, cols, cols_a, cols_b, ring1, ring2, p in self.streams:
                got = self.dst.at[self.far].at[:, rows16(row), cols]
                remote(got, got, self.cs.at[self.n, h], self.cr.at[self.n, h], self.cross).wait_recv()
                ring1.start()
        elif k == 2:
            for h, row, cols, cols_a, cols_b, ring1, ring2, p in self.streams:
                ring1.forward()
        elif k == 3:
            for h, row, cols, cols_a, cols_b, ring1, ring2, p in self.streams:
                ring1.finish()
                ring2.start()
                self.pass_on(h, 0, rows64(p), cols)
        elif k == 4:
            for h, row, cols, cols_a, cols_b, ring1, ring2, p in self.streams:
                ring2.forward()
                self.pass_on(h, 1, rows64(lax.rem(p + 3, 4)), cols)
                self.pass_on(h, 2, rows64(lax.rem(p + 1, 4)), cols)
        elif k == 5:
            for h, row, cols, cols_a, cols_b, ring1, ring2, p in self.streams:
                ring2.finish()
                self.pass_on(h, 3, rows64(lax.rem(p + 2, 4)), cols)
        else:
            self.local.wait()
            self.own.wait_send()
            got = self.dst.at[self.sib_shard]
            remote(got, got, self.os, self.orr, self.sibling).wait_recv()
            for h, row, cols, cols_a, cols_b, ring1, ring2, p in self.streams:
                for j, shift in enumerate((0, 3, 1, 2)):
                    got = self.dst.at[self.far_sib].at[:, rows64(lax.rem(p + shift, 4)), cols]
                    remote(
                        got, got, self.fs.at[self.n, h, j], self.fr.at[self.n, h, j], self.sibling
                    ).wait_recv()
            for copy in self.sent:
                copy.wait_send()

    def pass_on(self, h, j, rows, cols):
        part = self.dst.at[self.far].at[:, rows, cols]
        self.sent.append(
            send(part, part, self.fs.at[self.n, h, j], self.fr.at[self.n, h, j], self.sibling)
        )


def weight_sems(count):
    dma = pltpu.SemaphoreType.DMA
    return [
        dma((count,)), dma((count,)), dma((count,)), dma((count, 2)), dma((count, 2)),
        dma((count, 2, 2, 4)), dma((count, 2, 2, 4)), dma((count, 2, 4)), dma((count, 2, 4)),
    ]


def group_ids():
    c = lax.axis_index("ctx")
    s = lax.axis_index("shard")
    core = lax.rem(s, 2)
    other = 2 - 2 * lax.div(s, 2)
    sibling = s + 1 - 2 * core
    cross_c = lax.rem(c + NC // 2, NC)
    return ((c, sibling), (cross_c, other + core), (cross_c, other + 1 - core))


def mesh_id(pair):
    return {"ctx": pair[0], "shard": pair[1]}


def first_kernel(w, small, w_all, small_all, ls, os, orr, cs, cr, gs, gr, fs, fr, ss, sr, sl):
    unused_c, s, *unused = place()
    peers = [mesh_id(peer) for peer in group_ids()]
    around = [ring[k] for ring in rings() for k in (1, 2)]
    barrier = pltpu.get_barrier_semaphore()
    for peer in peers + around:
        pl.semaphore_signal(barrier, inc=1, device_id=peer, device_id_type=MESH)
    pl.semaphore_wait(barrier, len(peers) + len(around))
    gather = WeightGather(w, w_all, 0, ls, os, orr, cs, cr, gs, gr, fs, fr)
    gather.step(0)
    pending = [
        send(small, small_all.at[s], ss.at[k], sr.at[k], peer) for k, peer in enumerate(peers)
    ]
    own = pltpu.make_async_copy(small, small_all.at[s], sl)
    own.start()
    for k in range(1, WeightGather.STEPS):
        gather.step(k)
    own.wait()
    for k, peer in enumerate(group_ids()):
        pending[k].wait_send()
        got = small_all.at[peer[1]]
        remote(got, got, ss.at[k], sr.at[k], peers[k]).wait_recv()


def gather_first(w, small):
    dma = pltpu.SemaphoreType.DMA
    return pl.pallas_call(
        first_kernel,
        out_shape=(
            jax.ShapeDtypeStruct((4, *w.shape), w.dtype),
            jax.ShapeDtypeStruct((4, *small.shape), small.dtype),
        ),
        in_specs=[ANY, ANY],
        out_specs=(ANY, ANY),
        scratch_shapes=weight_sems(1) + [dma((3,)), dma((3,)), dma],
        compiler_params=pltpu.CompilerParams(collective_id=3, has_side_effects=True),
    )(w, small)


QB = 256


def attn_fwd_kernel(
    proj, w0, w1, w2, ctx_out, qkv_out, o_out, lse_out, all0, all1, all2,
    send, recv, send2, recv2, keys, vt, ssem, rsem, ssem2, rsem2, *wsems
):
    me = lax.axis_index("ctx")
    barrier = pltpu.get_barrier_semaphore()
    signal_ctx_peers(barrier, me)
    for peer in group_ids()[:2]:
        pl.semaphore_signal(barrier, inc=1, device_id=mesh_id(peer), device_id_type=MESH)
    pack_tokens(proj, send, 3)
    pl.semaphore_wait(barrier, NC + 1)
    a2a_start(send, recv, ssem, rsem, me)
    gathers = [
        WeightGather(w, out, n, *wsems)
        for n, (w, out) in enumerate(((w0, all0), (w1, all1), (w2, all2)))
    ]

    def advance(k):
        for gather in gathers:
            gather.step(k)

    advance(0)
    recv[me] = send[me]
    a2a_wait(send, recv, ssem, rsem, me)
    qkv_out[...] = recv[...]
    keys[...] = halves(recv[:, 32:64, :].reshape(1024, 128))
    vp = recv[:, 64:96, :].reshape(1024, 128).astype(jnp.float32).T.astype(jnp.bfloat16)
    vt[...] = jnp.concatenate([vp[:64], vp[64:]], axis=1)
    advance(1)

    def step(i, carry):
        qp = recv[pl.ds(i * 8, 8), 0:32, :].reshape(QB, 128) * jnp.bfloat16(SCALE)
        s = dot_nt(keys[...], halves(qp))
        m = jnp.max(s, axis=0, keepdims=True)
        p = jnp.exp(s - m)
        total = jnp.sum(p, axis=0, keepdims=True)
        ot = dot_nn(vt[...], p.astype(jnp.bfloat16)) / total
        o = jnp.concatenate([ot[:, :QB], ot[:, QB:]], axis=0).T
        o_out[pl.ds(pl.multiple_of(i * QB, QB), QB), :] = o
        lse_out[i] = m + jnp.log(total)
        send2[pl.ds(i * 8, 8)] = o.astype(jnp.bfloat16).reshape(8, 32, 128)
        return carry

    lax.fori_loop(0, 1, step, 0)
    advance(2)
    lax.fori_loop(1, 2, step, 0)
    advance(3)
    lax.fori_loop(2, 4, step, 0)
    a2a_start(send2, recv2, ssem2, rsem2, me)
    recv2[me] = send2[me]
    advance(4)
    a2a_wait(send2, recv2, ssem2, rsem2, me)
    unpack_tokens(recv2, ctx_out, 1)
    advance(5)
    advance(6)


def attn_fwd(projected, w_out, w_in, w_ff):
    return pl.pallas_call(
        attn_fwd_kernel,
        out_shape=(
            jax.ShapeDtypeStruct((128, D), jnp.bfloat16),
            jax.ShapeDtypeStruct((NC, 96, 128), jnp.bfloat16),
            jax.ShapeDtypeStruct((1024, 128), jnp.float32),
            jax.ShapeDtypeStruct((4, 1, 2 * QB), jnp.float32),
        )
        + tuple(jax.ShapeDtypeStruct((4, *w.shape), w.dtype) for w in (w_out, w_in, w_ff)),
        in_specs=[VM, ANY, ANY, ANY],
        out_specs=(VM, VM, VM, VM, ANY, ANY, ANY),
        scratch_shapes=[
            pltpu.VMEM((NC, 96, 128), jnp.bfloat16),
            pltpu.VMEM((NC, 96, 128), jnp.bfloat16),
            pltpu.VMEM((NC, 32, 128), jnp.bfloat16),
            pltpu.VMEM((NC, 32, 128), jnp.bfloat16),
            pltpu.VMEM((2048, DH), jnp.bfloat16),
            pltpu.VMEM((DH, 2048), jnp.bfloat16),
            pltpu.SemaphoreType.DMA((NC,)),
            pltpu.SemaphoreType.DMA((NC,)),
            pltpu.SemaphoreType.DMA((NC,)),
            pltpu.SemaphoreType.DMA((NC,)),
        ]
        + weight_sems(3),
        compiler_params=pltpu.CompilerParams(
            collective_id=0, has_side_effects=True, vmem_limit_bytes=VMEM_LIMIT
        ),
    )(projected, w_out, w_in, w_ff)


def attn_bwd_kernel(
    dctx, qkv, o_in, lse_in, small_in, act, dpre, datt, hid, dbr, ctx, xin,
    dproj_out, dproj_g, act_g, dpre_g, datt_g, hid_g, dbr_g, ctx_g, x_g, small_g,
    send, recv, send2, recv2, keys, kt, vals, dk, dv, dproj, small,
    ssem, rsem, ssem2, rsem2, xs, xr, fs, fr, ls, ps, pr, pls,
):
    me = lax.axis_index("ctx")
    shard = lax.axis_index("shard")
    peers = group_ids()
    barrier = pltpu.get_barrier_semaphore()
    signal_ctx_peers(barrier, me)
    for peer in peers:
        pl.semaphore_signal(barrier, inc=1, device_id=mesh_id(peer), device_id_type=MESH)
    pack_tokens(dctx, send, 1)
    pl.semaphore_wait(barrier, NC + 2)
    a2a_start(send, recv, ssem, rsem, me)

    def to_peer(src, dst, ssem_, rsem_, peer):
        copy = remote(src, dst, ssem_, rsem_, mesh_id(peer))
        copy.start()
        return copy

    slices = ((act, act_g, 1024), (dpre, dpre_g, 1024), (datt, datt_g, 256))
    whole = ((hid, hid_g), (dbr, dbr_g), (ctx, ctx_g), (xin, x_g))
    pending, arriving = [], []
    for n, (src, dst) in enumerate(whole):
        pending.append(to_peer(src, dst.at[1], xs.at[n, 0], xr.at[n, 0], peers[0]))
        arriving.append(to_peer(src, dst.at[2], xs.at[n, 1], xr.at[n, 1], peers[1]))
        local = pltpu.make_async_copy(src, dst.at[0], ls.at[n])
        local.start()
        pending.append(local)
    for n, (src, dst, width) in enumerate(slices):
        for k, peer in enumerate(peers):
            cols = pl.ds(pl.multiple_of(peer[1] * width, width), width)
            pending.append(
                to_peer(src.at[:, cols], dst.at[k + 1], xs.at[4 + n, k], xr.at[4 + n, k], peer)
            )
        cols = pl.ds(pl.multiple_of(shard * width, width), width)
        local = pltpu.make_async_copy(src.at[:, cols], dst.at[0], ls.at[4 + n])
        local.start()
        pending.append(local)

    recv[me] = send[me]
    keys[...] = halves(qkv[:, 32:64, :].reshape(1024, 128))
    vals[...] = halves(qkv[:, 64:96, :].reshape(1024, 128))
    kp = qkv[:, 32:64, :].reshape(1024, 128).astype(jnp.float32).T.astype(jnp.bfloat16)
    kt[...] = jnp.concatenate([kp[:64], kp[64:]], axis=1)
    dk[...] = jnp.zeros_like(dk)
    dv[...] = jnp.zeros_like(dv)
    a2a_wait(send, recv, ssem, rsem, me)

    def step(i, carry):
        blocks = pl.ds(i * 8, 8)
        qb = halves(qkv[blocks, 0:32, :].reshape(QB, 128) * jnp.bfloat16(SCALE))
        dop = recv[blocks].reshape(QB, 128)
        o = o_in[pl.ds(pl.multiple_of(i * QB, QB), QB), :]
        prod = (dop.astype(jnp.float32) * o).T
        delta = jnp.concatenate(
            [
                jnp.sum(prod[:64], axis=0, keepdims=True),
                jnp.sum(prod[64:], axis=0, keepdims=True),
            ],
            axis=1,
        )
        dob = halves(dop)
        probs = jnp.exp(dot_nt(keys[...], qb) - lse_in[i])
        dv[...] += dot_nn(probs.astype(jnp.bfloat16), dob)
        ds = (probs * (dot_nt(vals[...], dob) - delta)).astype(jnp.bfloat16)
        dk[...] += dot_nn(ds, qb)
        dqt = dot_nn(kt[...], ds) * SCALE
        dq = jnp.concatenate([dqt[:, :QB], dqt[:, QB:]], axis=0).T
        send2[blocks, 0:32, :] = dq.astype(jnp.bfloat16).reshape(8, 32, 128)
        return carry

    lax.fori_loop(0, 4, step, 0)
    for n, total in enumerate((dk, dv)):
        packed = jnp.concatenate([total[0:1024, :], total[1024:2048, :]], axis=1)
        send2[:, 32 + 32 * n : 64 + 32 * n, :] = packed.astype(jnp.bfloat16).reshape(NC, 32, 128)
    a2a_start(send2, recv2, ssem2, rsem2, me)
    recv2[me] = send2[me]
    for n, (src, dst) in enumerate(whole):
        arriving[n].wait()
        pending.append(to_peer(dst.at[2], dst.at[3], fs.at[n], fr.at[n], peers[0]))
    a2a_wait(send2, recv2, ssem2, rsem2, me)
    unpack_tokens(recv2, dproj, 3)
    for k, peer in enumerate(peers):
        cols = pl.ds(pl.multiple_of(peer[1] * 768, 256), 768)
        pending.append(to_peer(dproj.at[:, cols], dproj_g.at[k + 1], ps.at[k], pr.at[k], peer))
    cols = pl.ds(pl.multiple_of(shard * 768, 256), 768)
    small[...] = small_in[...]
    for n, part in enumerate((0, 2 * D)):
        sums = jnp.sum(dproj[:, part : part + D].astype(jnp.float32), axis=0, keepdims=True)
        for j in range(8):
            row = 20 + 2 * n + j % 2
            small[j // 2, row : row + 1, :] = sums[:, 128 * j : 128 * j + 128]
    for k, peer in enumerate(peers):
        pending.append(
            to_peer(small.at[peer[1]], small_g.at[k + 1], ps.at[3 + k], pr.at[3 + k], peer)
        )
    local = pltpu.make_async_copy(small.at[shard], small_g.at[0], pls.at[2])
    local.start()
    pending.append(local)
    local = pltpu.make_async_copy(dproj.at[:, cols], dproj_g.at[0], pls.at[0])
    local.start()
    pending.append(local)
    local = pltpu.make_async_copy(dproj, dproj_out, pls.at[1])
    local.start()
    pending.append(local)
    for copy in pending:
        copy.wait()


def attn_bwd(dctx, qkv, o, lse, small, act, dpre, datt, hid, dbr, ctx, xin):
    bf = jnp.bfloat16
    sds = jax.ShapeDtypeStruct
    dma = pltpu.SemaphoreType.DMA
    return pl.pallas_call(
        attn_bwd_kernel,
        out_shape=(
            sds((128, 3 * D), bf), sds((4, 128, 768), bf), sds((4, 128, 1024), bf),
            sds((4, 128, 1024), bf), sds((4, 128, 256), bf), sds((4, 128, 1024), bf),
            sds((4, 128, 1024), bf), sds((4, 128, 1024), bf), sds((4, 128, 1024), bf),
            sds((4, 24, 128), jnp.float32),
        ),
        in_specs=[VM] * 5 + [ANY] * 7,
        out_specs=(ANY,) * 10,
        scratch_shapes=[
            pltpu.VMEM((NC, 32, 128), bf),
            pltpu.VMEM((NC, 32, 128), bf),
            pltpu.VMEM((NC, 96, 128), bf),
            pltpu.VMEM((NC, 96, 128), bf),
            pltpu.VMEM((2048, DH), bf),
            pltpu.VMEM((DH, 2048), bf),
            pltpu.VMEM((2048, DH), bf),
            pltpu.VMEM((2048, DH), jnp.float32),
            pltpu.VMEM((2048, DH), jnp.float32),
            pltpu.VMEM((128, 3 * D), bf),
            pltpu.VMEM((4, 24, 128), jnp.float32),
            dma((NC,)), dma((NC,)), dma((NC,)), dma((NC,)),
            dma((7, 3)), dma((7, 3)), dma((4,)), dma((4,)), dma((7,)),
            dma((6,)), dma((6,)), dma((3,)),
        ],
        compiler_params=pltpu.CompilerParams(
            collective_id=1, has_side_effects=True, vmem_limit_bytes=VMEM_LIMIT
        ),
    )(dctx, qkv, o, lse, small, act, dpre, datt, hid, dbr, ctx, xin)


def widen(a):
    return a.astype(jnp.float32)


class RingReduce:
    def __init__(self, part, total, bufs, ring, ssem, rsem):
        self.part, self.total, self.bufs = part, total, bufs
        self.p, self.up, self.down = ring
        self.ssem, self.rsem = ssem, rsem

    def at(self, k):
        return lax.rem(self.p + k, 4)

    def start(self):
        ra, rb, sa, sb, from_down, from_up = self.bufs
        part, at, ssem, rsem = self.part, self.at, self.ssem, self.rsem
        up, down = self.up, self.down
        self.sent = [
            send(part(at(2), 0), ra, ssem(0), rsem(0), up),
            send(part(at(2), 1), rb, ssem(1), rsem(1), down),
            send(part(at(1), 1), from_down.at[2:4], ssem(2), rsem(2), up),
            send(part(at(3), 0), from_up.at[0:2], ssem(3), rsem(3), down),
        ]

    def middle(self):
        ra, rb, sa, sb, from_down, from_up = self.bufs
        part, at, ssem, rsem = self.part, self.at, self.ssem, self.rsem
        up, down = self.up, self.down
        self.sent[0].wait_recv()
        sa[...] = (widen(part(at(1), 0)[...]) + widen(ra[...])).astype(jnp.bfloat16)
        self.sent.append(send(sa, from_down.at[0:2], ssem(4), rsem(4), up))
        self.sent[1].wait_recv()
        sb[...] = (widen(part(at(3), 1)[...]) + widen(rb[...])).astype(jnp.bfloat16)
        self.sent.append(send(sb, from_up.at[2:4], ssem(5), rsem(5), down))

    def finish(self):
        from_down, from_up = self.bufs[4:]
        for copy in self.sent[2:]:
            copy.wait_recv()
        for k in range(2):
            half = pl.ds(2 * k, 2)
            self.total[half] = (
                widen(self.part(self.p, k)[...]) + widen(from_down[half]) + widen(from_up[half])
            ).astype(jnp.bfloat16)
        for copy in self.sent:
            copy.wait_send()


class Stream:
    STEPS = 12

    def __init__(self, grad, out, m, h, scratch, dsems):
        (big, t1, small, t2, ybuf, u, v) = scratch
        (p1s, p1r, p2s, p2r, ys, yr, ts, tr, ms, as_, ar, g1s, g1r, g2s, g2r) = dsems
        c, s, y, z, x = place()
        along_x, along_z = rings()
        one, two = (along_x, along_z) if h == 0 else (along_z, along_x)
        n = 2 * m + h
        self.m, self.c, self.s, self.y = m, c, s, y
        self.pair = {"ctx": lax.rem(c + 16, 32)}
        self.t1, self.t2, self.u, self.v = t1.at[n], t2.at[n], u.at[n], v.at[n]
        self.ybuf = ybuf.at[n]
        self.out = out
        self.ys, self.yr, self.ts, self.tr = ys.at[n], yr.at[n], ts.at[n], tr.at[n]
        self.ms, self.as_, self.ar = ms.at[n], as_.at[n], ar.at[n]
        cols = pl.ds(h * 512, 512)
        self.reduce1 = RingReduce(
            lambda p, k: grad.at[pl.ds(2 * k, 2), rows64(p), cols], self.t1,
            [b.at[n] for b in big], one, sems(p1s, n), sems(p1r, n),
        )
        self.reduce2 = RingReduce(
            lambda p, k: self.t1.at[pl.ds(2 * k, 2), rows16(p)], self.t2,
            [b.at[n] for b in small], two, sems(p2s, n), sems(p2r, n),
        )
        row = one[0] * 4 + two[0]

        def mine(who):
            at = pl.multiple_of(h * 512 + who * 256, 256)
            return out.at[:, rows16(row), pl.ds(at, 256)]

        self.mine = mine

        def small_block(p, lead=pl.ds(0, 4)):
            return out.at[lead, rows16(one[0] * 4 + p), cols]

        def big_block(p, lead=pl.ds(0, 4)):
            return out.at[lead, rows64(p), cols]

        def half_of(make, k):
            return lambda p: make(p, lead=pl.ds(2 * k, 2))

        self.gather1 = RingGather(
            small_block, half_of(small_block, 0), half_of(small_block, 1), two,
            sems(g1s, n), sems(g1r, n),
        )
        self.gather2 = RingGather(
            big_block, half_of(big_block, 0), half_of(big_block, 1), one,
            sems(g2s, n), sems(g2r, n),
        )

    def step(self, k):
        if k == 0:
            self.reduce1.start()
        elif k == 1:
            self.reduce1.middle()
        elif k == 2:
            self.reduce1.finish()
            self.reduce2.start()
        elif k == 3:
            self.reduce2.middle()
        elif k == 4:
            self.reduce2.finish()
            other = pl.ds(pl.multiple_of(256 - self.y * 256, 256), 256)
            self.sent_y = send(self.t2.at[:, :, other], self.ybuf, self.ys, self.yr, self.pair)
        elif k == 5:
            self.sent_y.wait()
            own = pl.ds(pl.multiple_of(self.y * 256, 256), 256)
            total = (widen(self.t2[:, :, own]) + widen(self.ybuf[...])).astype(jnp.bfloat16)
            if self.m == 0:
                self.v[...] = total
            else:
                self.u[...] = total
                self.turned = []
                for j in range(1, 4):
                    owner = lax.rem(self.s + j, 4)
                    self.turned.append(
                        send(
                            self.u.at[owner], self.v.at[self.s], self.ts.at[j], self.tr.at[j],
                            {"shard": owner},
                        )
                    )
                self.v[self.s] = self.u[self.s]
        elif k == 6:
            if self.m > 0:
                for j in range(1, 4):
                    source = lax.rem(self.s + 4 - j, 4)
                    got = self.v.at[source]
                    remote(got, got, self.ts.at[j], self.tr.at[j], {"shard": source}).wait_recv()
                    self.turned[j - 1].wait_send()
            self.kept = pltpu.make_async_copy(self.v, self.mine(self.y), self.ms)
            self.kept.start()
            self.shared = send(self.v, self.mine(self.y), self.as_, self.ar, self.pair)
        elif k == 7:
            self.kept.wait()
            self.shared.wait_send()
            got = self.mine(1 - self.y)
            remote(got, got, self.as_, self.ar, self.pair).wait_recv()
            self.gather1.start()
        elif k == 8:
            self.gather1.forward()
        elif k == 9:
            self.gather1.finish()
            self.gather2.start()
        elif k == 10:
            self.gather2.forward()
        else:
            self.gather2.finish()


def reduce_kernel(
    act, dbr, hid, dpre, x, dproj, ctx, datt, small_g, ff_out, in_out, qo_out, small_out,
    grads, ra, rb, sa, sb, fd, fu, ra2, rb2, sa2, sb2, fd2, fu2, t1, t2, ybuf, u, v,
    small, small_all, small_s, small_r, *dsems
):
    c, s, *unused = place()
    barrier = pltpu.get_barrier_semaphore()
    signal_ctx_peers(barrier, c)
    for j in range(1, 4):
        pl.semaphore_signal(
            barrier, inc=1, device_id={"shard": lax.rem(s + j, 4)}, device_id_type=MESH
        )
    small[...] = small_g[0] + small_g[1] + small_g[2] + small_g[3]
    pl.semaphore_wait(barrier, NC + 2)
    scratch = ((ra, rb, sa, sb, fd, fu), t1, (ra2, rb2, sa2, sb2, fd2, fu2), t2, ybuf, u, v)
    streams = []
    products = (((act, dbr, 0),), ((hid, dpre, 0),), ((x, dproj, 0), (ctx, datt, 768)))
    for m, (terms, out) in enumerate(zip(products, (ff_out, in_out, qo_out))):
        for left, right, at in terms:
            width = right.shape[-1]

            def block(q, carry):
                part = left[:, :, pl.ds(pl.multiple_of(q * 256, 256), 256)].reshape(512, 256)
                grads[m, q, :, at : at + width] = lax.dot_general(
                    part, right[...].reshape(512, width), (((0,), (0,)), ((), ())),
                    preferred_element_type=jnp.float32,
                ).astype(jnp.bfloat16)
                return carry

            lax.fori_loop(0, 4, block, 0)
        for h in range(2):
            streams.append(Stream(grads.at[m], out, m, h, scratch, dsems))
            streams[-1].step(0)

    def spread(k, carry):
        dest = lax.rem(c + k, NC)
        remote(small, small_all.at[c], small_s.at[k], small_r.at[k], {"ctx": dest}).start()
        return carry

    lax.fori_loop(1, NC, spread, 0)
    for k in range(1, Stream.STEPS):
        for stream in streams:
            stream.step(k)

    def arrive(k, carry):
        source = lax.rem(c + NC - k, NC)
        copy = remote(small, small_all.at[source], small_s.at[k], small_r.at[k], {"ctx": source})
        copy.wait_send()
        copy.wait_recv()
        return carry

    lax.fori_loop(1, NC, arrive, 0)
    small_all[c] = small[...]
    small_out[...] = lax.fori_loop(
        0, NC, lambda k, acc: acc + small_all[k], jnp.zeros((24, 128), jnp.float32)
    )


def reduce_grads(act, dbr, hid, dpre, x, dproj, ctx, datt, small):
    bf, f32 = jnp.bfloat16, jnp.float32
    dma = pltpu.SemaphoreType.DMA
    vm = pltpu.VMEM
    full = jax.ShapeDtypeStruct((4, 256, 1024), bf)

    def ring_bufs(rows):
        return [vm((6, 2, rows, 512), bf)] * 4 + [vm((6, 4, rows, 512), bf)] * 2

    return pl.pallas_call(
        reduce_kernel,
        out_shape=(full, full, full, jax.ShapeDtypeStruct((24, 128), f32)),
        in_specs=[VM] * 9,
        out_specs=(ANY, ANY, ANY, VM),
        scratch_shapes=[vm((3, 4, 256, 1024), bf)]
        + ring_bufs(64)
        + ring_bufs(16)
        + [
            vm((6, 4, 64, 512), bf), vm((6, 4, 16, 512), bf), vm((6, 4, 16, 256), bf),
            vm((6, 4, 16, 256), bf), vm((6, 4, 16, 256), bf),
            vm((24, 128), f32), vm((NC, 24, 128), f32), dma((NC,)), dma((NC,)),
            dma((6, 6)), dma((6, 6)), dma((6, 6)), dma((6, 6)), dma((6,)), dma((6,)),
            dma((6, 4)), dma((6, 4)), dma((6,)), dma((6,)), dma((6,)),
            dma((6, 4)), dma((6, 4)), dma((6, 4)), dma((6, 4)),
        ],
        compiler_params=pltpu.CompilerParams(
            collective_id=2, has_side_effects=True, vmem_limit_bytes=VMEM_LIMIT
        ),
    )(act, dbr, hid, dpre, x, dproj, ctx, datt, small)


def widen_kernel(ff, in_, qo, ff_out, in_out, qkv_out, w_out):
    ff_out[...] = widen(ff[0])
    in_out[...] = widen(in_[0])
    qkv_out[...] = widen(qo[0, :, :768])
    w_out[...] = widen(qo[0, :, 768:])


def widen_grads(ff, in_, qo):
    sds = jax.ShapeDtypeStruct
    f32 = jnp.float32
    block = pl.BlockSpec((1, 256, 1024), lambda q: (q, 0, 0))
    return pl.pallas_call(
        widen_kernel,
        grid=(4,),
        out_shape=(
            sds((1024, 1024), f32), sds((256, 4096), f32), sds((256, 3072), f32),
            sds((256, 1024), f32),
        ),
        in_specs=[block] * 3,
        out_specs=(
            pl.BlockSpec((256, 1024), lambda q: (q, 0)),
            pl.BlockSpec((256, 1024), lambda q: (0, q)),
            pl.BlockSpec((256, 768), lambda q: (0, q)),
            pl.BlockSpec((256, 256), lambda q: (0, q)),
        ),
        compiler_params=pltpu.CompilerParams(vmem_limit_bytes=VMEM_LIMIT),
    )(ff, in_, qo)


def local(
    inputs, cotangent, w_qkv, bias_qv, w_out, bias_out, ln1_gain, ln1_bias, w_in, bias_in,
    w_ff_out, bias_ff_out, ln2_gain, ln2_bias,
):
    bf, f32 = jnp.bfloat16, jnp.float32
    small = jnp.concatenate(
        [
            bias_qv.reshape(512), bias_out, ln1_gain, ln1_bias, bias_ff_out, ln2_gain, ln2_bias,
            bias_in, jnp.zeros((1024,), bf),
        ]
    )
    w_qkv_all, small_all = gather_first(w_qkv.reshape(1, 256, 3 * D), small.reshape(32, 128))
    w_qkv_all = w_qkv_all.reshape(D, 3 * D)
    small_all = small_all.reshape(4, 4096).astype(f32)
    bias_q, bias_v, bias_o, gain_one, shift_one, bias_ff, gain_two, shift_two = (
        small_all[:, 256 * k : 256 * k + 256].reshape(D) for k in range(8)
    )
    bias_i = small_all[:, 2048:3072].reshape(FF)
    groups, rows_dev = inputs.shape[0], inputs.shape[1]
    token_count = groups * rows_dev
    tokens_in = inputs.reshape(token_count, D)
    bias_full = jnp.concatenate([bias_q, jnp.zeros((D,), f32), bias_v])
    projected = (jnp.dot(tokens_in, w_qkv_all, preferred_element_type=f32) + bias_full).astype(bf)
    flat_context, qkv, o, lse, w_out_all, w_in_all, w_ff_all = attn_fwd(
        projected, w_out.reshape(1, 256, D), w_in.reshape(1, 256, FF), w_ff_out.reshape(4, 256, D)
    )
    w_out_all = w_out_all.reshape(D, D)
    w_in_all = w_in_all.reshape(D, FF)
    w_ff_all = w_ff_all.reshape(FF, D)
    attended = jnp.dot(flat_context, w_out_all, preferred_element_type=f32) + bias_o
    first_sum = tokens_in.astype(f32) + attended
    hidden = layer_norm(first_sum, gain_one, shift_one)
    hidden_low = hidden.astype(bf)
    pre_act = jnp.dot(hidden_low, w_in_all, preferred_element_type=f32) + bias_i
    act_low = gelu_exact(pre_act).astype(bf)
    branch = jnp.dot(act_low, w_ff_all, preferred_element_type=f32) + bias_ff
    second_sum = hidden + branch
    result_rows = layer_norm(second_sum, gain_two, shift_two)
    upstream = cotangent.reshape(token_count, D).astype(f32)
    unused_two, pull_two = jax.vjp(layer_norm, second_sum, gain_two, shift_two)
    d_second, d_gain_two, d_shift_two = pull_two(upstream)
    d_branch = d_second.astype(bf)
    grad_bias_ff = jnp.sum(d_branch.astype(f32), axis=0)
    d_act = times_transposed(d_branch, w_ff_all)
    unused_act, pull_gelu = jax.vjp(gelu_exact, pre_act)
    d_pre_act = pull_gelu(d_act)[0].astype(bf)
    grad_bias_in = jnp.sum(d_pre_act.astype(f32), axis=0)
    d_hidden = d_second + times_transposed(d_pre_act, w_in_all)
    unused_one, pull_one = jax.vjp(layer_norm, first_sum, gain_one, shift_one)
    d_first, d_gain_one, d_shift_one = pull_one(d_hidden)
    d_attended = d_first.astype(bf)
    grad_bias_out = jnp.sum(d_attended.astype(f32), axis=0)
    d_context = times_transposed(d_attended, w_out_all).astype(bf)
    small_sums = jnp.concatenate(
        [
            a.reshape(4, -1)
            for a in (
                grad_bias_out, d_gain_one, d_shift_one, grad_bias_ff, d_gain_two, d_shift_two,
                grad_bias_in, jnp.zeros((2048,), f32),
            )
        ],
        axis=1,
    ).reshape(4, 24, 128)
    d_projected, dproj_g, act_g, dpre_g, datt_g, hid_g, dbr_g, ctx_g, x_g, small_g = attn_bwd(
        d_context, qkv, o, lse, small_sums, act_low, d_pre_act, d_attended, hidden_low, d_branch,
        flat_context, tokens_in,
    )
    red_ff, red_in, red_qo, sums = reduce_grads(
        act_g, dbr_g, hid_g, dpre_g, x_g, dproj_g, ctx_g, datt_g, small_g
    )
    own_ff, own_in, own_qkv, own_out = widen_grads(red_ff, red_in, red_qo)
    d_inputs = d_first + times_transposed(d_projected, w_qkv_all)
    sums = sums.reshape(3072)

    def own(k):
        return sums[256 * k : 256 * k + 256]

    own_bias_in = sums[1536:2560]
    own_bias_qv = sums[2560:].reshape(2, 256)
    return (
        result_rows.astype(bf).reshape(groups, rows_dev, D),
        d_inputs.reshape(groups, rows_dev, D),
        own_qkv,
        own_bias_qv,
        own_out,
        own(0),
        own(1),
        own(2),
        own_in,
        own_bias_in,
        own_ff,
        own(3),
        own(4),
        own(5),
    )


def solution(mesh):
    specs = (
        P("shard", "ctx", None),
        P("shard", "ctx", None),
        P("shard", None),
        P(None, "shard"),
        P("shard", None),
        P("shard"),
        P("shard"),
        P("shard"),
        P("shard", None),
        P("shard"),
        P("shard", None),
        P("shard"),
        P("shard"),
        P("shard"),
    )
    return jax.shard_map(local, mesh=mesh, in_specs=specs, out_specs=specs, check_vma=False)
```

```python
import functools

import jax
import jax.numpy as jnp
from jax import lax
from jax.experimental import pallas as pl
from jax.experimental.pallas import tpu as pltpu
from jax.sharding import PartitionSpec as P

D = 1024
H = 16
DH = 64
FF = 4096
NC = 32
SCALE = DH ** (-0.5)
MESH = pl.DeviceIdType.MESH
NORM_EPS = 1e-05
VMEM_LIMIT = 56 * 1024 * 1024
VM = pl.BlockSpec(memory_space=pltpu.VMEM)
ANY = pl.BlockSpec(memory_space=pl.ANY)


def layer_norm(values, norm_gain, norm_shift):
    row_mean = jnp.mean(values, axis=-1, keepdims=True)
    centered = values - row_mean
    row_var = jnp.mean(centered * centered, axis=-1, keepdims=True)
    return centered * lax.rsqrt(row_var + NORM_EPS) * norm_gain + norm_shift


def gelu_exact(values):
    return 0.5 * values * (1.0 + lax.erf(values * 0.7071067811865476))


def outer_sum(left, right):
    return lax.dot_general(
        left, right, (((0,), (0,)), ((), ())), preferred_element_type=jnp.float32
    )


def times_transposed(left, right):
    return lax.dot_general(
        left, right, (((1,), (1,)), ((), ())), preferred_element_type=jnp.float32
    )


def pack_tokens(src, send, parts):
    def step(hp, carry):
        for g in range(2):
            for part in range(parts):
                cols = pl.ds(pl.multiple_of(part * D + hp * 128, 128), 128)
                a = src[pl.ds(g * 64, 32), cols]
                b = src[pl.ds(g * 64 + 32, 32), cols]
                rows = pl.ds(part * 32, 32)
                send[g * 16 + 2 * hp, rows, :] = jnp.concatenate([a[:, :64], b[:, :64]], axis=1)
                send[g * 16 + 2 * hp + 1, rows, :] = jnp.concatenate(
                    [a[:, 64:], b[:, 64:]], axis=1
                )
        return carry

    lax.fori_loop(0, H // 2, step, 0)


def unpack_tokens(recv, dst, parts):
    def step(hp, carry):
        for g in range(2):
            for part in range(parts):
                cols = pl.ds(pl.multiple_of(part * D + hp * 128, 128), 128)
                rows = pl.ds(part * 32, 32)
                even = recv[g * 16 + 2 * hp, rows, :]
                odd = recv[g * 16 + 2 * hp + 1, rows, :]
                dst[pl.ds(g * 64, 32), cols] = jnp.concatenate([even[:, :64], odd[:, :64]], axis=1)
                dst[pl.ds(g * 64 + 32, 32), cols] = jnp.concatenate(
                    [even[:, 64:], odd[:, 64:]], axis=1
                )
        return carry

    lax.fori_loop(0, H // 2, step, 0)


def a2a_start(send, recv, ssem, rsem, me):
    def step(k, carry):
        dest = lax.rem(me + k, NC)
        pltpu.make_async_remote_copy(
            src_ref=send.at[dest],
            dst_ref=recv.at[me],
            send_sem=ssem.at[k],
            recv_sem=rsem.at[k],
            device_id={"ctx": dest},
            device_id_type=MESH,
        ).start()
        return carry

    lax.fori_loop(1, NC, step, 0)


def a2a_wait(send, recv, ssem, rsem, me):
    def step(k, carry):
        source = lax.rem(me + NC - k, NC)
        copy = pltpu.make_async_remote_copy(
            src_ref=send.at[source],
            dst_ref=recv.at[source],
            send_sem=ssem.at[k],
            recv_sem=rsem.at[k],
            device_id={"ctx": source},
            device_id_type=MESH,
        )
        copy.wait_send()
        copy.wait_recv()
        return carry

    lax.fori_loop(1, NC, step, 0)


def signal_ctx_peers(barrier, me):
    def step(k, carry):
        pl.semaphore_signal(
            barrier, inc=1, device_id={"ctx": lax.rem(me + k, NC)}, device_id_type=MESH
        )
        return carry

    lax.fori_loop(1, NC, step, 0)


def halves(packed):
    return jnp.concatenate([packed[:, :64], packed[:, 64:]], axis=0)


def dot_nt(a, b):
    return lax.dot_general(a, b, (((1,), (1,)), ((), ())), preferred_element_type=jnp.float32)


def dot_nn(a, b):
    return jnp.dot(a, b, preferred_element_type=jnp.float32)


def place():
    c = lax.axis_index("ctx")
    return c, lax.axis_index("shard"), lax.div(c, 16), lax.rem(lax.div(c, 4), 4), lax.rem(c, 4)


def remote(src, dst, send_sem, recv_sem, peer):
    return pltpu.make_async_remote_copy(
        src_ref=src, dst_ref=dst, send_sem=send_sem, recv_sem=recv_sem,
        device_id=peer, device_id_type=MESH,
    )


def send(src, dst, send_sem, recv_sem, peer):
    copy = remote(src, dst, send_sem, recv_sem, peer)
    copy.start()
    return copy


def rings():
    c, unused_s, y, z, x = place()
    along_x = (
        x,
        {"ctx": c - x + lax.rem(x + 1, 4)},
        {"ctx": c - x + lax.rem(x + 3, 4)},
    )
    along_z = (
        z,
        {"ctx": y * 16 + lax.rem(z + 1, 4) * 4 + x},
        {"ctx": y * 16 + lax.rem(z + 3, 4) * 4 + x},
    )
    return along_x, along_z


class RingGather:
    def __init__(self, block, first, second, ring, ssem, rsem):
        self.block, self.first, self.second = block, first, second
        self.p, self.up, self.down = ring
        self.ssem, self.rsem = ssem, rsem

    def at(self, k):
        return lax.rem(self.p + k, 4)

    def start(self):
        own = self.block(self.p)
        self.sent = [
            send(own, own, self.ssem(0), self.rsem(0), self.up),
            send(own, own, self.ssem(1), self.rsem(1), self.down),
        ]

    def forward(self):
        from_down, from_up = self.block(self.at(3)), self.block(self.at(1))
        remote(from_down, from_down, self.ssem(0), self.rsem(0), self.up).wait_recv()
        part = self.first(self.at(3))
        self.sent.append(send(part, part, self.ssem(2), self.rsem(2), self.up))
        remote(from_up, from_up, self.ssem(1), self.rsem(1), self.down).wait_recv()
        part = self.second(self.at(1))
        self.sent.append(send(part, part, self.ssem(3), self.rsem(3), self.down))

    def finish(self):
        part = self.first(self.at(2))
        remote(part, part, self.ssem(2), self.rsem(2), self.up).wait_recv()
        part = self.second(self.at(2))
        remote(part, part, self.ssem(3), self.rsem(3), self.down).wait_recv()
        for copy in self.sent:
            copy.wait_send()


def sems(ref, *lead):
    return lambda k: ref.at[(*lead, k)]


def rows16(index):
    return pl.ds(pl.multiple_of(index * 16, 16), 16)


def rows64(index):
    return pl.ds(pl.multiple_of(index * 64, 64), 64)


class WeightGather:
    STEPS = 7

    def __init__(self, src, dst, n, ls, os, orr, cs, cr, gs, gr, fs, fr):
        c, s, y, z, x = place()
        sibling, cross, unused = group_ids()
        self.sibling, self.cross = mesh_id(sibling), mesh_id(cross)
        self.src, self.dst, self.s = src, dst, s
        self.far, self.far_sib = cross[1], unused[1]
        self.sib_shard = sibling[1]
        self.ls, self.os, self.orr = ls.at[n], os.at[n], orr.at[n]
        self.cs, self.cr, self.fs, self.fr = cs, cr, fs, fr
        self.n = n
        width = src.shape[-1]
        self.half, self.quarter = width // 2, width // 4
        along_x, along_z = rings()
        self.streams = []
        for h in range(2):
            one, two = (along_z, along_x) if h == 0 else (along_x, along_z)
            base = x if h == 0 else z
            cols = pl.ds(h * self.half, self.half)
            cols_a = pl.ds(h * self.half, self.quarter)
            cols_b = pl.ds(h * self.half + self.quarter, self.quarter)
            own = self.dst.at[self.far]

            def small_block(p, cols=cols, base=base, own=own):
                return own.at[:, rows16(base * 4 + p), cols]

            def big_block(p, cols=cols, own=own):
                return own.at[:, rows64(p), cols]

            def part_of(make, cols):
                return lambda p: make(p, cols=cols)

            ring1 = RingGather(
                small_block, part_of(small_block, cols_a), part_of(small_block, cols_b), one,
                sems(gs, n, h, 0), sems(gr, n, h, 0),
            )
            ring2 = RingGather(
                big_block, part_of(big_block, cols_a), part_of(big_block, cols_b), two,
                sems(gs, n, h, 1), sems(gr, n, h, 1),
            )
            row = base * 4 + one[0]
            self.streams.append((h, row, cols, cols_a, cols_b, ring1, ring2, two[0]))
        self.sent = []

    def step(self, k):
        if k == 0:
            for h, row, cols, *unused in self.streams:
                self.sent.append(
                    send(
                        self.src.at[:, rows16(row), cols],
                        self.dst.at[self.s].at[:, rows16(row), cols],
                        self.cs.at[self.n, h], self.cr.at[self.n, h], self.cross,
                    )
                )
            self.local = pltpu.make_async_copy(self.src, self.dst.at[self.s], self.ls)
            self.local.start()
            self.own = send(self.src, self.dst.at[self.s], self.os, self.orr, self.sibling)
        elif k == 1:
            for h, row, cols, cols_a, cols_b, ring1, ring2, p in self.streams:
                got = self.dst.at[self.far].at[:, rows16(row), cols]
                remote(got, got, self.cs.at[self.n, h], self.cr.at[self.n, h], self.cross).wait_recv()
                ring1.start()
        elif k == 2:
            for h, row, cols, cols_a, cols_b, ring1, ring2, p in self.streams:
                ring1.forward()
        elif k == 3:
            for h, row, cols, cols_a, cols_b, ring1, ring2, p in self.streams:
                ring1.finish()
                ring2.start()
                self.pass_on(h, 0, rows64(p), cols)
        elif k == 4:
            for h, row, cols, cols_a, cols_b, ring1, ring2, p in self.streams:
                ring2.forward()
                self.pass_on(h, 1, rows64(lax.rem(p + 3, 4)), cols)
                self.pass_on(h, 2, rows64(lax.rem(p + 1, 4)), cols)
        elif k == 5:
            for h, row, cols, cols_a, cols_b, ring1, ring2, p in self.streams:
                ring2.finish()
                self.pass_on(h, 3, rows64(lax.rem(p + 2, 4)), cols)
        else:
            self.local.wait()
            self.own.wait_send()
            got = self.dst.at[self.sib_shard]
            remote(got, got, self.os, self.orr, self.sibling).wait_recv()
            for h, row, cols, cols_a, cols_b, ring1, ring2, p in self.streams:
                for j, shift in enumerate((0, 3, 1, 2)):
                    got = self.dst.at[self.far_sib].at[:, rows64(lax.rem(p + shift, 4)), cols]
                    remote(
                        got, got, self.fs.at[self.n, h, j], self.fr.at[self.n, h, j], self.sibling
                    ).wait_recv()
            for copy in self.sent:
                copy.wait_send()

    def pass_on(self, h, j, rows, cols):
        part = self.dst.at[self.far].at[:, rows, cols]
        self.sent.append(
            send(part, part, self.fs.at[self.n, h, j], self.fr.at[self.n, h, j], self.sibling)
        )


def weight_sems(count):
    dma = pltpu.SemaphoreType.DMA
    return [
        dma((count,)), dma((count,)), dma((count,)), dma((count, 2)), dma((count, 2)),
        dma((count, 2, 2, 4)), dma((count, 2, 2, 4)), dma((count, 2, 4)), dma((count, 2, 4)),
    ]


def group_ids():
    c = lax.axis_index("ctx")
    s = lax.axis_index("shard")
    core = lax.rem(s, 2)
    other = 2 - 2 * lax.div(s, 2)
    sibling = s + 1 - 2 * core
    cross_c = lax.rem(c + NC // 2, NC)
    return ((c, sibling), (cross_c, other + core), (cross_c, other + 1 - core))


def mesh_id(pair):
    return {"ctx": pair[0], "shard": pair[1]}


def first_kernel(w, small, w_all, small_all, ls, os, orr, cs, cr, gs, gr, fs, fr, ss, sr, sl):
    unused_c, s, *unused = place()
    peers = [mesh_id(peer) for peer in group_ids()]
    around = [ring[k] for ring in rings() for k in (1, 2)]
    barrier = pltpu.get_barrier_semaphore()
    for peer in peers + around:
        pl.semaphore_signal(barrier, inc=1, device_id=peer, device_id_type=MESH)
    pl.semaphore_wait(barrier, len(peers) + len(around))
    gather = WeightGather(w, w_all, 0, ls, os, orr, cs, cr, gs, gr, fs, fr)
    gather.step(0)
    pending = [
        send(small, small_all.at[s], ss.at[k], sr.at[k], peer) for k, peer in enumerate(peers)
    ]
    own = pltpu.make_async_copy(small, small_all.at[s], sl)
    own.start()
    for k in range(1, WeightGather.STEPS):
        gather.step(k)
    own.wait()
    for k, peer in enumerate(group_ids()):
        pending[k].wait_send()
        got = small_all.at[peer[1]]
        remote(got, got, ss.at[k], sr.at[k], peers[k]).wait_recv()


def gather_first(w, small):
    dma = pltpu.SemaphoreType.DMA
    return pl.pallas_call(
        first_kernel,
        out_shape=(
            jax.ShapeDtypeStruct((4, *w.shape), w.dtype),
            jax.ShapeDtypeStruct((4, *small.shape), small.dtype),
        ),
        in_specs=[ANY, VM],
        out_specs=(VM, VM),
        scratch_shapes=weight_sems(1) + [dma((3,)), dma((3,)), dma],
        compiler_params=pltpu.CompilerParams(
            collective_id=3, has_side_effects=True, vmem_limit_bytes=VMEM_LIMIT
        ),
    )(w, small)


QB = 256


def attn_fwd_kernel(
    proj, w0, w1, w2, ctx_out, qkv_out, o_out, lse_out, all0, all1, all2,
    send, recv, send2, recv2, keys, vt, ssem, rsem, ssem2, rsem2, *wsems
):
    me = lax.axis_index("ctx")
    barrier = pltpu.get_barrier_semaphore()
    signal_ctx_peers(barrier, me)
    for peer in group_ids()[:2]:
        pl.semaphore_signal(barrier, inc=1, device_id=mesh_id(peer), device_id_type=MESH)
    pack_tokens(proj, send, 3)
    pl.semaphore_wait(barrier, NC + 1)
    a2a_start(send, recv, ssem, rsem, me)
    gathers = [
        WeightGather(w, out, n, *wsems)
        for n, (w, out) in enumerate(((w0, all0), (w1, all1), (w2, all2)))
    ]

    def advance(k):
        for gather in gathers:
            gather.step(k)

    advance(0)
    recv[me] = send[me]
    a2a_wait(send, recv, ssem, rsem, me)
    qkv_out[...] = recv[...]
    keys[...] = halves(recv[:, 32:64, :].reshape(1024, 128))
    vp = recv[:, 64:96, :].reshape(1024, 128).astype(jnp.float32).T.astype(jnp.bfloat16)
    vt[...] = jnp.concatenate([vp[:64], vp[64:]], axis=1)
    advance(1)

    def step(i, carry):
        qp = recv[pl.ds(i * 8, 8), 0:32, :].reshape(QB, 128) * jnp.bfloat16(SCALE)
        s = dot_nt(keys[...], halves(qp))
        m = jnp.max(s, axis=0, keepdims=True)
        p = jnp.exp(s - m)
        total = jnp.sum(p, axis=0, keepdims=True)
        ot = dot_nn(vt[...], p.astype(jnp.bfloat16)) / total
        o = jnp.concatenate([ot[:, :QB], ot[:, QB:]], axis=0).T
        o_out[pl.ds(pl.multiple_of(i * QB, QB), QB), :] = o
        lse_out[i] = m + jnp.log(total)
        send2[pl.ds(i * 8, 8)] = o.astype(jnp.bfloat16).reshape(8, 32, 128)
        return carry

    lax.fori_loop(0, 1, step, 0)
    advance(2)
    lax.fori_loop(1, 2, step, 0)
    advance(3)
    lax.fori_loop(2, 4, step, 0)
    a2a_start(send2, recv2, ssem2, rsem2, me)
    recv2[me] = send2[me]
    advance(4)
    a2a_wait(send2, recv2, ssem2, rsem2, me)
    unpack_tokens(recv2, ctx_out, 1)
    advance(5)
    advance(6)


def attn_fwd(projected, w_out, w_in, w_ff):
    return pl.pallas_call(
        attn_fwd_kernel,
        out_shape=(
            jax.ShapeDtypeStruct((128, D), jnp.bfloat16),
            jax.ShapeDtypeStruct((NC, 96, 128), jnp.bfloat16),
            jax.ShapeDtypeStruct((1024, 128), jnp.float32),
            jax.ShapeDtypeStruct((4, 1, 2 * QB), jnp.float32),
        )
        + tuple(jax.ShapeDtypeStruct((4, *w.shape), w.dtype) for w in (w_out, w_in, w_ff)),
        in_specs=[VM, ANY, ANY, ANY],
        out_specs=(VM,) * 7,
        scratch_shapes=[
            pltpu.VMEM((NC, 96, 128), jnp.bfloat16),
            pltpu.VMEM((NC, 96, 128), jnp.bfloat16),
            pltpu.VMEM((NC, 32, 128), jnp.bfloat16),
            pltpu.VMEM((NC, 32, 128), jnp.bfloat16),
            pltpu.VMEM((2048, DH), jnp.bfloat16),
            pltpu.VMEM((DH, 2048), jnp.bfloat16),
            pltpu.SemaphoreType.DMA((NC,)),
            pltpu.SemaphoreType.DMA((NC,)),
            pltpu.SemaphoreType.DMA((NC,)),
            pltpu.SemaphoreType.DMA((NC,)),
        ]
        + weight_sems(3),
        compiler_params=pltpu.CompilerParams(
            collective_id=0, has_side_effects=True, vmem_limit_bytes=VMEM_LIMIT
        ),
    )(projected, w_out, w_in, w_ff)


def attn_bwd_kernel(
    dctx, qkv, o_in, lse_in, small_in, act, dpre, datt, hid, dbr, ctx, xin,
    dproj_out, dproj_g, act_g, dpre_g, datt_g, hid_g, dbr_g, ctx_g, x_g, small_g,
    send, recv, send2, recv2, keys, kt, vals, dk, dv, dproj, small,
    ssem, rsem, ssem2, rsem2, xs, xr, fs, fr, ls, ps, pr, pls,
):
    me = lax.axis_index("ctx")
    shard = lax.axis_index("shard")
    peers = group_ids()
    barrier = pltpu.get_barrier_semaphore()
    signal_ctx_peers(barrier, me)
    for peer in peers:
        pl.semaphore_signal(barrier, inc=1, device_id=mesh_id(peer), device_id_type=MESH)
    pack_tokens(dctx, send, 1)
    pl.semaphore_wait(barrier, NC + 2)
    a2a_start(send, recv, ssem, rsem, me)

    def to_peer(src, dst, ssem_, rsem_, peer):
        copy = remote(src, dst, ssem_, rsem_, mesh_id(peer))
        copy.start()
        return copy

    slices = ((act, act_g, 1024), (dpre, dpre_g, 1024), (datt, datt_g, 256))
    whole = ((hid, hid_g), (dbr, dbr_g), (ctx, ctx_g), (xin, x_g))
    pending, arriving = [], []
    for n, (src, dst) in enumerate(whole):
        pending.append(to_peer(src, dst.at[1], xs.at[n, 0], xr.at[n, 0], peers[0]))
        arriving.append(to_peer(src, dst.at[2], xs.at[n, 1], xr.at[n, 1], peers[1]))
        local = pltpu.make_async_copy(src, dst.at[0], ls.at[n])
        local.start()
        pending.append(local)
    for n, (src, dst, width) in enumerate(slices):
        for k, peer in enumerate(peers):
            cols = pl.ds(pl.multiple_of(peer[1] * width, width), width)
            pending.append(
                to_peer(src.at[:, cols], dst.at[k + 1], xs.at[4 + n, k], xr.at[4 + n, k], peer)
            )
        cols = pl.ds(pl.multiple_of(shard * width, width), width)
        local = pltpu.make_async_copy(src.at[:, cols], dst.at[0], ls.at[4 + n])
        local.start()
        pending.append(local)

    recv[me] = send[me]
    keys[...] = halves(qkv[:, 32:64, :].reshape(1024, 128))
    vals[...] = halves(qkv[:, 64:96, :].reshape(1024, 128))
    kp = qkv[:, 32:64, :].reshape(1024, 128).astype(jnp.float32).T.astype(jnp.bfloat16)
    kt[...] = jnp.concatenate([kp[:64], kp[64:]], axis=1)
    dk[...] = jnp.zeros_like(dk)
    dv[...] = jnp.zeros_like(dv)
    a2a_wait(send, recv, ssem, rsem, me)

    def step(i, carry):
        blocks = pl.ds(i * 8, 8)
        qb = halves(qkv[blocks, 0:32, :].reshape(QB, 128) * jnp.bfloat16(SCALE))
        dop = recv[blocks].reshape(QB, 128)
        o = o_in[pl.ds(pl.multiple_of(i * QB, QB), QB), :]
        prod = (dop.astype(jnp.float32) * o).T
        delta = jnp.concatenate(
            [
                jnp.sum(prod[:64], axis=0, keepdims=True),
                jnp.sum(prod[64:], axis=0, keepdims=True),
            ],
            axis=1,
        )
        dob = halves(dop)
        probs = jnp.exp(dot_nt(keys[...], qb) - lse_in[i])
        dv[...] += dot_nn(probs.astype(jnp.bfloat16), dob)
        ds = (probs * (dot_nt(vals[...], dob) - delta)).astype(jnp.bfloat16)
        dk[...] += dot_nn(ds, qb)
        dqt = dot_nn(kt[...], ds) * SCALE
        dq = jnp.concatenate([dqt[:, :QB], dqt[:, QB:]], axis=0).T
        send2[blocks, 0:32, :] = dq.astype(jnp.bfloat16).reshape(8, 32, 128)
        return carry

    lax.fori_loop(0, 4, step, 0)
    for n, total in enumerate((dk, dv)):
        packed = jnp.concatenate([total[0:1024, :], total[1024:2048, :]], axis=1)
        send2[:, 32 + 32 * n : 64 + 32 * n, :] = packed.astype(jnp.bfloat16).reshape(NC, 32, 128)
    a2a_start(send2, recv2, ssem2, rsem2, me)
    recv2[me] = send2[me]
    for n, (src, dst) in enumerate(whole):
        arriving[n].wait()
        pending.append(to_peer(dst.at[2], dst.at[3], fs.at[n], fr.at[n], peers[0]))
    a2a_wait(send2, recv2, ssem2, rsem2, me)
    unpack_tokens(recv2, dproj, 3)
    for k, peer in enumerate(peers):
        cols = pl.ds(pl.multiple_of(peer[1] * 768, 256), 768)
        pending.append(to_peer(dproj.at[:, cols], dproj_g.at[k + 1], ps.at[k], pr.at[k], peer))
    cols = pl.ds(pl.multiple_of(shard * 768, 256), 768)
    small[...] = small_in[...]
    for n, part in enumerate((0, 2 * D)):
        sums = jnp.sum(dproj[:, part : part + D].astype(jnp.float32), axis=0, keepdims=True)
        for j in range(8):
            row = 20 + 2 * n + j % 2
            small[j // 2, row : row + 1, :] = sums[:, 128 * j : 128 * j + 128]
    for k, peer in enumerate(peers):
        pending.append(
            to_peer(small.at[peer[1]], small_g.at[k + 1], ps.at[3 + k], pr.at[3 + k], peer)
        )
    local = pltpu.make_async_copy(small.at[shard], small_g.at[0], pls.at[2])
    local.start()
    pending.append(local)
    local = pltpu.make_async_copy(dproj.at[:, cols], dproj_g.at[0], pls.at[0])
    local.start()
    pending.append(local)
    local = pltpu.make_async_copy(dproj, dproj_out, pls.at[1])
    local.start()
    pending.append(local)
    for copy in pending:
        copy.wait()


def attn_bwd(dctx, qkv, o, lse, small, act, dpre, datt, hid, dbr, ctx, xin):
    bf = jnp.bfloat16
    sds = jax.ShapeDtypeStruct
    dma = pltpu.SemaphoreType.DMA
    return pl.pallas_call(
        attn_bwd_kernel,
        out_shape=(
            sds((128, 3 * D), bf), sds((4, 128, 768), bf), sds((4, 128, 1024), bf),
            sds((4, 128, 1024), bf), sds((4, 128, 256), bf), sds((4, 128, 1024), bf),
            sds((4, 128, 1024), bf), sds((4, 128, 1024), bf), sds((4, 128, 1024), bf),
            sds((4, 24, 128), jnp.float32),
        ),
        in_specs=[VM] * 5 + [ANY] * 7,
        out_specs=(VM,) * 10,
        scratch_shapes=[
            pltpu.VMEM((NC, 32, 128), bf),
            pltpu.VMEM((NC, 32, 128), bf),
            pltpu.VMEM((NC, 96, 128), bf),
            pltpu.VMEM((NC, 96, 128), bf),
            pltpu.VMEM((2048, DH), bf),
            pltpu.VMEM((DH, 2048), bf),
            pltpu.VMEM((2048, DH), bf),
            pltpu.VMEM((2048, DH), jnp.float32),
            pltpu.VMEM((2048, DH), jnp.float32),
            pltpu.VMEM((128, 3 * D), bf),
            pltpu.VMEM((4, 24, 128), jnp.float32),
            dma((NC,)), dma((NC,)), dma((NC,)), dma((NC,)),
            dma((7, 3)), dma((7, 3)), dma((4,)), dma((4,)), dma((7,)),
            dma((6,)), dma((6,)), dma((3,)),
        ],
        compiler_params=pltpu.CompilerParams(
            collective_id=1, has_side_effects=True, vmem_limit_bytes=VMEM_LIMIT
        ),
    )(dctx, qkv, o, lse, small, act, dpre, datt, hid, dbr, ctx, xin)


def widen(a):
    return a.astype(jnp.float32)


class RingReduce:
    def __init__(self, part, total, bufs, ring, ssem, rsem):
        self.part, self.total, self.bufs = part, total, bufs
        self.p, self.up, self.down = ring
        self.ssem, self.rsem = ssem, rsem

    def at(self, k):
        return lax.rem(self.p + k, 4)

    def start(self):
        ra, rb, sa, sb, from_down, from_up = self.bufs
        part, at, ssem, rsem = self.part, self.at, self.ssem, self.rsem
        up, down = self.up, self.down
        self.sent = [
            send(part(at(2), 0), ra, ssem(0), rsem(0), up),
            send(part(at(2), 1), rb, ssem(1), rsem(1), down),
            send(part(at(1), 1), from_down.at[2:4], ssem(2), rsem(2), up),
            send(part(at(3), 0), from_up.at[0:2], ssem(3), rsem(3), down),
        ]

    def middle(self):
        ra, rb, sa, sb, from_down, from_up = self.bufs
        part, at, ssem, rsem = self.part, self.at, self.ssem, self.rsem
        up, down = self.up, self.down
        self.sent[0].wait_recv()
        sa[...] = (widen(part(at(1), 0)[...]) + widen(ra[...])).astype(jnp.bfloat16)
        self.sent.append(send(sa, from_down.at[0:2], ssem(4), rsem(4), up))
        self.sent[1].wait_recv()
        sb[...] = (widen(part(at(3), 1)[...]) + widen(rb[...])).astype(jnp.bfloat16)
        self.sent.append(send(sb, from_up.at[2:4], ssem(5), rsem(5), down))

    def finish(self):
        from_down, from_up = self.bufs[4:]
        for copy in self.sent[2:]:
            copy.wait_recv()
        for k in range(2):
            half = pl.ds(2 * k, 2)
            self.total[half] = (
                widen(self.part(self.p, k)[...]) + widen(from_down[half]) + widen(from_up[half])
            ).astype(jnp.bfloat16)
        for copy in self.sent:
            copy.wait_send()


class Stream:
    STEPS = 12

    def __init__(self, grad, out, m, h, scratch, dsems):
        (big, t1, small, t2, ybuf, u, v) = scratch
        (p1s, p1r, p2s, p2r, ys, yr, ts, tr, ms, as_, ar, g1s, g1r, g2s, g2r) = dsems
        c, s, y, z, x = place()
        along_x, along_z = rings()
        one, two = (along_x, along_z) if h == 0 else (along_z, along_x)
        n = 2 * m + h
        self.m, self.c, self.s, self.y = m, c, s, y
        self.pair = {"ctx": lax.rem(c + 16, 32)}
        self.t1, self.t2, self.u, self.v = t1.at[n], t2.at[n], u.at[n], v.at[n]
        self.ybuf = ybuf.at[n]
        self.out = out
        self.ys, self.yr, self.ts, self.tr = ys.at[n], yr.at[n], ts.at[n], tr.at[n]
        self.ms, self.as_, self.ar = ms.at[n], as_.at[n], ar.at[n]
        cols = pl.ds(h * 512, 512)
        self.reduce1 = RingReduce(
            lambda p, k: grad.at[pl.ds(2 * k, 2), rows64(p), cols], self.t1,
            [b.at[n] for b in big], one, sems(p1s, n), sems(p1r, n),
        )
        self.reduce2 = RingReduce(
            lambda p, k: self.t1.at[pl.ds(2 * k, 2), rows16(p)], self.t2,
            [b.at[n] for b in small], two, sems(p2s, n), sems(p2r, n),
        )
        row = one[0] * 4 + two[0]

        def mine(who):
            at = pl.multiple_of(h * 512 + who * 256, 256)
            return out.at[:, rows16(row), pl.ds(at, 256)]

        self.mine = mine

        def small_block(p, lead=pl.ds(0, 4)):
            return out.at[lead, rows16(one[0] * 4 + p), cols]

        def big_block(p, lead=pl.ds(0, 4)):
            return out.at[lead, rows64(p), cols]

        def half_of(make, k):
            return lambda p: make(p, lead=pl.ds(2 * k, 2))

        self.gather1 = RingGather(
            small_block, half_of(small_block, 0), half_of(small_block, 1), two,
            sems(g1s, n), sems(g1r, n),
        )
        self.gather2 = RingGather(
            big_block, half_of(big_block, 0), half_of(big_block, 1), one,
            sems(g2s, n), sems(g2r, n),
        )

    def step(self, k):
        if k == 0:
            self.reduce1.start()
        elif k == 1:
            self.reduce1.middle()
        elif k == 2:
            self.reduce1.finish()
            self.reduce2.start()
        elif k == 3:
            self.reduce2.middle()
        elif k == 4:
            self.reduce2.finish()
            other = pl.ds(pl.multiple_of(256 - self.y * 256, 256), 256)
            self.sent_y = send(self.t2.at[:, :, other], self.ybuf, self.ys, self.yr, self.pair)
        elif k == 5:
            self.sent_y.wait()
            own = pl.ds(pl.multiple_of(self.y * 256, 256), 256)
            total = (widen(self.t2[:, :, own]) + widen(self.ybuf[...])).astype(jnp.bfloat16)
            if self.m == 0:
                self.v[...] = total
            else:
                self.u[...] = total
                self.turned = []
                for j in range(1, 4):
                    owner = lax.rem(self.s + j, 4)
                    self.turned.append(
                        send(
                            self.u.at[owner], self.v.at[self.s], self.ts.at[j], self.tr.at[j],
                            {"shard": owner},
                        )
                    )
                self.v[self.s] = self.u[self.s]
        elif k == 6:
            if self.m > 0:
                for j in range(1, 4):
                    source = lax.rem(self.s + 4 - j, 4)
                    got = self.v.at[source]
                    remote(got, got, self.ts.at[j], self.tr.at[j], {"shard": source}).wait_recv()
                    self.turned[j - 1].wait_send()
            self.kept = pltpu.make_async_copy(self.v, self.mine(self.y), self.ms)
            self.kept.start()
            self.shared = send(self.v, self.mine(self.y), self.as_, self.ar, self.pair)
        elif k == 7:
            self.kept.wait()
            self.shared.wait_send()
            got = self.mine(1 - self.y)
            remote(got, got, self.as_, self.ar, self.pair).wait_recv()
            self.gather1.start()
        elif k == 8:
            self.gather1.forward()
        elif k == 9:
            self.gather1.finish()
            self.gather2.start()
        elif k == 10:
            self.gather2.forward()
        else:
            self.gather2.finish()


def reduce_kernel(
    act, dbr, hid, dpre, x, dproj, ctx, datt, small_g, ff_out, in_out, qo_out, small_out,
    grads, ra, rb, sa, sb, fd, fu, ra2, rb2, sa2, sb2, fd2, fu2, t1, t2, ybuf, u, v,
    small, small_all, small_s, small_r, *dsems
):
    c, s, *unused = place()
    barrier = pltpu.get_barrier_semaphore()
    signal_ctx_peers(barrier, c)
    for j in range(1, 4):
        pl.semaphore_signal(
            barrier, inc=1, device_id={"shard": lax.rem(s + j, 4)}, device_id_type=MESH
        )
    small[...] = small_g[0] + small_g[1] + small_g[2] + small_g[3]
    pl.semaphore_wait(barrier, NC + 2)
    scratch = ((ra, rb, sa, sb, fd, fu), t1, (ra2, rb2, sa2, sb2, fd2, fu2), t2, ybuf, u, v)
    streams = []
    products = (((act, dbr, 0),), ((hid, dpre, 0),), ((x, dproj, 0), (ctx, datt, 768)))
    for m, (terms, out) in enumerate(zip(products, (ff_out, in_out, qo_out))):
        for left, right, at in terms:
            width = right.shape[-1]

            def block(q, carry):
                part = left[:, :, pl.ds(pl.multiple_of(q * 256, 256), 256)].reshape(512, 256)
                grads[m, q, :, at : at + width] = lax.dot_general(
                    part, right[...].reshape(512, width), (((0,), (0,)), ((), ())),
                    preferred_element_type=jnp.float32,
                ).astype(jnp.bfloat16)
                return carry

            lax.fori_loop(0, 4, block, 0)
        for h in range(2):
            streams.append(Stream(grads.at[m], out, m, h, scratch, dsems))
            streams[-1].step(0)

    def spread(k, carry):
        dest = lax.rem(c + k, NC)
        remote(small, small_all.at[c], small_s.at[k], small_r.at[k], {"ctx": dest}).start()
        return carry

    lax.fori_loop(1, NC, spread, 0)
    for k in range(1, Stream.STEPS):
        for stream in streams:
            stream.step(k)

    def arrive(k, carry):
        source = lax.rem(c + NC - k, NC)
        copy = remote(small, small_all.at[source], small_s.at[k], small_r.at[k], {"ctx": source})
        copy.wait_send()
        copy.wait_recv()
        return carry

    lax.fori_loop(1, NC, arrive, 0)
    small_all[c] = small[...]
    small_out[...] = lax.fori_loop(
        0, NC, lambda k, acc: acc + small_all[k], jnp.zeros((24, 128), jnp.float32)
    )


def reduce_grads(act, dbr, hid, dpre, x, dproj, ctx, datt, small):
    bf, f32 = jnp.bfloat16, jnp.float32
    dma = pltpu.SemaphoreType.DMA
    vm = pltpu.VMEM
    full = jax.ShapeDtypeStruct((4, 256, 1024), bf)

    def ring_bufs(rows):
        return [vm((6, 2, rows, 512), bf)] * 4 + [vm((6, 4, rows, 512), bf)] * 2

    return pl.pallas_call(
        reduce_kernel,
        out_shape=(full, full, full, jax.ShapeDtypeStruct((24, 128), f32)),
        in_specs=[VM] * 9,
        out_specs=(VM,) * 4,
        scratch_shapes=[vm((3, 4, 256, 1024), bf)]
        + ring_bufs(64)
        + ring_bufs(16)
        + [
            vm((6, 4, 64, 512), bf), vm((6, 4, 16, 512), bf), vm((6, 4, 16, 256), bf),
            vm((6, 4, 16, 256), bf), vm((6, 4, 16, 256), bf),
            vm((24, 128), f32), vm((NC, 24, 128), f32), dma((NC,)), dma((NC,)),
            dma((6, 6)), dma((6, 6)), dma((6, 6)), dma((6, 6)), dma((6,)), dma((6,)),
            dma((6, 4)), dma((6, 4)), dma((6,)), dma((6,)), dma((6,)),
            dma((6, 4)), dma((6, 4)), dma((6, 4)), dma((6, 4)),
        ],
        compiler_params=pltpu.CompilerParams(
            collective_id=2, has_side_effects=True, vmem_limit_bytes=VMEM_LIMIT
        ),
    )(act, dbr, hid, dpre, x, dproj, ctx, datt, small)


def widen_kernel(ff, in_, qo, ff_out, in_out, qkv_out, w_out):
    ff_out[...] = widen(ff[0])
    in_out[...] = widen(in_[0])
    qkv_out[...] = widen(qo[0, :, :768])
    w_out[...] = widen(qo[0, :, 768:])


def widen_grads(ff, in_, qo):
    sds = jax.ShapeDtypeStruct
    f32 = jnp.float32
    block = pl.BlockSpec((1, 256, 1024), lambda q: (q, 0, 0))
    return pl.pallas_call(
        widen_kernel,
        grid=(4,),
        out_shape=(
            sds((1024, 1024), f32), sds((256, 4096), f32), sds((256, 3072), f32),
            sds((256, 1024), f32),
        ),
        in_specs=[block] * 3,
        out_specs=(
            pl.BlockSpec((256, 1024), lambda q: (q, 0)),
            pl.BlockSpec((256, 1024), lambda q: (0, q)),
            pl.BlockSpec((256, 768), lambda q: (0, q)),
            pl.BlockSpec((256, 256), lambda q: (0, q)),
        ),
        compiler_params=pltpu.CompilerParams(vmem_limit_bytes=VMEM_LIMIT),
    )(ff, in_, qo)


def local(
    inputs, cotangent, w_qkv, bias_qv, w_out, bias_out, ln1_gain, ln1_bias, w_in, bias_in,
    w_ff_out, bias_ff_out, ln2_gain, ln2_bias,
):
    bf, f32 = jnp.bfloat16, jnp.float32
    small = jnp.concatenate(
        [
            bias_qv.reshape(512), bias_out, ln1_gain, ln1_bias, bias_ff_out, ln2_gain, ln2_bias,
            bias_in, jnp.zeros((1024,), bf),
        ]
    )
    w_qkv_all, small_all = gather_first(w_qkv.reshape(1, 256, 3 * D), small.reshape(32, 128))
    w_qkv_all = w_qkv_all.reshape(D, 3 * D)
    small_all = small_all.reshape(4, 4096).astype(f32)
    bias_q, bias_v, bias_o, gain_one, shift_one, bias_ff, gain_two, shift_two = (
        small_all[:, 256 * k : 256 * k + 256].reshape(D) for k in range(8)
    )
    bias_i = small_all[:, 2048:3072].reshape(FF)
    groups, rows_dev = inputs.shape[0], inputs.shape[1]
    token_count = groups * rows_dev
    tokens_in = inputs.reshape(token_count, D)
    bias_full = jnp.concatenate([bias_q, jnp.zeros((D,), f32), bias_v])
    projected = (jnp.dot(tokens_in, w_qkv_all, preferred_element_type=f32) + bias_full).astype(bf)
    flat_context, qkv, o, lse, w_out_all, w_in_all, w_ff_all = attn_fwd(
        projected, w_out.reshape(1, 256, D), w_in.reshape(1, 256, FF), w_ff_out.reshape(4, 256, D)
    )
    w_out_all = w_out_all.reshape(D, D)
    w_in_all = w_in_all.reshape(D, FF)
    w_ff_all = w_ff_all.reshape(FF, D)
    attended = jnp.dot(flat_context, w_out_all, preferred_element_type=f32) + bias_o
    first_sum = tokens_in.astype(f32) + attended
    hidden = layer_norm(first_sum, gain_one, shift_one)
    hidden_low = hidden.astype(bf)
    pre_act = jnp.dot(hidden_low, w_in_all, preferred_element_type=f32) + bias_i
    act_low = gelu_exact(pre_act).astype(bf)
    branch = jnp.dot(act_low, w_ff_all, preferred_element_type=f32) + bias_ff
    second_sum = hidden + branch
    result_rows = layer_norm(second_sum, gain_two, shift_two)
    upstream = cotangent.reshape(token_count, D).astype(f32)
    unused_two, pull_two = jax.vjp(layer_norm, second_sum, gain_two, shift_two)
    d_second, d_gain_two, d_shift_two = pull_two(upstream)
    d_branch = d_second.astype(bf)
    grad_bias_ff = jnp.sum(d_branch.astype(f32), axis=0)
    d_act = times_transposed(d_branch, w_ff_all)
    unused_act, pull_gelu = jax.vjp(gelu_exact, pre_act)
    d_pre_act = pull_gelu(d_act)[0].astype(bf)
    grad_bias_in = jnp.sum(d_pre_act.astype(f32), axis=0)
    d_hidden = d_second + times_transposed(d_pre_act, w_in_all)
    unused_one, pull_one = jax.vjp(layer_norm, first_sum, gain_one, shift_one)
    d_first, d_gain_one, d_shift_one = pull_one(d_hidden)
    d_attended = d_first.astype(bf)
    grad_bias_out = jnp.sum(d_attended.astype(f32), axis=0)
    d_context = times_transposed(d_attended, w_out_all).astype(bf)
    small_sums = jnp.concatenate(
        [
            a.reshape(4, -1)
            for a in (
                grad_bias_out, d_gain_one, d_shift_one, grad_bias_ff, d_gain_two, d_shift_two,
                grad_bias_in, jnp.zeros((2048,), f32),
            )
        ],
        axis=1,
    ).reshape(4, 24, 128)
    d_projected, dproj_g, act_g, dpre_g, datt_g, hid_g, dbr_g, ctx_g, x_g, small_g = attn_bwd(
        d_context, qkv, o, lse, small_sums, act_low, d_pre_act, d_attended, hidden_low, d_branch,
        flat_context, tokens_in,
    )
    red_ff, red_in, red_qo, sums = reduce_grads(
        act_g, dbr_g, hid_g, dpre_g, x_g, dproj_g, ctx_g, datt_g, small_g
    )
    own_ff, own_in, own_qkv, own_out = widen_grads(red_ff, red_in, red_qo)
    d_inputs = d_first + times_transposed(d_projected, w_qkv_all)
    sums = sums.reshape(3072)

    def own(k):
        return sums[256 * k : 256 * k + 256]

    own_bias_in = sums[1536:2560]
    own_bias_qv = sums[2560:].reshape(2, 256)
    return (
        result_rows.astype(bf).reshape(groups, rows_dev, D),
        d_inputs.reshape(groups, rows_dev, D),
        own_qkv,
        own_bias_qv,
        own_out,
        own(0),
        own(1),
        own(2),
        own_in,
        own_bias_in,
        own_ff,
        own(3),
        own(4),
        own(5),
    )


def solution(mesh):
    specs = (
        P("shard", "ctx", None),
        P("shard", "ctx", None),
        P("shard", None),
        P(None, "shard"),
        P("shard", None),
        P("shard"),
        P("shard"),
        P("shard"),
        P("shard", None),
        P("shard"),
        P("shard", None),
        P("shard"),
        P("shard"),
        P("shard"),
    )
    return jax.shard_map(local, mesh=mesh, in_specs=specs, out_specs=specs, check_vma=False)
```

```python
import jax
import jax.numpy as jnp
from jax import lax
from jax.experimental import pallas as pl
from jax.experimental.pallas import tpu as pltpu
from jax.sharding import PartitionSpec as P

D = 1024
H = 16
DH = 64
FF = 4096
NC = 32
SCALE = DH ** (-0.5)
MESH = pl.DeviceIdType.MESH
NORM_EPS = 1e-05
VMEM_LIMIT = 56 * 1024 * 1024
VM = pl.BlockSpec(memory_space=pltpu.VMEM)
ANY = pl.BlockSpec(memory_space=pl.ANY)


def pack_tokens(src, send, parts):
    def step(hp, carry):
        for g in range(2):
            for part in range(parts):
                cols = pl.ds(pl.multiple_of(part * D + hp * 128, 128), 128)
                a = src[pl.ds(g * 64, 32), cols]
                b = src[pl.ds(g * 64 + 32, 32), cols]
                rows = pl.ds(part * 32, 32)
                send[g * 16 + 2 * hp, rows, :] = jnp.concatenate([a[:, :64], b[:, :64]], axis=1)
                send[g * 16 + 2 * hp + 1, rows, :] = jnp.concatenate(
                    [a[:, 64:], b[:, 64:]], axis=1
                )
        return carry

    lax.fori_loop(0, H // 2, step, 0)


def unpack_tokens(recv, dst, parts):
    def step(hp, carry):
        for g in range(2):
            for part in range(parts):
                cols = pl.ds(pl.multiple_of(part * D + hp * 128, 128), 128)
                rows = pl.ds(part * 32, 32)
                even = recv[g * 16 + 2 * hp, rows, :]
                odd = recv[g * 16 + 2 * hp + 1, rows, :]
                dst[pl.ds(g * 64, 32), cols] = jnp.concatenate([even[:, :64], odd[:, :64]], axis=1)
                dst[pl.ds(g * 64 + 32, 32), cols] = jnp.concatenate(
                    [even[:, 64:], odd[:, 64:]], axis=1
                )
        return carry

    lax.fori_loop(0, H // 2, step, 0)


def a2a_start(send, recv, ssem, rsem, me):
    def step(k, carry):
        dest = lax.rem(me + k, NC)
        pltpu.make_async_remote_copy(
            src_ref=send.at[dest],
            dst_ref=recv.at[me],
            send_sem=ssem.at[k],
            recv_sem=rsem.at[k],
            device_id={"ctx": dest},
            device_id_type=MESH,
        ).start()
        return carry

    lax.fori_loop(1, NC, step, 0)


def a2a_wait(send, recv, ssem, rsem, me):
    def step(k, carry):
        source = lax.rem(me + NC - k, NC)
        copy = pltpu.make_async_remote_copy(
            src_ref=send.at[source],
            dst_ref=recv.at[source],
            send_sem=ssem.at[k],
            recv_sem=rsem.at[k],
            device_id={"ctx": source},
            device_id_type=MESH,
        )
        copy.wait_send()
        copy.wait_recv()
        return carry

    lax.fori_loop(1, NC, step, 0)


def signal_ctx_peers(barrier, me):
    def step(k, carry):
        pl.semaphore_signal(
            barrier, inc=1, device_id={"ctx": lax.rem(me + k, NC)}, device_id_type=MESH
        )
        return carry

    lax.fori_loop(1, NC, step, 0)


def halves(packed):
    return jnp.concatenate([packed[:, :64], packed[:, 64:]], axis=0)


def dot_nt(a, b):
    return lax.dot_general(a, b, (((1,), (1,)), ((), ())), preferred_element_type=jnp.float32)


def dot_nn(a, b):
    return jnp.dot(a, b, preferred_element_type=jnp.float32)


def place():
    c = lax.axis_index("ctx")
    return c, lax.axis_index("shard"), lax.div(c, 16), lax.rem(lax.div(c, 4), 4), lax.rem(c, 4)


def remote(src, dst, send_sem, recv_sem, peer):
    return pltpu.make_async_remote_copy(
        src_ref=src, dst_ref=dst, send_sem=send_sem, recv_sem=recv_sem,
        device_id=peer, device_id_type=MESH,
    )


def send(src, dst, send_sem, recv_sem, peer):
    copy = remote(src, dst, send_sem, recv_sem, peer)
    copy.start()
    return copy


def rings():
    c, unused_s, y, z, x = place()
    along_x = (
        x,
        {"ctx": c - x + lax.rem(x + 1, 4)},
        {"ctx": c - x + lax.rem(x + 3, 4)},
    )
    along_z = (
        z,
        {"ctx": y * 16 + lax.rem(z + 1, 4) * 4 + x},
        {"ctx": y * 16 + lax.rem(z + 3, 4) * 4 + x},
    )
    return along_x, along_z


class RingGather:
    def __init__(self, block, first, second, ring, ssem, rsem):
        self.block, self.first, self.second = block, first, second
        self.p, self.up, self.down = ring
        self.ssem, self.rsem = ssem, rsem

    def at(self, k):
        return lax.rem(self.p + k, 4)

    def start(self):
        own = self.block(self.p)
        self.sent = [
            send(own, own, self.ssem(0), self.rsem(0), self.up),
            send(own, own, self.ssem(1), self.rsem(1), self.down),
        ]

    def forward(self):
        from_down, from_up = self.block(self.at(3)), self.block(self.at(1))
        remote(from_down, from_down, self.ssem(0), self.rsem(0), self.up).wait_recv()
        part = self.first(self.at(3))
        self.sent.append(send(part, part, self.ssem(2), self.rsem(2), self.up))
        remote(from_up, from_up, self.ssem(1), self.rsem(1), self.down).wait_recv()
        part = self.second(self.at(1))
        self.sent.append(send(part, part, self.ssem(3), self.rsem(3), self.down))

    def finish(self):
        part = self.first(self.at(2))
        remote(part, part, self.ssem(2), self.rsem(2), self.up).wait_recv()
        part = self.second(self.at(2))
        remote(part, part, self.ssem(3), self.rsem(3), self.down).wait_recv()
        for copy in self.sent:
            copy.wait_send()


def sems(ref, *lead):
    return lambda k: ref.at[(*lead, k)]


def rows16(index):
    return pl.ds(pl.multiple_of(index * 16, 16), 16)


def rows64(index):
    return pl.ds(pl.multiple_of(index * 64, 64), 64)


class WeightGather:
    STEPS = 7

    def __init__(self, src, dst, n, ls, os, orr, cs, cr, gs, gr, fs, fr):
        c, s, y, z, x = place()
        sibling, cross, unused = group_ids()
        self.sibling, self.cross = mesh_id(sibling), mesh_id(cross)
        self.src, self.dst, self.s = src, dst, s
        self.far, self.far_sib = cross[1], unused[1]
        self.sib_shard = sibling[1]
        self.ls, self.os, self.orr = ls.at[n], os.at[n], orr.at[n]
        self.cs, self.cr, self.fs, self.fr = cs, cr, fs, fr
        self.n = n
        width = src.shape[-1]
        self.half, self.quarter = width // 2, width // 4
        along_x, along_z = rings()
        self.streams = []
        for h in range(2):
            one, two = (along_z, along_x) if h == 0 else (along_x, along_z)
            base = x if h == 0 else z
            cols = pl.ds(h * self.half, self.half)
            cols_a = pl.ds(h * self.half, self.quarter)
            cols_b = pl.ds(h * self.half + self.quarter, self.quarter)
            own = self.dst.at[self.far]

            def small_block(p, cols=cols, base=base, own=own):
                return own.at[:, rows16(base * 4 + p), cols]

            def big_block(p, cols=cols, own=own):
                return own.at[:, rows64(p), cols]

            def part_of(make, cols):
                return lambda p: make(p, cols=cols)

            ring1 = RingGather(
                small_block, part_of(small_block, cols_a), part_of(small_block, cols_b), one,
                sems(gs, n, h, 0), sems(gr, n, h, 0),
            )
            ring2 = RingGather(
                big_block, part_of(big_block, cols_a), part_of(big_block, cols_b), two,
                sems(gs, n, h, 1), sems(gr, n, h, 1),
            )
            row = base * 4 + one[0]
            self.streams.append((h, row, cols, cols_a, cols_b, ring1, ring2, two[0]))
        self.sent = []

    def step(self, k):
        if k == 0:
            for h, row, cols, *unused in self.streams:
                self.sent.append(
                    send(
                        self.src.at[:, rows16(row), cols],
                        self.dst.at[self.s].at[:, rows16(row), cols],
                        self.cs.at[self.n, h], self.cr.at[self.n, h], self.cross,
                    )
                )
            self.local = pltpu.make_async_copy(self.src, self.dst.at[self.s], self.ls)
            self.local.start()
            self.own = send(self.src, self.dst.at[self.s], self.os, self.orr, self.sibling)
        elif k == 1:
            for h, row, cols, cols_a, cols_b, ring1, ring2, p in self.streams:
                got = self.dst.at[self.far].at[:, rows16(row), cols]
                remote(got, got, self.cs.at[self.n, h], self.cr.at[self.n, h], self.cross).wait_recv()
                ring1.start()
        elif k == 2:
            for h, row, cols, cols_a, cols_b, ring1, ring2, p in self.streams:
                ring1.forward()
        elif k == 3:
            for h, row, cols, cols_a, cols_b, ring1, ring2, p in self.streams:
                ring1.finish()
                ring2.start()
                self.pass_on(h, 0, rows64(p), cols)
        elif k == 4:
            for h, row, cols, cols_a, cols_b, ring1, ring2, p in self.streams:
                ring2.forward()
                self.pass_on(h, 1, rows64(lax.rem(p + 3, 4)), cols)
                self.pass_on(h, 2, rows64(lax.rem(p + 1, 4)), cols)
        elif k == 5:
            for h, row, cols, cols_a, cols_b, ring1, ring2, p in self.streams:
                ring2.finish()
                self.pass_on(h, 3, rows64(lax.rem(p + 2, 4)), cols)
        else:
            self.local.wait()
            self.own.wait_send()
            got = self.dst.at[self.sib_shard]
            remote(got, got, self.os, self.orr, self.sibling).wait_recv()
            for h, row, cols, cols_a, cols_b, ring1, ring2, p in self.streams:
                for j, shift in enumerate((0, 3, 1, 2)):
                    got = self.dst.at[self.far_sib].at[:, rows64(lax.rem(p + shift, 4)), cols]
                    remote(
                        got, got, self.fs.at[self.n, h, j], self.fr.at[self.n, h, j], self.sibling
                    ).wait_recv()
            for copy in self.sent:
                copy.wait_send()

    def pass_on(self, h, j, rows, cols):
        part = self.dst.at[self.far].at[:, rows, cols]
        self.sent.append(
            send(part, part, self.fs.at[self.n, h, j], self.fr.at[self.n, h, j], self.sibling)
        )


def weight_sems(count):
    dma = pltpu.SemaphoreType.DMA
    return [
        dma((count,)), dma((count,)), dma((count,)), dma((count, 2)), dma((count, 2)),
        dma((count, 2, 2, 4)), dma((count, 2, 2, 4)), dma((count, 2, 4)), dma((count, 2, 4)),
    ]


def group_ids():
    c = lax.axis_index("ctx")
    s = lax.axis_index("shard")
    core = lax.rem(s, 2)
    other = 2 - 2 * lax.div(s, 2)
    sibling = s + 1 - 2 * core
    cross_c = lax.rem(c + NC // 2, NC)
    return ((c, sibling), (cross_c, other + core), (cross_c, other + 1 - core))


def mesh_id(pair):
    return {"ctx": pair[0], "shard": pair[1]}


QB = 128


def normalized(values):
    centered = values - jnp.mean(values, axis=-1, keepdims=True)
    scale = lax.rsqrt(jnp.mean(centered * centered, axis=-1, keepdims=True) + NORM_EPS)
    return centered * scale, scale


def norm_back(upstream, unit, scale):
    mean = jnp.mean(upstream, axis=-1, keepdims=True)
    along = jnp.mean(upstream * unit, axis=-1, keepdims=True)
    return scale * (upstream - mean - unit * along)


def layer_kernel(
    x, cot, b_qv, b_out, g_one, s_one, b_ff, g_two, s_two, b_in, w_qkv, w_out, w_in, w_ff,
    result, d_inputs, dproj_g, act_g, dpre_g, datt_g, hid_g, dbr_g, ctx_g, x_g, small_g,
    wq, wo, wi, wf, params, params_all, proj, q_send, q_recv, c_send, c_recv, g_send, g_recv,
    p_send, p_recv, keys, vt, kt, vals, dk, dv, o_s, lse_s, act, gelu_d, dpre, datt, dctx, dproj,
    hidden, unit_one, d_first, small,
    qss, qrs, css, crs, gss, grs, pss, prs, xs, xr, fs, fr, ls, es, er, els, ms, mr, ml, *wsems
):
    bf, f32 = jnp.bfloat16, jnp.float32
    me = lax.axis_index("ctx")
    shard = lax.axis_index("shard")
    peers = group_ids()
    barrier = pltpu.get_barrier_semaphore()
    signal_ctx_peers(barrier, me)
    for peer in peers:
        pl.semaphore_signal(barrier, inc=1, device_id=mesh_id(peer), device_id_type=MESH)
    x_g[0] = x[...]
    for n, ref in enumerate((b_out, g_one, s_one, b_ff, g_two, s_two)):
        params[2 * n : 2 * n + 2, :] = widen(ref[...])
    params[12:20, :] = widen(b_in[...])
    for n in range(2):
        for k in range(2):
            row = 20 + 2 * n + k
            params[row : row + 1, :] = widen(b_qv[n : n + 1, 128 * k : 128 * k + 128])
    params_all[shard] = params[...]
    pl.semaphore_wait(barrier, NC + 2)

    gather_q, *gathers = [
        WeightGather(w, out, n, *wsems)
        for n, (w, out) in enumerate(((w_qkv, wq), (w_out, wo), (w_in, wi), (w_ff, wf)))
    ]
    early, late = gathers[:2], gathers[2:]

    def advance(group, k):
        for gather in group:
            gather.step(k)

    def to_peer(src, dst, send_sem, recv_sem, peer):
        return send(src, dst, send_sem, recv_sem, mesh_id(peer))

    pending, arriving = [], {}

    def share_whole(n, ref):
        pending.append(to_peer(ref.at[0], ref.at[1], xs.at[n, 0], xr.at[n, 0], peers[0]))
        arriving[n] = to_peer(ref.at[0], ref.at[2], xs.at[n, 1], xr.at[n, 1], peers[1])

    def pass_on(n, ref):
        arriving[n].wait()
        pending.append(to_peer(ref.at[2], ref.at[3], fs.at[n], fr.at[n], peers[0]))

    def share_slices(n, src, dst, width):
        for k, peer in enumerate(peers):
            cols = pl.ds(pl.multiple_of(peer[1] * width, width), width)
            pending.append(
                to_peer(src.at[:, cols], dst.at[k + 1], xs.at[4 + n, k], xr.at[4 + n, k], peer)
            )
        cols = pl.ds(pl.multiple_of(shard * width, width), width)
        own = pltpu.make_async_copy(src.at[:, cols], dst.at[0], ls.at[n])
        own.start()
        pending.append(own)

    gather_q.step(0)
    sent_params = [
        to_peer(params, params_all.at[shard], ms.at[k], mr.at[k], peer)
        for k, peer in enumerate(peers)
    ]
    advance(gathers, 0)
    share_whole(3, x_g)
    gather_q.step(1)
    gather_q.step(2)
    gather_q.step(3)
    advance(gathers, 1)
    gather_q.step(4)
    advance(gathers, 2)
    gather_q.step(5)
    gather_q.step(6)
    advance(early, 3)
    for k, peer in enumerate(peers):
        sent_params[k].wait_send()
        got = params_all.at[peer[1]]
        remote(got, got, ms.at[k], mr.at[k], mesh_id(peer)).wait_recv()

    def vector(n):
        return jnp.concatenate(
            [params_all[k // 2, 2 * n + k % 2 : 2 * n + k % 2 + 1, :] for k in range(8)], axis=1
        )

    def cols_of(j):
        return pl.ds(pl.multiple_of(j * D, D), D)

    def project(j, carry):
        part = jnp.where(j == 0, 1.0, 0.0) * vector(10) + jnp.where(j == 2, 1.0, 0.0) * vector(11)
        weight = wq[:, 0, :, cols_of(j)].reshape(D, D)
        proj[:, cols_of(j)] = (dot_nn(x[...], weight) + part).astype(bf)
        return carry

    lax.fori_loop(0, 3, project, 0)
    pack_tokens(proj, q_send, 3)
    a2a_start(q_send, q_recv, qss, qrs, me)
    q_recv[me] = q_send[me]
    a2a_wait(q_send, q_recv, qss, qrs, me)
    advance(early, 4)
    advance(late, 3)
    keys[...] = halves(q_recv[:, 32:64, :].reshape(1024, 128))
    vals[...] = halves(q_recv[:, 64:96, :].reshape(1024, 128))
    vp = widen(q_recv[:, 64:96, :].reshape(1024, 128)).T.astype(bf)
    vt[...] = jnp.concatenate([vp[:64], vp[64:]], axis=1)
    kp = widen(q_recv[:, 32:64, :].reshape(1024, 128)).T.astype(bf)
    kt[...] = jnp.concatenate([kp[:64], kp[64:]], axis=1)
    steps = 1024 // QB
    blocks_of = QB // 32

    def attend(i, carry):
        blocks = pl.ds(i * blocks_of, blocks_of)
        qb = halves(q_recv[blocks, 0:32, :].reshape(QB, 128) * bf(SCALE))
        s = dot_nt(keys[...], qb)
        m = jnp.max(s, axis=0, keepdims=True)
        p = jnp.exp(s - m)
        total = jnp.sum(p, axis=0, keepdims=True)
        ot = dot_nn(vt[...], p.astype(bf)) / total
        o = jnp.concatenate([ot[:, :QB], ot[:, QB:]], axis=0).T
        o_s[pl.ds(pl.multiple_of(i * QB, QB), QB), :] = o
        lse_s[i] = m + jnp.log(total)
        c_send[blocks] = o.astype(bf).reshape(blocks_of, 32, 128)
        return carry

    lax.fori_loop(0, steps // 2, attend, 0)
    advance(early, 5)
    advance(late, 4)
    lax.fori_loop(steps // 2, steps, attend, 0)
    a2a_start(c_send, c_recv, css, crs, me)
    c_recv[me] = c_send[me]
    a2a_wait(c_send, c_recv, css, crs, me)
    unpack_tokens(c_recv, ctx_g.at[0], 1)
    share_whole(2, ctx_g)
    advance(early, 6)

    w_out_whole = wo[...].reshape(D, D)
    first_sum = widen(x[...]) + (dot_nn(ctx_g[0], w_out_whole) + vector(0))
    unit, scale_one = normalized(first_sum)
    unit_one[...] = unit
    hidden[...] = unit * vector(1) + vector(2)
    hid_g[0] = hidden[...].astype(bf)
    share_whole(0, hid_g)
    pass_on(3, x_g)

    def feed(j, carry):
        bias = jnp.concatenate([params_all[j, 12 + k : 13 + k, :] for k in range(8)], axis=1)
        pre = dot_nn(hid_g[0], wi[:, 0, :, cols_of(j)].reshape(D, D)) + bias
        grown = 0.5 * (1.0 + lax.erf(pre * 0.7071067811865476))
        act[:, cols_of(j)] = (pre * grown).astype(bf)
        gelu_d[:, cols_of(j)] = grown + pre * (0.3989422804014327 * jnp.exp(-0.5 * pre * pre))
        return carry

    lax.fori_loop(0, 4, feed, 0)
    share_slices(0, act, act_g, 1024)
    advance(late, 5)
    advance(late, 6)

    def feed_out(j, total):
        return total + dot_nn(act[:, cols_of(j)], wf[j].reshape(D, D))

    branch = lax.fori_loop(0, 4, feed_out, jnp.zeros((128, D), f32))
    unit_two, scale_two = normalized(hidden[...] + (branch + vector(3)))
    result[...] = (unit_two * vector(4) + vector(5)).astype(bf)

    def put_sums(n, values):
        sums = jnp.sum(values, axis=0, keepdims=True)
        for k in range(8):
            row = 2 * n + k % 2
            small[k // 2, row : row + 1, :] = sums[:, 128 * k : 128 * k + 128]

    upstream = widen(cot[...])
    put_sums(4, upstream * unit_two)
    put_sums(5, upstream)
    d_second = norm_back(upstream * vector(4), unit_two, scale_two)
    dbr_g[0] = d_second.astype(bf)
    share_whole(1, dbr_g)
    put_sums(3, widen(dbr_g[0]))

    def feed_back(j, total):
        d_act = dot_nt(dbr_g[0], wf[j].reshape(D, D))
        part = (d_act * gelu_d[:, cols_of(j)]).astype(bf)
        dpre[:, cols_of(j)] = part
        sums = jnp.sum(widen(part), axis=0, keepdims=True)
        for k in range(8):
            small[j, 12 + k : 13 + k, :] = sums[:, 128 * k : 128 * k + 128]
        return total + dot_nt(part, wi[:, 0, :, cols_of(j)].reshape(D, D))

    d_hidden = lax.fori_loop(0, 4, feed_back, d_second)
    share_slices(1, dpre, dpre_g, 1024)
    put_sums(1, d_hidden * unit_one[...])
    put_sums(2, d_hidden)
    d_first[...] = norm_back(d_hidden * vector(1), unit_one[...], scale_one)
    datt[...] = d_first[...].astype(bf)
    put_sums(0, widen(datt[...]))
    dctx[...] = dot_nt(datt[...], wo[...].reshape(D, D)).astype(bf)
    pack_tokens(dctx, g_send, 1)
    a2a_start(g_send, g_recv, gss, grs, me)
    share_slices(2, datt, datt_g, 256)
    g_recv[me] = g_send[me]
    dk[...] = jnp.zeros_like(dk)
    dv[...] = jnp.zeros_like(dv)
    pass_on(2, ctx_g)
    pass_on(0, hid_g)
    a2a_wait(g_send, g_recv, gss, grs, me)

    def attend_back(i, carry):
        blocks = pl.ds(i * blocks_of, blocks_of)
        qb = halves(q_recv[blocks, 0:32, :].reshape(QB, 128) * bf(SCALE))
        dop = g_recv[blocks].reshape(QB, 128)
        o = o_s[pl.ds(pl.multiple_of(i * QB, QB), QB), :]
        prod = (widen(dop) * o).T
        delta = jnp.concatenate(
            [
                jnp.sum(prod[:64], axis=0, keepdims=True),
                jnp.sum(prod[64:], axis=0, keepdims=True),
            ],
            axis=1,
        )
        dob = halves(dop)
        probs = jnp.exp(dot_nt(keys[...], qb) - lse_s[i])
        dv[...] += dot_nn(probs.astype(bf), dob)
        ds = (probs * (dot_nt(vals[...], dob) - delta)).astype(bf)
        dk[...] += dot_nn(ds, qb)
        dqt = dot_nn(kt[...], ds) * SCALE
        dq = jnp.concatenate([dqt[:, :QB], dqt[:, QB:]], axis=0).T
        p_send[blocks, 0:32, :] = dq.astype(bf).reshape(blocks_of, 32, 128)
        return carry

    lax.fori_loop(0, steps, attend_back, 0)
    for n, total in enumerate((dk, dv)):
        packed = jnp.concatenate([total[0:1024, :], total[1024:2048, :]], axis=1)
        p_send[:, 32 + 32 * n : 64 + 32 * n, :] = packed.astype(bf).reshape(NC, 32, 128)
    a2a_start(p_send, p_recv, pss, prs, me)
    p_recv[me] = p_send[me]
    pass_on(1, dbr_g)
    a2a_wait(p_send, p_recv, pss, prs, me)
    unpack_tokens(p_recv, dproj, 3)
    for k, peer in enumerate(peers):
        cols = pl.ds(pl.multiple_of(peer[1] * 768, 256), 768)
        pending.append(to_peer(dproj.at[:, cols], dproj_g.at[k + 1], es.at[k], er.at[k], peer))
    cols = pl.ds(pl.multiple_of(shard * 768, 256), 768)
    own = pltpu.make_async_copy(dproj.at[:, cols], dproj_g.at[0], els.at[0])
    own.start()
    pending.append(own)
    put_sums(10, widen(dproj[:, 0:D]))
    put_sums(11, widen(dproj[:, 2 * D : 3 * D]))
    for k, peer in enumerate(peers):
        pending.append(
            to_peer(small.at[peer[1]], small_g.at[k + 1], es.at[3 + k], er.at[3 + k], peer)
        )
    small_g[0] = small[shard]

    def back_in(j, total):
        weight = wq[:, 0, :, cols_of(j)].reshape(D, D)
        return total + dot_nt(dproj[:, cols_of(j)], weight)

    d_inputs[...] = lax.fori_loop(0, 3, back_in, d_first[...])
    for copy in pending:
        copy.wait()


def layer(x, cot, smalls, weights):
    bf, f32 = jnp.bfloat16, jnp.float32
    sds = jax.ShapeDtypeStruct
    dma = pltpu.SemaphoreType.DMA
    vm = pltpu.VMEM
    rows = (128, D)
    return pl.pallas_call(
        layer_kernel,
        out_shape=(
            sds(rows, bf), sds(rows, f32), sds((4, 128, 768), bf), sds((4, *rows), bf),
            sds((4, *rows), bf), sds((4, 128, 256), bf), sds((4, *rows), bf), sds((4, *rows), bf),
            sds((4, *rows), bf), sds((4, *rows), bf), sds((4, 24, 128), f32),
        ),
        in_specs=[VM] * 10 + [ANY] * 4,
        out_specs=(VM,) * 11,
        scratch_shapes=[vm((4, *w.shape), bf) for w in weights]
        + [
            vm((24, 128), f32), vm((4, 24, 128), f32), vm((128, 3 * D), bf),
            vm((NC, 96, 128), bf), vm((NC, 96, 128), bf), vm((NC, 32, 128), bf),
            vm((NC, 32, 128), bf), vm((NC, 32, 128), bf), vm((NC, 32, 128), bf),
            vm((NC, 96, 128), bf), vm((NC, 96, 128), bf), vm((2048, DH), bf),
            vm((DH, 2048), bf), vm((DH, 2048), bf), vm((2048, DH), bf), vm((2048, DH), f32),
            vm((2048, DH), f32), vm((1024, 128), f32), vm((1024 // QB, 1, 2 * QB), f32),
            vm((128, FF), bf), vm((128, FF), f32), vm((128, FF), bf), vm(rows, bf), vm(rows, bf),
            vm((128, 3 * D), bf), vm(rows, f32), vm(rows, f32), vm(rows, f32),
            vm((4, 24, 128), f32),
        ]
        + [dma((NC,))] * 8
        + [
            dma((7, 3)), dma((7, 3)), dma((4,)), dma((4,)), dma((3,)),
            dma((6,)), dma((6,)), dma((1,)), dma((3,)), dma((3,)), dma,
        ]
        + weight_sems(4),
        compiler_params=pltpu.CompilerParams(
            collective_id=0, has_side_effects=True, vmem_limit_bytes=62 * 1024 * 1024
        ),
    )(x, cot, *smalls, *weights)


def widen(a):
    return a.astype(jnp.float32)


class RingReduce:
    def __init__(self, part, total, bufs, ring, ssem, rsem):
        self.part, self.total, self.bufs = part, total, bufs
        self.p, self.up, self.down = ring
        self.ssem, self.rsem = ssem, rsem

    def at(self, k):
        return lax.rem(self.p + k, 4)

    def start(self):
        ra, rb, sa, sb, from_down, from_up = self.bufs
        part, at, ssem, rsem = self.part, self.at, self.ssem, self.rsem
        up, down = self.up, self.down
        self.sent = [
            send(part(at(2), 0), ra, ssem(0), rsem(0), up),
            send(part(at(2), 1), rb, ssem(1), rsem(1), down),
            send(part(at(1), 1), from_down.at[2:4], ssem(2), rsem(2), up),
            send(part(at(3), 0), from_up.at[0:2], ssem(3), rsem(3), down),
        ]

    def middle(self):
        ra, rb, sa, sb, from_down, from_up = self.bufs
        part, at, ssem, rsem = self.part, self.at, self.ssem, self.rsem
        up, down = self.up, self.down
        self.sent[0].wait_recv()
        sa[...] = (widen(part(at(1), 0)[...]) + widen(ra[...])).astype(jnp.bfloat16)
        self.sent.append(send(sa, from_down.at[0:2], ssem(4), rsem(4), up))
        self.sent[1].wait_recv()
        sb[...] = (widen(part(at(3), 1)[...]) + widen(rb[...])).astype(jnp.bfloat16)
        self.sent.append(send(sb, from_up.at[2:4], ssem(5), rsem(5), down))

    def finish(self):
        from_down, from_up = self.bufs[4:]
        for copy in self.sent[2:]:
            copy.wait_recv()
        for k in range(2):
            half = pl.ds(2 * k, 2)
            self.total[half] = (
                widen(self.part(self.p, k)[...]) + widen(from_down[half]) + widen(from_up[half])
            ).astype(jnp.bfloat16)
        for copy in self.sent:
            copy.wait_send()


class Stream:
    STEPS = 12

    def __init__(self, grad, out, m, h, scratch, dsems):
        (big, t1, small, t2, ybuf, u, v) = scratch
        (p1s, p1r, p2s, p2r, ys, yr, ts, tr, ms, as_, ar, g1s, g1r, g2s, g2r) = dsems
        c, s, y, z, x = place()
        along_x, along_z = rings()
        one, two = (along_x, along_z) if h == 0 else (along_z, along_x)
        n = 2 * m + h
        self.m, self.c, self.s, self.y = m, c, s, y
        self.pair = {"ctx": lax.rem(c + 16, 32)}
        self.t1, self.t2, self.u, self.v = t1.at[n], t2.at[n], u.at[n], v.at[n]
        self.ybuf = ybuf.at[n]
        self.out = out
        self.ys, self.yr, self.ts, self.tr = ys.at[n], yr.at[n], ts.at[n], tr.at[n]
        self.ms, self.as_, self.ar = ms.at[n], as_.at[n], ar.at[n]
        cols = pl.ds(h * 512, 512)
        self.reduce1 = RingReduce(
            lambda p, k: grad.at[pl.ds(2 * k, 2), rows64(p), cols], self.t1,
            [b.at[n] for b in big], one, sems(p1s, n), sems(p1r, n),
        )
        self.reduce2 = RingReduce(
            lambda p, k: self.t1.at[pl.ds(2 * k, 2), rows16(p)], self.t2,
            [b.at[n] for b in small], two, sems(p2s, n), sems(p2r, n),
        )
        row = one[0] * 4 + two[0]

        def mine(who):
            at = pl.multiple_of(h * 512 + who * 256, 256)
            return out.at[:, rows16(row), pl.ds(at, 256)]

        self.mine = mine

        def small_block(p, lead=pl.ds(0, 4)):
            return out.at[lead, rows16(one[0] * 4 + p), cols]

        def big_block(p, lead=pl.ds(0, 4)):
            return out.at[lead, rows64(p), cols]

        def half_of(make, k):
            return lambda p: make(p, lead=pl.ds(2 * k, 2))

        self.gather1 = RingGather(
            small_block, half_of(small_block, 0), half_of(small_block, 1), two,
            sems(g1s, n), sems(g1r, n),
        )
        self.gather2 = RingGather(
            big_block, half_of(big_block, 0), half_of(big_block, 1), one,
            sems(g2s, n), sems(g2r, n),
        )

    def step(self, k):
        if k == 0:
            self.reduce1.start()
        elif k == 1:
            self.reduce1.middle()
        elif k == 2:
            self.reduce1.finish()
            self.reduce2.start()
        elif k == 3:
            self.reduce2.middle()
        elif k == 4:
            self.reduce2.finish()
            other = pl.ds(pl.multiple_of(256 - self.y * 256, 256), 256)
            self.sent_y = send(self.t2.at[:, :, other], self.ybuf, self.ys, self.yr, self.pair)
        elif k == 5:
            self.sent_y.wait()
            own = pl.ds(pl.multiple_of(self.y * 256, 256), 256)
            total = (widen(self.t2[:, :, own]) + widen(self.ybuf[...])).astype(jnp.bfloat16)
            if self.m == 0:
                self.v[...] = total
            else:
                self.u[...] = total
                self.turned = []
                for j in range(1, 4):
                    owner = lax.rem(self.s + j, 4)
                    self.turned.append(
                        send(
                            self.u.at[owner], self.v.at[self.s], self.ts.at[j], self.tr.at[j],
                            {"shard": owner},
                        )
                    )
                self.v[self.s] = self.u[self.s]
        elif k == 6:
            if self.m > 0:
                for j in range(1, 4):
                    source = lax.rem(self.s + 4 - j, 4)
                    got = self.v.at[source]
                    remote(got, got, self.ts.at[j], self.tr.at[j], {"shard": source}).wait_recv()
                    self.turned[j - 1].wait_send()
            self.kept = pltpu.make_async_copy(self.v, self.mine(self.y), self.ms)
            self.kept.start()
            self.shared = send(self.v, self.mine(self.y), self.as_, self.ar, self.pair)
        elif k == 7:
            self.kept.wait()
            self.shared.wait_send()
            got = self.mine(1 - self.y)
            remote(got, got, self.as_, self.ar, self.pair).wait_recv()
            self.gather1.start()
        elif k == 8:
            self.gather1.forward()
        elif k == 9:
            self.gather1.finish()
            self.gather2.start()
        elif k == 10:
            self.gather2.forward()
        else:
            self.gather2.finish()


def reduce_kernel(
    act, dbr, hid, dpre, x, dproj, ctx, datt, small_g, ff_out, in_out, qo_out, small_out,
    grads, ra, rb, sa, sb, fd, fu, ra2, rb2, sa2, sb2, fd2, fu2, t1, t2, ybuf, u, v,
    small, small_all, small_s, small_r, *dsems
):
    c, s, *unused = place()
    barrier = pltpu.get_barrier_semaphore()
    signal_ctx_peers(barrier, c)
    for j in range(1, 4):
        pl.semaphore_signal(
            barrier, inc=1, device_id={"shard": lax.rem(s + j, 4)}, device_id_type=MESH
        )
    small[...] = small_g[0] + small_g[1] + small_g[2] + small_g[3]
    pl.semaphore_wait(barrier, NC + 2)
    scratch = ((ra, rb, sa, sb, fd, fu), t1, (ra2, rb2, sa2, sb2, fd2, fu2), t2, ybuf, u, v)
    streams = []
    products = (((act, dbr, 0),), ((hid, dpre, 0),), ((x, dproj, 0), (ctx, datt, 768)))
    for m, (terms, out) in enumerate(zip(products, (ff_out, in_out, qo_out))):
        for left, right, at in terms:
            width = right.shape[-1]

            def block(q, carry):
                part = left[:, :, pl.ds(pl.multiple_of(q * 256, 256), 256)].reshape(512, 256)
                grads[m, q, :, at : at + width] = lax.dot_general(
                    part, right[...].reshape(512, width), (((0,), (0,)), ((), ())),
                    preferred_element_type=jnp.float32,
                ).astype(jnp.bfloat16)
                return carry

            lax.fori_loop(0, 4, block, 0)
        for h in range(2):
            streams.append(Stream(grads.at[m], out, m, h, scratch, dsems))
            streams[-1].step(0)

    def spread(k, carry):
        dest = lax.rem(c + k, NC)
        remote(small, small_all.at[c], small_s.at[k], small_r.at[k], {"ctx": dest}).start()
        return carry

    lax.fori_loop(1, NC, spread, 0)
    for k in range(1, Stream.STEPS):
        for stream in streams:
            stream.step(k)

    def arrive(k, carry):
        source = lax.rem(c + NC - k, NC)
        copy = remote(small, small_all.at[source], small_s.at[k], small_r.at[k], {"ctx": source})
        copy.wait_send()
        copy.wait_recv()
        return carry

    lax.fori_loop(1, NC, arrive, 0)
    small_all[c] = small[...]
    small_out[...] = lax.fori_loop(
        0, NC, lambda k, acc: acc + small_all[k], jnp.zeros((24, 128), jnp.float32)
    )


def reduce_grads(act, dbr, hid, dpre, x, dproj, ctx, datt, small):
    bf, f32 = jnp.bfloat16, jnp.float32
    dma = pltpu.SemaphoreType.DMA
    vm = pltpu.VMEM
    full = jax.ShapeDtypeStruct((4, 256, 1024), bf)

    def ring_bufs(rows):
        return [vm((6, 2, rows, 512), bf)] * 4 + [vm((6, 4, rows, 512), bf)] * 2

    return pl.pallas_call(
        reduce_kernel,
        out_shape=(full, full, full, jax.ShapeDtypeStruct((24, 128), f32)),
        in_specs=[VM] * 9,
        out_specs=(VM,) * 4,
        scratch_shapes=[vm((3, 4, 256, 1024), bf)]
        + ring_bufs(64)
        + ring_bufs(16)
        + [
            vm((6, 4, 64, 512), bf), vm((6, 4, 16, 512), bf), vm((6, 4, 16, 256), bf),
            vm((6, 4, 16, 256), bf), vm((6, 4, 16, 256), bf),
            vm((24, 128), f32), vm((NC, 24, 128), f32), dma((NC,)), dma((NC,)),
            dma((6, 6)), dma((6, 6)), dma((6, 6)), dma((6, 6)), dma((6,)), dma((6,)),
            dma((6, 4)), dma((6, 4)), dma((6,)), dma((6,)), dma((6,)),
            dma((6, 4)), dma((6, 4)), dma((6, 4)), dma((6, 4)),
        ],
        compiler_params=pltpu.CompilerParams(
            collective_id=2, has_side_effects=True, vmem_limit_bytes=VMEM_LIMIT
        ),
    )(act, dbr, hid, dpre, x, dproj, ctx, datt, small)


def widen_kernel(ff, in_, qo, ff_out, in_out, qkv_out, w_out):
    ff_out[...] = widen(ff[0])
    in_out[...] = widen(in_[0])
    qkv_out[...] = widen(qo[0, :, :768])
    w_out[...] = widen(qo[0, :, 768:])


def widen_grads(ff, in_, qo):
    sds = jax.ShapeDtypeStruct
    f32 = jnp.float32
    block = pl.BlockSpec((1, 256, 1024), lambda q: (q, 0, 0))
    return pl.pallas_call(
        widen_kernel,
        grid=(4,),
        out_shape=(
            sds((1024, 1024), f32), sds((256, 4096), f32), sds((256, 3072), f32),
            sds((256, 1024), f32),
        ),
        in_specs=[block] * 3,
        out_specs=(
            pl.BlockSpec((256, 1024), lambda q: (q, 0)),
            pl.BlockSpec((256, 1024), lambda q: (0, q)),
            pl.BlockSpec((256, 768), lambda q: (0, q)),
            pl.BlockSpec((256, 256), lambda q: (0, q)),
        ),
        compiler_params=pltpu.CompilerParams(vmem_limit_bytes=VMEM_LIMIT),
    )(ff, in_, qo)


def local(
    inputs, cotangent, w_qkv, bias_qv, w_out, bias_out, ln1_gain, ln1_bias, w_in, bias_in,
    w_ff_out, bias_ff_out, ln2_gain, ln2_bias,
):
    smalls = (bias_out, ln1_gain, ln1_bias, bias_ff_out, ln2_gain, ln2_bias)
    result, d_inputs, dproj_g, act_g, dpre_g, datt_g, hid_g, dbr_g, ctx_g, x_g, small_g = layer(
        inputs.reshape(128, D),
        cotangent.reshape(128, D),
        (bias_qv, *(a.reshape(2, 128) for a in smalls), bias_in.reshape(8, 128)),
        (
            w_qkv.reshape(1, 256, 3 * D), w_out.reshape(1, 256, D), w_in.reshape(1, 256, FF),
            w_ff_out.reshape(4, 256, D),
        ),
    )
    red_ff, red_in, red_qo, sums = reduce_grads(
        act_g, dbr_g, hid_g, dpre_g, x_g, dproj_g, ctx_g, datt_g, small_g
    )
    own_ff, own_in, own_qkv, own_out = widen_grads(red_ff, red_in, red_qo)
    sums = sums.reshape(3072)

    def own(k):
        return sums[256 * k : 256 * k + 256]

    return (
        result.reshape(inputs.shape),
        d_inputs.reshape(inputs.shape),
        own_qkv,
        sums[2560:].reshape(2, 256),
        own_out,
        own(0),
        own(1),
        own(2),
        own_in,
        sums[1536:2560],
        own_ff,
        own(3),
        own(4),
        own(5),
    )


def solution(mesh):
    specs = (
        P("shard", "ctx", None),
        P("shard", "ctx", None),
        P("shard", None),
        P(None, "shard"),
        P("shard", None),
        P("shard"),
        P("shard"),
        P("shard"),
        P("shard", None),
        P("shard"),
        P("shard", None),
        P("shard"),
        P("shard"),
        P("shard"),
    )
    return jax.shard_map(local, mesh=mesh, in_specs=specs, out_specs=specs, check_vma=False)
```

```python
import jax
import jax.numpy as jnp
from jax import lax
from jax.experimental import pallas as pl
from jax.experimental.pallas import tpu as pltpu
from jax.sharding import PartitionSpec as P

D = 1024
H = 16
DH = 64
FF = 4096
NC = 32
SCALE = DH ** (-0.5)
MESH = pl.DeviceIdType.MESH
NORM_EPS = 1e-05
VMEM_LIMIT = 56 * 1024 * 1024
VM = pl.BlockSpec(memory_space=pltpu.VMEM)
ANY = pl.BlockSpec(memory_space=pl.ANY)


def pack_tokens(src, send, parts):
    def step(hp, carry):
        for g in range(2):
            for part in range(parts):
                cols = pl.ds(pl.multiple_of(part * D + hp * 128, 128), 128)
                a = src[pl.ds(g * 64, 32), cols]
                b = src[pl.ds(g * 64 + 32, 32), cols]
                rows = pl.ds(part * 32, 32)
                send[g * 16 + 2 * hp, rows, :] = jnp.concatenate([a[:, :64], b[:, :64]], axis=1)
                send[g * 16 + 2 * hp + 1, rows, :] = jnp.concatenate(
                    [a[:, 64:], b[:, 64:]], axis=1
                )
        return carry

    lax.fori_loop(0, H // 2, step, 0)


def unpack_tokens(recv, dst, parts):
    def step(hp, carry):
        for g in range(2):
            for part in range(parts):
                cols = pl.ds(pl.multiple_of(part * D + hp * 128, 128), 128)
                rows = pl.ds(part * 32, 32)
                even = recv[g * 16 + 2 * hp, rows, :]
                odd = recv[g * 16 + 2 * hp + 1, rows, :]
                dst[pl.ds(g * 64, 32), cols] = jnp.concatenate([even[:, :64], odd[:, :64]], axis=1)
                dst[pl.ds(g * 64 + 32, 32), cols] = jnp.concatenate(
                    [even[:, 64:], odd[:, 64:]], axis=1
                )
        return carry

    lax.fori_loop(0, H // 2, step, 0)


def a2a_start(send, recv, ssem, rsem, me):
    def step(k, carry):
        dest = lax.rem(me + k, NC)
        pltpu.make_async_remote_copy(
            src_ref=send.at[dest],
            dst_ref=recv.at[me],
            send_sem=ssem.at[k],
            recv_sem=rsem.at[k],
            device_id={"ctx": dest},
            device_id_type=MESH,
        ).start()
        return carry

    lax.fori_loop(1, NC, step, 0)


def a2a_wait(send, recv, ssem, rsem, me):
    def step(k, carry):
        source = lax.rem(me + NC - k, NC)
        copy = pltpu.make_async_remote_copy(
            src_ref=send.at[source],
            dst_ref=recv.at[source],
            send_sem=ssem.at[k],
            recv_sem=rsem.at[k],
            device_id={"ctx": source},
            device_id_type=MESH,
        )
        copy.wait_send()
        copy.wait_recv()
        return carry

    lax.fori_loop(1, NC, step, 0)


def signal_ctx_peers(barrier, me):
    def step(k, carry):
        pl.semaphore_signal(
            barrier, inc=1, device_id={"ctx": lax.rem(me + k, NC)}, device_id_type=MESH
        )
        return carry

    lax.fori_loop(1, NC, step, 0)


def halves(packed):
    return jnp.concatenate([packed[:, :64], packed[:, 64:]], axis=0)


def dot_nt(a, b):
    return lax.dot_general(a, b, (((1,), (1,)), ((), ())), preferred_element_type=jnp.float32)


def dot_nn(a, b):
    return jnp.dot(a, b, preferred_element_type=jnp.float32)


def place():
    c = lax.axis_index("ctx")
    return c, lax.axis_index("shard"), lax.div(c, 16), lax.rem(lax.div(c, 4), 4), lax.rem(c, 4)


def remote(src, dst, send_sem, recv_sem, peer):
    return pltpu.make_async_remote_copy(
        src_ref=src, dst_ref=dst, send_sem=send_sem, recv_sem=recv_sem,
        device_id=peer, device_id_type=MESH,
    )


def send(src, dst, send_sem, recv_sem, peer):
    copy = remote(src, dst, send_sem, recv_sem, peer)
    copy.start()
    return copy


def rings():
    c, unused_s, y, z, x = place()
    along_x = (
        x,
        {"ctx": c - x + lax.rem(x + 1, 4)},
        {"ctx": c - x + lax.rem(x + 3, 4)},
    )
    along_z = (
        z,
        {"ctx": y * 16 + lax.rem(z + 1, 4) * 4 + x},
        {"ctx": y * 16 + lax.rem(z + 3, 4) * 4 + x},
    )
    return along_x, along_z


class RingGather:
    def __init__(self, block, first, second, ring, ssem, rsem):
        self.block, self.first, self.second = block, first, second
        self.p, self.up, self.down = ring
        self.ssem, self.rsem = ssem, rsem

    def at(self, k):
        return lax.rem(self.p + k, 4)

    def start(self):
        own = self.block(self.p)
        self.sent = [
            send(own, own, self.ssem(0), self.rsem(0), self.up),
            send(own, own, self.ssem(1), self.rsem(1), self.down),
        ]

    def forward(self):
        from_down, from_up = self.block(self.at(3)), self.block(self.at(1))
        remote(from_down, from_down, self.ssem(0), self.rsem(0), self.up).wait_recv()
        part = self.first(self.at(3))
        self.sent.append(send(part, part, self.ssem(2), self.rsem(2), self.up))
        remote(from_up, from_up, self.ssem(1), self.rsem(1), self.down).wait_recv()
        part = self.second(self.at(1))
        self.sent.append(send(part, part, self.ssem(3), self.rsem(3), self.down))

    def finish(self):
        part = self.first(self.at(2))
        remote(part, part, self.ssem(2), self.rsem(2), self.up).wait_recv()
        part = self.second(self.at(2))
        remote(part, part, self.ssem(3), self.rsem(3), self.down).wait_recv()
        for copy in self.sent:
            copy.wait_send()


def sems(ref, *lead):
    return lambda k: ref.at[(*lead, k)]


def rows16(index):
    return pl.ds(pl.multiple_of(index * 16, 16), 16)


def rows64(index):
    return pl.ds(pl.multiple_of(index * 64, 64), 64)


class WeightGather:
    STEPS = 7

    def __init__(self, src, dst, n, ls, os, orr, cs, cr, gs, gr, fs, fr):
        c, s, y, z, x = place()
        sibling, cross, unused = group_ids()
        self.sibling, self.cross = mesh_id(sibling), mesh_id(cross)
        self.src, self.dst, self.s = src, dst, s
        self.far, self.far_sib = cross[1], unused[1]
        self.sib_shard = sibling[1]
        self.ls, self.os, self.orr = ls.at[n], os.at[n], orr.at[n]
        self.cs, self.cr, self.fs, self.fr = cs, cr, fs, fr
        self.n = n
        width = src.shape[-1]
        self.half, self.quarter = width // 2, width // 4
        along_x, along_z = rings()
        self.streams = []
        for h in range(2):
            one, two = (along_z, along_x) if h == 0 else (along_x, along_z)
            base = x if h == 0 else z
            cols = pl.ds(h * self.half, self.half)
            cols_a = pl.ds(h * self.half, self.quarter)
            cols_b = pl.ds(h * self.half + self.quarter, self.quarter)
            own = self.dst.at[self.far]

            def small_block(p, cols=cols, base=base, own=own):
                return own.at[:, rows16(base * 4 + p), cols]

            def big_block(p, cols=cols, own=own):
                return own.at[:, rows64(p), cols]

            def part_of(make, cols):
                return lambda p: make(p, cols=cols)

            ring1 = RingGather(
                small_block, part_of(small_block, cols_a), part_of(small_block, cols_b), one,
                sems(gs, n, h, 0), sems(gr, n, h, 0),
            )
            ring2 = RingGather(
                big_block, part_of(big_block, cols_a), part_of(big_block, cols_b), two,
                sems(gs, n, h, 1), sems(gr, n, h, 1),
            )
            row = base * 4 + one[0]
            self.streams.append((h, row, cols, cols_a, cols_b, ring1, ring2, two[0]))
        self.sent = []

    def step(self, k):
        if k == 0:
            for h, row, cols, *unused in self.streams:
                self.sent.append(
                    send(
                        self.src.at[:, rows16(row), cols],
                        self.dst.at[self.s].at[:, rows16(row), cols],
                        self.cs.at[self.n, h], self.cr.at[self.n, h], self.cross,
                    )
                )
            self.local = pltpu.make_async_copy(self.src, self.dst.at[self.s], self.ls)
            self.local.start()
            self.own = send(self.src, self.dst.at[self.s], self.os, self.orr, self.sibling)
        elif k == 1:
            for h, row, cols, cols_a, cols_b, ring1, ring2, p in self.streams:
                got = self.dst.at[self.far].at[:, rows16(row), cols]
                remote(got, got, self.cs.at[self.n, h], self.cr.at[self.n, h], self.cross).wait_recv()
                ring1.start()
        elif k == 2:
            for h, row, cols, cols_a, cols_b, ring1, ring2, p in self.streams:
                ring1.forward()
        elif k == 3:
            for h, row, cols, cols_a, cols_b, ring1, ring2, p in self.streams:
                ring1.finish()
                ring2.start()
                self.pass_on(h, 0, rows64(p), cols)
        elif k == 4:
            for h, row, cols, cols_a, cols_b, ring1, ring2, p in self.streams:
                ring2.forward()
                self.pass_on(h, 1, rows64(lax.rem(p + 3, 4)), cols)
                self.pass_on(h, 2, rows64(lax.rem(p + 1, 4)), cols)
        elif k == 5:
            for h, row, cols, cols_a, cols_b, ring1, ring2, p in self.streams:
                ring2.finish()
                self.pass_on(h, 3, rows64(lax.rem(p + 2, 4)), cols)
        else:
            self.local.wait()
            self.own.wait_send()
            got = self.dst.at[self.sib_shard]
            remote(got, got, self.os, self.orr, self.sibling).wait_recv()
            for h, row, cols, cols_a, cols_b, ring1, ring2, p in self.streams:
                for j, shift in enumerate((0, 3, 1, 2)):
                    got = self.dst.at[self.far_sib].at[:, rows64(lax.rem(p + shift, 4)), cols]
                    remote(
                        got, got, self.fs.at[self.n, h, j], self.fr.at[self.n, h, j], self.sibling
                    ).wait_recv()
            for copy in self.sent:
                copy.wait_send()

    def pass_on(self, h, j, rows, cols):
        part = self.dst.at[self.far].at[:, rows, cols]
        self.sent.append(
            send(part, part, self.fs.at[self.n, h, j], self.fr.at[self.n, h, j], self.sibling)
        )


def weight_sems(count):
    dma = pltpu.SemaphoreType.DMA
    return [
        dma((count,)), dma((count,)), dma((count,)), dma((count, 2)), dma((count, 2)),
        dma((count, 2, 2, 4)), dma((count, 2, 2, 4)), dma((count, 2, 4)), dma((count, 2, 4)),
    ]


def group_ids():
    c = lax.axis_index("ctx")
    s = lax.axis_index("shard")
    core = lax.rem(s, 2)
    other = 2 - 2 * lax.div(s, 2)
    sibling = s + 1 - 2 * core
    cross_c = lax.rem(c + NC // 2, NC)
    return ((c, sibling), (cross_c, other + core), (cross_c, other + 1 - core))


def mesh_id(pair):
    return {"ctx": pair[0], "shard": pair[1]}


QB = 128


def widen(a):
    return a.astype(jnp.float32)


class RingReduce:
    def __init__(self, part, total, bufs, ring, ssem, rsem):
        self.part, self.total, self.bufs = part, total, bufs
        self.p, self.up, self.down = ring
        self.ssem, self.rsem = ssem, rsem

    def at(self, k):
        return lax.rem(self.p + k, 4)

    def start(self):
        ra, rb, sa, sb, from_down, from_up = self.bufs
        part, at, ssem, rsem = self.part, self.at, self.ssem, self.rsem
        up, down = self.up, self.down
        self.sent = [
            send(part(at(2), 0), ra, ssem(0), rsem(0), up),
            send(part(at(2), 1), rb, ssem(1), rsem(1), down),
            send(part(at(1), 1), from_down.at[2:4], ssem(2), rsem(2), up),
            send(part(at(3), 0), from_up.at[0:2], ssem(3), rsem(3), down),
        ]

    def middle(self):
        ra, rb, sa, sb, from_down, from_up = self.bufs
        part, at, ssem, rsem = self.part, self.at, self.ssem, self.rsem
        up, down = self.up, self.down
        self.sent[0].wait_recv()
        sa[...] = (widen(part(at(1), 0)[...]) + widen(ra[...])).astype(jnp.bfloat16)
        self.sent.append(send(sa, from_down.at[0:2], ssem(4), rsem(4), up))
        self.sent[1].wait_recv()
        sb[...] = (widen(part(at(3), 1)[...]) + widen(rb[...])).astype(jnp.bfloat16)
        self.sent.append(send(sb, from_up.at[2:4], ssem(5), rsem(5), down))

    def finish(self):
        from_down, from_up = self.bufs[4:]
        for copy in self.sent[2:]:
            copy.wait_recv()
        for k in range(2):
            half = pl.ds(2 * k, 2)
            self.total[half] = (
                widen(self.part(self.p, k)[...]) + widen(from_down[half]) + widen(from_up[half])
            ).astype(jnp.bfloat16)
        for copy in self.sent:
            copy.wait_send()


class SmallSums:
    STEPS = 4

    def __init__(self, parts, totals, landed, out, send_sem, recv_sem):
        c, unused_s, y, z, x = place()
        self.parts, self.totals, self.landed, self.out = parts, totals, landed, out
        self.ss, self.rs = send_sem, recv_sem
        self.targets = (
            [{"ctx": c - x + lax.rem(x + j, 4)} for j in range(1, 4)],
            [{"ctx": y * 16 + lax.rem(z + j, 4) * 4 + x} for j in range(1, 4)],
            [{"ctx": lax.rem(c + 16, 32)}],
        )

    def spread(self, k):
        self.sent = [
            send(
                self.totals.at[k], self.landed.at[k, j], self.ss.at[k, j], self.rs.at[k, j], target
            )
            for j, target in enumerate(self.targets[k])
        ]

    def step(self, k):
        if k == 0:
            self.totals[0] = self.parts[0] + self.parts[1] + self.parts[2] + self.parts[3]
            self.spread(0)
            return
        total = self.totals[k - 1]
        for j, copy in enumerate(self.sent):
            copy.wait()
            total = total + self.landed[k - 1, j]
        if k < 3:
            self.totals[k] = total
            self.spread(k)
        else:
            self.out[...] = total


class Stream:
    STEPS = 12

    def __init__(self, grad, out, m, h, scratch, dsems):
        (room, small, t2, ybuf, u, v) = scratch
        (p1s, p1r, p2s, p2r, ys, yr, ts, tr, ms, as_, ar, g1s, g1r, g2s, g2r) = dsems
        c, s, y, z, x = place()
        along_x, along_z = rings()
        one, two = (along_x, along_z) if h == 0 else (along_z, along_x)
        n = 2 * m + h
        self.m, self.c, self.s, self.y = m, c, s, y
        self.pair = {"ctx": lax.rem(c + 16, 32)}
        self.t1, self.t2, self.u, self.v = room(24 + n), t2.at[n], u.at[n], v.at[n]
        down, up, first, second = (room(4 * n + k) for k in range(4))
        big = (first.at[0:2], first.at[2:4], second.at[0:2], second.at[2:4], down, up)
        self.ybuf = ybuf.at[n]
        self.out = out
        self.ys, self.yr, self.ts, self.tr = ys.at[n], yr.at[n], ts.at[n], tr.at[n]
        self.ms, self.as_, self.ar = ms.at[n], as_.at[n], ar.at[n]
        cols = pl.ds(h * 512, 512)
        self.reduce1 = RingReduce(
            lambda p, k: grad.at[pl.ds(2 * k, 2), rows64(p), cols], self.t1,
            big, one, sems(p1s, n), sems(p1r, n),
        )
        self.reduce2 = RingReduce(
            lambda p, k: self.t1.at[pl.ds(2 * k, 2), rows16(p)], self.t2,
            [b.at[n] for b in small], two, sems(p2s, n), sems(p2r, n),
        )
        row = one[0] * 4 + two[0]

        def mine(who):
            at = pl.multiple_of(h * 512 + who * 256, 256)
            return out.at[:, rows16(row), pl.ds(at, 256)]

        self.mine = mine

        def small_block(p, lead=pl.ds(0, 4)):
            return out.at[lead, rows16(one[0] * 4 + p), cols]

        def big_block(p, lead=pl.ds(0, 4)):
            return out.at[lead, rows64(p), cols]

        def half_of(make, k):
            return lambda p: make(p, lead=pl.ds(2 * k, 2))

        self.gather1 = RingGather(
            small_block, half_of(small_block, 0), half_of(small_block, 1), two,
            sems(g1s, n), sems(g1r, n),
        )
        self.gather2 = RingGather(
            big_block, half_of(big_block, 0), half_of(big_block, 1), one,
            sems(g2s, n), sems(g2r, n),
        )

    def step(self, k):
        if k == 0:
            self.reduce1.start()
        elif k == 1:
            self.reduce1.middle()
        elif k == 2:
            self.reduce1.finish()
            self.reduce2.start()
        elif k == 3:
            self.reduce2.middle()
        elif k == 4:
            self.reduce2.finish()
            other = pl.ds(pl.multiple_of(256 - self.y * 256, 256), 256)
            self.sent_y = send(self.t2.at[:, :, other], self.ybuf, self.ys, self.yr, self.pair)
        elif k == 5:
            self.sent_y.wait()
            own = pl.ds(pl.multiple_of(self.y * 256, 256), 256)
            total = (widen(self.t2[:, :, own]) + widen(self.ybuf[...])).astype(jnp.bfloat16)
            if self.m == 0:
                self.v[...] = total
            else:
                self.u[...] = total
                self.turned = []
                for j in range(1, 4):
                    owner = lax.rem(self.s + j, 4)
                    self.turned.append(
                        send(
                            self.u.at[owner], self.v.at[self.s], self.ts.at[j], self.tr.at[j],
                            {"shard": owner},
                        )
                    )
                self.v[self.s] = self.u[self.s]
        elif k == 6:
            if self.m > 0:
                for j in range(1, 4):
                    source = lax.rem(self.s + 4 - j, 4)
                    got = self.v.at[source]
                    remote(got, got, self.ts.at[j], self.tr.at[j], {"shard": source}).wait_recv()
                    self.turned[j - 1].wait_send()
            self.kept = pltpu.make_async_copy(self.v, self.mine(self.y), self.ms)
            self.kept.start()
            self.shared = send(self.v, self.mine(self.y), self.as_, self.ar, self.pair)
        elif k == 7:
            self.kept.wait()
            self.shared.wait_send()
            got = self.mine(1 - self.y)
            remote(got, got, self.as_, self.ar, self.pair).wait_recv()
            self.gather1.start()
        elif k == 8:
            self.gather1.forward()
        elif k == 9:
            self.gather1.finish()
            self.gather2.start()
        elif k == 10:
            self.gather2.forward()
        else:
            self.gather2.finish()


def normalized(values):
    centered = values - jnp.mean(values, axis=-1, keepdims=True)
    scale = lax.rsqrt(jnp.mean(centered * centered, axis=-1, keepdims=True) + NORM_EPS)
    return centered * scale, scale


def norm_back(upstream, unit, scale):
    mean = jnp.mean(upstream, axis=-1, keepdims=True)
    along = jnp.mean(upstream * unit, axis=-1, keepdims=True)
    return scale * (upstream - mean - unit * along)


def layer_kernel(
    x, cot, b_qv, b_out, g_one, s_one, b_ff, g_two, s_two, b_in, w_qkv, w_out, w_in, w_ff,
    result, d_inputs, ff_out, in_out, qo_out, small_out,
    dproj_g, act_g, dpre_g, datt_g, hid_g, dbr_g, ctx_g, x_g, small_g,
    wq, wo, wi, wf, params, params_all, proj, q_send, q_recv, c_send, c_recv, g_send, g_recv,
    p_send, p_recv, keys, vt, kt, vals, dk, dv, o_s, lse_s, act, gelu_d, dpre, datt, dctx, dproj,
    hidden, unit_one, d_first, small, small_totals, small_landed,
    ra2, rb2, sa2, sb2, fd2, fu2, t2, ybuf, u, v,
    qss, qrs, css, crs, gss, grs, pss, prs, xs, xr, fs, fr, ls, es, er, els, ms, mr, sss, srs, *more
):
    bf, f32 = jnp.bfloat16, jnp.float32
    wsems, dsems = more[:9], more[9:]
    me = lax.axis_index("ctx")
    shard = lax.axis_index("shard")
    peers = group_ids()
    barrier = pltpu.get_barrier_semaphore()
    signal_ctx_peers(barrier, me)
    for peer in peers:
        pl.semaphore_signal(barrier, inc=1, device_id=mesh_id(peer), device_id_type=MESH)
    for peer in peers[1:]:
        pl.semaphore_signal(
            barrier, inc=1, device_id=mesh_id((me, peer[1])), device_id_type=MESH
        )
    x_g[0] = x[...]
    for n, ref in enumerate((b_out, g_one, s_one, b_ff, g_two, s_two)):
        params[2 * n : 2 * n + 2, :] = widen(ref[...])
    params[12:20, :] = widen(b_in[...])
    for n in range(2):
        for k in range(2):
            row = 20 + 2 * n + k
            params[row : row + 1, :] = widen(b_qv[n : n + 1, 128 * k : 128 * k + 128])
    params_all[shard] = params[...]
    pl.semaphore_wait(barrier, NC + 4)

    gather_q, *gathers = [
        WeightGather(w, out, n, *wsems)
        for n, (w, out) in enumerate(((w_qkv, wq), (w_out, wo), (w_in, wi), (w_ff, wf)))
    ]
    early, late = gathers[:2], gathers[2:]

    def advance(group, k):
        for gather in group:
            gather.step(k)

    def to_peer(src, dst, send_sem, recv_sem, peer):
        return send(src, dst, send_sem, recv_sem, mesh_id(peer))

    pending, arriving = {}, {}

    def share_whole(n, ref):
        pending[n] = [to_peer(ref.at[0], ref.at[1], xs.at[n, 0], xr.at[n, 0], peers[0])]
        arriving[n] = to_peer(ref.at[0], ref.at[2], xs.at[n, 1], xr.at[n, 1], peers[1])

    def pass_on(n, ref):
        arriving[n].wait()
        pending[n].append(to_peer(ref.at[2], ref.at[3], fs.at[n], fr.at[n], peers[0]))

    def share_slices(n, src, dst, width):
        cols = pl.ds(pl.multiple_of(shard * width, width), width)
        own = pltpu.make_async_copy(src.at[:, cols], dst.at[0], ls.at[n - 4])
        own.start()
        pending[n] = [own]
        for k, peer in enumerate(peers):
            cols = pl.ds(pl.multiple_of(peer[1] * width, 256), width)
            pending[n].append(
                to_peer(src.at[:, cols], dst.at[k + 1], xs.at[n, k], xr.at[n, k], peer)
            )

    def arrived(*which):
        for n in which:
            for copy in pending[n]:
                copy.wait()

    gather_q.step(0)
    sent_params = [
        to_peer(params, params_all.at[shard], ms.at[k], mr.at[k], peer)
        for k, peer in enumerate(peers)
    ]
    advance(gathers, 0)
    share_whole(3, x_g)
    gather_q.step(1)
    gather_q.step(2)
    gather_q.step(3)
    advance(gathers, 1)
    gather_q.step(4)
    advance(gathers, 2)
    gather_q.step(5)
    gather_q.step(6)
    advance(early, 3)
    for k, peer in enumerate(peers):
        sent_params[k].wait_send()
        got = params_all.at[peer[1]]
        remote(got, got, ms.at[k], mr.at[k], mesh_id(peer)).wait_recv()

    def vector(n):
        return jnp.concatenate(
            [params_all[k // 2, 2 * n + k % 2 : 2 * n + k % 2 + 1, :] for k in range(8)], axis=1
        )

    def cols_of(j):
        return pl.ds(pl.multiple_of(j * D, D), D)

    def project(j, carry):
        part = jnp.where(j == 0, 1.0, 0.0) * vector(10) + jnp.where(j == 2, 1.0, 0.0) * vector(11)
        weight = wq[:, 0, :, cols_of(j)].reshape(D, D)
        proj[:, cols_of(j)] = (dot_nn(x[...], weight) + part).astype(bf)
        return carry

    lax.fori_loop(0, 3, project, 0)
    pack_tokens(proj, q_send, 3)
    a2a_start(q_send, q_recv, qss, qrs, me)
    q_recv[me] = q_send[me]
    a2a_wait(q_send, q_recv, qss, qrs, me)
    advance(early, 4)
    advance(late, 3)
    keys[...] = halves(q_recv[:, 32:64, :].reshape(1024, 128))
    vals[...] = halves(q_recv[:, 64:96, :].reshape(1024, 128))
    vp = widen(q_recv[:, 64:96, :].reshape(1024, 128)).T.astype(bf)
    vt[...] = jnp.concatenate([vp[:64], vp[64:]], axis=1)
    kp = widen(q_recv[:, 32:64, :].reshape(1024, 128)).T.astype(bf)
    kt[...] = jnp.concatenate([kp[:64], kp[64:]], axis=1)
    steps = 1024 // QB
    blocks_of = QB // 32

    def attend(i, carry):
        blocks = pl.ds(i * blocks_of, blocks_of)
        qb = halves(q_recv[blocks, 0:32, :].reshape(QB, 128) * bf(SCALE))
        s = dot_nt(keys[...], qb)
        m = jnp.max(s, axis=0, keepdims=True)
        p = jnp.exp(s - m)
        total = jnp.sum(p, axis=0, keepdims=True)
        ot = dot_nn(vt[...], p.astype(bf)) / total
        o = jnp.concatenate([ot[:, :QB], ot[:, QB:]], axis=0).T
        o_s[pl.ds(pl.multiple_of(i * QB, QB), QB), :] = o
        lse_s[i] = m + jnp.log(total)
        c_send[blocks] = o.astype(bf).reshape(blocks_of, 32, 128)
        return carry

    lax.fori_loop(0, steps // 2, attend, 0)
    advance(early, 5)
    advance(late, 4)
    lax.fori_loop(steps // 2, steps, attend, 0)
    a2a_start(c_send, c_recv, css, crs, me)
    c_recv[me] = c_send[me]
    a2a_wait(c_send, c_recv, css, crs, me)
    unpack_tokens(c_recv, ctx_g.at[0], 1)
    share_whole(2, ctx_g)
    advance(early, 6)

    w_out_whole = wo[...].reshape(D, D)
    first_sum = widen(x[...]) + (dot_nn(ctx_g[0], w_out_whole) + vector(0))
    unit, scale_one = normalized(first_sum)
    unit_one[...] = unit
    hidden[...] = unit * vector(1) + vector(2)
    hid_g[0] = hidden[...].astype(bf)
    share_whole(0, hid_g)
    pass_on(3, x_g)

    def feed(j, carry):
        bias = jnp.concatenate([params_all[j, 12 + k : 13 + k, :] for k in range(8)], axis=1)
        pre = dot_nn(hid_g[0], wi[:, 0, :, cols_of(j)].reshape(D, D)) + bias
        grown = 0.5 * (1.0 + lax.erf(pre * 0.7071067811865476))
        act[:, cols_of(j)] = (pre * grown).astype(bf)
        gelu_d[:, cols_of(j)] = grown + pre * (0.3989422804014327 * jnp.exp(-0.5 * pre * pre))
        return carry

    lax.fori_loop(0, 4, feed, 0)
    share_slices(4, act, act_g, 1024)
    advance(late, 5)
    advance(late, 6)

    def feed_out(j, total):
        return total + dot_nn(act[:, cols_of(j)], wf[j].reshape(D, D))

    branch = lax.fori_loop(0, 4, feed_out, jnp.zeros((128, D), f32))
    unit_two, scale_two = normalized(hidden[...] + (branch + vector(3)))
    result[...] = (unit_two * vector(4) + vector(5)).astype(bf)

    def put_sums(n, values):
        sums = jnp.sum(values, axis=0, keepdims=True)
        for k in range(8):
            row = 2 * n + k % 2
            small[k // 2, row : row + 1, :] = sums[:, 128 * k : 128 * k + 128]

    upstream = widen(cot[...])
    put_sums(4, upstream * unit_two)
    put_sums(5, upstream)
    d_second = norm_back(upstream * vector(4), unit_two, scale_two)
    dbr_g[0] = d_second.astype(bf)
    share_whole(1, dbr_g)
    put_sums(3, widen(dbr_g[0]))

    def feed_back(j, total):
        d_act = dot_nt(dbr_g[0], wf[j].reshape(D, D))
        part = (d_act * gelu_d[:, cols_of(j)]).astype(bf)
        dpre[:, cols_of(j)] = part
        sums = jnp.sum(widen(part), axis=0, keepdims=True)
        for k in range(8):
            small[j, 12 + k : 13 + k, :] = sums[:, 128 * k : 128 * k + 128]
        return total + dot_nt(part, wi[:, 0, :, cols_of(j)].reshape(D, D))

    d_hidden = lax.fori_loop(0, 4, feed_back, d_second)
    share_slices(5, dpre, dpre_g, 1024)
    put_sums(1, d_hidden * unit_one[...])
    put_sums(2, d_hidden)
    d_first[...] = norm_back(d_hidden * vector(1), unit_one[...], scale_one)
    datt[...] = d_first[...].astype(bf)
    put_sums(0, widen(datt[...]))
    dctx[...] = dot_nt(datt[...], wo[...].reshape(D, D)).astype(bf)
    pack_tokens(dctx, g_send, 1)
    a2a_start(g_send, g_recv, gss, grs, me)
    share_slices(6, datt, datt_g, 256)
    g_recv[me] = g_send[me]
    dk[...] = jnp.zeros_like(dk)
    dv[...] = jnp.zeros_like(dv)
    pass_on(2, ctx_g)
    pass_on(0, hid_g)
    a2a_wait(g_send, g_recv, gss, grs, me)

    def room(k):
        return wi.at[:, 0, pl.ds(64 * (k % 4), 64), pl.ds(512 * (k // 4), 512)]

    scratch = (room, (ra2, rb2, sa2, sb2, fd2, fu2), t2, ybuf, u, v)

    def product(m, left, right, at):
        width = right.shape[-1]

        def block(q, carry):
            part = left[:, :, pl.ds(pl.multiple_of(q * 256, 256), 256)].reshape(512, 256)
            wf[m, q, :, at : at + width] = lax.dot_general(
                part, right[...].reshape(512, width), (((0,), (0,)), ((), ())),
                preferred_element_type=f32,
            ).astype(bf)
            return carry

        lax.fori_loop(0, 4, block, 0)

    def streams_of(m, out):
        streams = [Stream(wf.at[m], out, m, h, scratch, dsems) for h in range(2)]
        for stream in streams:
            stream.step(0)
        return streams

    def attend_back(i, carry):
        blocks = pl.ds(i * blocks_of, blocks_of)
        qb = halves(q_recv[blocks, 0:32, :].reshape(QB, 128) * bf(SCALE))
        dop = g_recv[blocks].reshape(QB, 128)
        o = o_s[pl.ds(pl.multiple_of(i * QB, QB), QB), :]
        prod = (widen(dop) * o).T
        delta = jnp.concatenate(
            [
                jnp.sum(prod[:64], axis=0, keepdims=True),
                jnp.sum(prod[64:], axis=0, keepdims=True),
            ],
            axis=1,
        )
        dob = halves(dop)
        probs = jnp.exp(dot_nt(keys[...], qb) - lse_s[i])
        dv[...] += dot_nn(probs.astype(bf), dob)
        ds = (probs * (dot_nt(vals[...], dob) - delta)).astype(bf)
        dk[...] += dot_nn(ds, qb)
        dqt = dot_nn(kt[...], ds) * SCALE
        dq = jnp.concatenate([dqt[:, :QB], dqt[:, QB:]], axis=0).T
        p_send[blocks, 0:32, :] = dq.astype(bf).reshape(blocks_of, 32, 128)
        return carry

    lax.fori_loop(0, steps // 2, attend_back, 0)
    pass_on(1, dbr_g)
    arrived(4, 1)
    product(0, act_g, dbr_g, 0)
    ff_streams = streams_of(0, ff_out)
    lax.fori_loop(steps // 2, steps, attend_back, 0)
    for n, total in enumerate((dk, dv)):
        packed = jnp.concatenate([total[0:1024, :], total[1024:2048, :]], axis=1)
        p_send[:, 32 + 32 * n : 64 + 32 * n, :] = packed.astype(bf).reshape(NC, 32, 128)
    a2a_start(p_send, p_recv, pss, prs, me)
    p_recv[me] = p_send[me]
    for stream in ff_streams:
        stream.step(1)
    arrived(0, 5)
    product(1, hid_g, dpre_g, 0)
    a2a_wait(p_send, p_recv, pss, prs, me)
    unpack_tokens(p_recv, dproj, 3)
    cols = pl.ds(pl.multiple_of(shard * 768, 256), 768)
    own = pltpu.make_async_copy(dproj.at[:, cols], dproj_g.at[0], els.at[0])
    own.start()
    pending[7] = [own]
    for k, peer in enumerate(peers):
        cols = pl.ds(pl.multiple_of(peer[1] * 768, 256), 768)
        pending[7].append(to_peer(dproj.at[:, cols], dproj_g.at[k + 1], es.at[k], er.at[k], peer))
    in_streams = streams_of(1, in_out)
    put_sums(10, widen(dproj[:, 0:D]))
    put_sums(11, widen(dproj[:, 2 * D : 3 * D]))
    small_g[0] = small[shard]
    pending[8] = [
        to_peer(small.at[peer[1]], small_g.at[k + 1], es.at[3 + k], er.at[3 + k], peer)
        for k, peer in enumerate(peers)
    ]
    for stream in ff_streams:
        stream.step(2)

    def back_in(j, total):
        weight = wq[:, 0, :, cols_of(j)].reshape(D, D)
        return total + dot_nt(dproj[:, cols_of(j)], weight)

    d_inputs[...] = lax.fori_loop(0, 3, back_in, d_first[...])
    for stream in in_streams:
        stream.step(1)
    arrived(2, 3, 6)
    product(2, ctx_g, datt_g, 768)
    arrived(7)
    product(2, x_g, dproj_g, 0)
    qo_streams = streams_of(2, qo_out)
    arrived(8)
    sums = SmallSums(small_g, small_totals, small_landed, small_out, sss, srs)
    sums.step(0)
    for k in range(1, Stream.STEPS):
        for streams, ahead in ((ff_streams, 2), (in_streams, 1), (qo_streams, 0)):
            if k + ahead < Stream.STEPS:
                for stream in streams:
                    stream.step(k + ahead)
        if k % 2 == 1 and k // 2 + 1 < SmallSums.STEPS:
            sums.step(k // 2 + 1)


def layer(x, cot, smalls, weights):
    bf, f32 = jnp.bfloat16, jnp.float32
    sds = jax.ShapeDtypeStruct
    dma = pltpu.SemaphoreType.DMA
    vm = pltpu.VMEM
    rows = (128, D)
    return pl.pallas_call(
        layer_kernel,
        out_shape=(
            sds(rows, bf), sds(rows, f32), sds((4, 256, 1024), bf), sds((4, 256, 1024), bf),
            sds((4, 256, 1024), bf), sds((24, 128), f32),
        ),
        in_specs=[VM] * 10 + [ANY] * 4,
        out_specs=(VM,) * 6,
        scratch_shapes=[
            vm((4, 128, 768), bf), vm((4, *rows), bf), vm((4, *rows), bf), vm((4, 128, 256), bf),
            vm((4, *rows), bf), vm((4, *rows), bf), vm((4, *rows), bf), vm((4, *rows), bf),
            vm((4, 24, 128), f32),
        ]
        + [vm((4, *w.shape), bf) for w in weights]
        + [
            vm((24, 128), f32), vm((4, 24, 128), f32), vm((128, 3 * D), bf),
            vm((NC, 96, 128), bf), vm((NC, 96, 128), bf), vm((NC, 32, 128), bf),
            vm((NC, 32, 128), bf), vm((NC, 32, 128), bf), vm((NC, 32, 128), bf),
            vm((NC, 96, 128), bf), vm((NC, 96, 128), bf), vm((2048, DH), bf),
            vm((DH, 2048), bf), vm((DH, 2048), bf), vm((2048, DH), bf), vm((2048, DH), f32),
            vm((2048, DH), f32), vm((1024, 128), f32), vm((1024 // QB, 1, 2 * QB), f32),
            vm((128, FF), bf), vm((128, FF), f32), vm((128, FF), bf), vm(rows, bf), vm(rows, bf),
            vm((128, 3 * D), bf), vm(rows, f32), vm(rows, f32), vm(rows, f32),
            vm((4, 24, 128), f32), vm((3, 24, 128), f32), vm((3, 3, 24, 128), f32),
        ]
        + [vm((6, 2, 16, 512), bf)] * 4
        + [vm((6, 4, 16, 512), bf)] * 3
        + [vm((6, 4, 16, 256), bf)] * 3
        + [dma((NC,))] * 8
        + [
            dma((7, 3)), dma((7, 3)), dma((4,)), dma((4,)), dma((3,)),
            dma((6,)), dma((6,)), dma((1,)), dma((3,)), dma((3,)), dma((3, 3)), dma((3, 3)),
        ]
        + weight_sems(4)
        + [
            dma((6, 6)), dma((6, 6)), dma((6, 6)), dma((6, 6)), dma((6,)), dma((6,)),
            dma((6, 4)), dma((6, 4)), dma((6,)), dma((6,)), dma((6,)),
            dma((6, 4)), dma((6, 4)), dma((6, 4)), dma((6, 4)),
        ],
        compiler_params=pltpu.CompilerParams(
            collective_id=0, has_side_effects=True, vmem_limit_bytes=62 * 1024 * 1024
        ),
    )(x, cot, *smalls, *weights)


def widen_kernel(ff, in_, qo, ff_out, in_out, qkv_out, w_out):
    ff_out[...] = widen(ff[0])
    in_out[...] = widen(in_[0])
    qkv_out[...] = widen(qo[0, :, :768])
    w_out[...] = widen(qo[0, :, 768:])


def widen_grads(ff, in_, qo):
    sds = jax.ShapeDtypeStruct
    f32 = jnp.float32
    block = pl.BlockSpec((1, 256, 1024), lambda q: (q, 0, 0))
    return pl.pallas_call(
        widen_kernel,
        grid=(4,),
        out_shape=(
            sds((1024, 1024), f32), sds((256, 4096), f32), sds((256, 3072), f32),
            sds((256, 1024), f32),
        ),
        in_specs=[block] * 3,
        out_specs=(
            pl.BlockSpec((256, 1024), lambda q: (q, 0)),
            pl.BlockSpec((256, 1024), lambda q: (0, q)),
            pl.BlockSpec((256, 768), lambda q: (0, q)),
            pl.BlockSpec((256, 256), lambda q: (0, q)),
        ),
        compiler_params=pltpu.CompilerParams(vmem_limit_bytes=VMEM_LIMIT),
    )(ff, in_, qo)


def local(
    inputs, cotangent, w_qkv, bias_qv, w_out, bias_out, ln1_gain, ln1_bias, w_in, bias_in,
    w_ff_out, bias_ff_out, ln2_gain, ln2_bias,
):
    smalls = (bias_out, ln1_gain, ln1_bias, bias_ff_out, ln2_gain, ln2_bias)
    result, d_inputs, red_ff, red_in, red_qo, sums = layer(
        inputs.reshape(128, D),
        cotangent.reshape(128, D),
        (bias_qv, *(a.reshape(2, 128) for a in smalls), bias_in.reshape(8, 128)),
        (
            w_qkv.reshape(1, 256, 3 * D), w_out.reshape(1, 256, D), w_in.reshape(1, 256, FF),
            w_ff_out.reshape(4, 256, D),
        ),
    )
    own_ff, own_in, own_qkv, own_out = widen_grads(red_ff, red_in, red_qo)
    sums = sums.reshape(3072)

    def own(k):
        return sums[256 * k : 256 * k + 256]

    return (
        result.reshape(inputs.shape),
        d_inputs.reshape(inputs.shape),
        own_qkv,
        sums[2560:].reshape(2, 256),
        own_out,
        own(0),
        own(1),
        own(2),
        own_in,
        sums[1536:2560],
        own_ff,
        own(3),
        own(4),
        own(5),
    )


def solution(mesh):
    specs = (
        P("shard", "ctx", None),
        P("shard", "ctx", None),
        P("shard", None),
        P(None, "shard"),
        P("shard", None),
        P("shard"),
        P("shard"),
        P("shard"),
        P("shard", None),
        P("shard"),
        P("shard", None),
        P("shard"),
        P("shard"),
        P("shard"),
    )
    return jax.shard_map(local, mesh=mesh, in_specs=specs, out_specs=specs, check_vma=False)
```

```python
import jax
import jax.numpy as jnp
from jax import lax
from jax.experimental import pallas as pl
from jax.experimental.pallas import tpu as pltpu
from jax.sharding import PartitionSpec as P

D = 1024
H = 16
DH = 64
FF = 4096
NC = 32
SCALE = DH ** (-0.5)
MESH = pl.DeviceIdType.MESH
NORM_EPS = 1e-05
VMEM_LIMIT = 56 * 1024 * 1024
VM = pl.BlockSpec(memory_space=pltpu.VMEM)
ANY = pl.BlockSpec(memory_space=pl.ANY)


def pack_tokens(src, send, parts):
    def step(hp, carry):
        for g in range(2):
            for part in range(parts):
                cols = pl.ds(pl.multiple_of(part * D + hp * 128, 128), 128)
                a = src[pl.ds(g * 64, 32), cols]
                b = src[pl.ds(g * 64 + 32, 32), cols]
                rows = pl.ds(part * 32, 32)
                send[g * 16 + 2 * hp, rows, :] = jnp.concatenate([a[:, :64], b[:, :64]], axis=1)
                send[g * 16 + 2 * hp + 1, rows, :] = jnp.concatenate(
                    [a[:, 64:], b[:, 64:]], axis=1
                )
        return carry

    lax.fori_loop(0, H // 2, step, 0)


def unpack_tokens(recv, dst, parts):
    def step(hp, carry):
        for g in range(2):
            for part in range(parts):
                cols = pl.ds(pl.multiple_of(part * D + hp * 128, 128), 128)
                rows = pl.ds(part * 32, 32)
                even = recv[g * 16 + 2 * hp, rows, :]
                odd = recv[g * 16 + 2 * hp + 1, rows, :]
                dst[pl.ds(g * 64, 32), cols] = jnp.concatenate([even[:, :64], odd[:, :64]], axis=1)
                dst[pl.ds(g * 64 + 32, 32), cols] = jnp.concatenate(
                    [even[:, 64:], odd[:, 64:]], axis=1
                )
        return carry

    lax.fori_loop(0, H // 2, step, 0)


def a2a_start(send, recv, ssem, rsem, me):
    def step(k, carry):
        dest = lax.rem(me + k, NC)
        pltpu.make_async_remote_copy(
            src_ref=send.at[dest],
            dst_ref=recv.at[me],
            send_sem=ssem,
            recv_sem=rsem,
            device_id={"ctx": dest},
            device_id_type=MESH,
        ).start()
        return carry

    lax.fori_loop(1, NC, step, 0)


def a2a_wait(send, recv, ssem, rsem, me):
    others = pl.ds(0, NC - 1)
    copy = pltpu.make_async_remote_copy(
        src_ref=send.at[others],
        dst_ref=recv.at[others],
        send_sem=ssem,
        recv_sem=rsem,
        device_id={"ctx": lax.rem(me + 1, NC)},
        device_id_type=MESH,
    )
    copy.wait_recv()
    copy.wait_send()


def signal_ctx_peers(barrier, me):
    def step(k, carry):
        pl.semaphore_signal(
            barrier, inc=1, device_id={"ctx": lax.rem(me + k, NC)}, device_id_type=MESH
        )
        return carry

    lax.fori_loop(1, NC, step, 0)


def halves(packed):
    return jnp.concatenate([packed[:, :64], packed[:, 64:]], axis=0)


def dot_nt(a, b):
    return lax.dot_general(a, b, (((1,), (1,)), ((), ())), preferred_element_type=jnp.float32)


def dot_nn(a, b):
    return jnp.dot(a, b, preferred_element_type=jnp.float32)


def place():
    c = lax.axis_index("ctx")
    return c, lax.axis_index("shard"), lax.div(c, 16), lax.rem(lax.div(c, 4), 4), lax.rem(c, 4)


def remote(src, dst, send_sem, recv_sem, peer):
    return pltpu.make_async_remote_copy(
        src_ref=src, dst_ref=dst, send_sem=send_sem, recv_sem=recv_sem,
        device_id=peer, device_id_type=MESH,
    )


def send(src, dst, send_sem, recv_sem, peer):
    copy = remote(src, dst, send_sem, recv_sem, peer)
    copy.start()
    return copy


def rings():
    c, unused_s, y, z, x = place()
    along_x = (x, *({"ctx": c - x + lax.rem(x + j, 4)} for j in range(1, 4)))
    along_z = (z, *({"ctx": y * 16 + lax.rem(z + j, 4) * 4 + x} for j in range(1, 4)))
    return along_x, along_z


class RingGather:
    def __init__(self, block, first, second, ring, ssem, rsem):
        self.block, self.first, self.second = block, first, second
        self.p, self.up, unused, self.down = ring
        self.ssem, self.rsem = ssem, rsem

    def at(self, k):
        return lax.rem(self.p + k, 4)

    def start(self):
        own = self.block(self.p)
        self.sent = [
            send(own, own, self.ssem(0), self.rsem(0), self.up),
            send(own, own, self.ssem(1), self.rsem(1), self.down),
        ]

    def forward(self):
        from_down, from_up = self.block(self.at(3)), self.block(self.at(1))
        remote(from_down, from_down, self.ssem(0), self.rsem(0), self.up).wait_recv()
        part = self.first(self.at(3))
        self.sent.append(send(part, part, self.ssem(2), self.rsem(2), self.up))
        remote(from_up, from_up, self.ssem(1), self.rsem(1), self.down).wait_recv()
        part = self.second(self.at(1))
        self.sent.append(send(part, part, self.ssem(3), self.rsem(3), self.down))

    def finish(self):
        part = self.first(self.at(2))
        remote(part, part, self.ssem(2), self.rsem(2), self.up).wait_recv()
        part = self.second(self.at(2))
        remote(part, part, self.ssem(3), self.rsem(3), self.down).wait_recv()
        for copy in self.sent:
            copy.wait_send()


class DirectGather:
    def __init__(self, block, ring, ssem, rsem):
        self.block, self.ring, self.ssem, self.rsem = block, ring, ssem, rsem

    def start(self):
        own = self.block(self.ring[0])
        self.sent = [
            send(own, own, self.ssem(j), self.rsem(j), self.ring[j]) for j in range(1, 4)
        ]

    def finish(self):
        for j in range(1, 4):
            got = self.block(lax.rem(self.ring[0] + 4 - j, 4))
            remote(got, got, self.ssem(j), self.rsem(j), self.ring[j]).wait_recv()
            self.sent[j - 1].wait_send()


def sems(ref, *lead):
    return lambda k: ref.at[(*lead, k)]


def rows16(index):
    return pl.ds(pl.multiple_of(index * 16, 16), 16)


def rows64(index):
    return pl.ds(pl.multiple_of(index * 64, 64), 64)


class WeightGather:
    def __init__(self, src, dst, n, ls, os, orr, cs, cr, gs, gr, fs, fr):
        c, s, y, z, x = place()
        sibling, cross, unused = group_ids()
        self.sibling, self.cross = mesh_id(sibling), mesh_id(cross)
        self.src, self.dst, self.s = src, dst, s
        self.far, self.far_sib = cross[1], unused[1]
        self.sib_shard = sibling[1]
        self.ls, self.os, self.orr = ls.at[n], os.at[n], orr.at[n]
        self.cs, self.cr, self.fs, self.fr = cs, cr, fs, fr
        self.n = n
        width = src.shape[-1]
        self.half, self.quarter = width // 2, width // 4
        along_x, along_z = rings()
        self.streams = []
        for h in range(2):
            one, two = (along_z, along_x) if h == 0 else (along_x, along_z)
            base = x if h == 0 else z
            cols = pl.ds(h * self.half, self.half)
            cols_a = pl.ds(h * self.half, self.quarter)
            cols_b = pl.ds(h * self.half + self.quarter, self.quarter)
            own = self.dst.at[self.far]

            def small_block(p, cols=cols, base=base, own=own):
                return own.at[:, rows16(base * 4 + p), cols]

            def big_block(p, cols=cols, own=own):
                return own.at[:, rows64(p), cols]

            def part_of(make, cols):
                return lambda p: make(p, cols=cols)

            ring1 = DirectGather(small_block, one, sems(gs, n, h, 0), sems(gr, n, h, 0))
            ring2 = RingGather(
                big_block, part_of(big_block, cols_a), part_of(big_block, cols_b), two,
                sems(gs, n, h, 1), sems(gr, n, h, 1),
            )
            row = base * 4 + one[0]
            self.streams.append((h, row, cols, cols_a, cols_b, ring1, ring2, two[0]))
        self.sent = []

    def step(self, k):
        if k == 0:
            for h, row, cols, *unused in self.streams:
                self.sent.append(
                    send(
                        self.src.at[:, rows16(row), cols],
                        self.dst.at[self.s].at[:, rows16(row), cols],
                        self.cs.at[self.n, h], self.cr.at[self.n, h], self.cross,
                    )
                )
        elif k == 1:
            for h, row, cols, cols_a, cols_b, ring1, ring2, p in self.streams:
                got = self.dst.at[self.far].at[:, rows16(row), cols]
                remote(got, got, self.cs.at[self.n, h], self.cr.at[self.n, h], self.cross).wait_recv()
                ring1.start()
        elif k == 2:
            for h, row, cols, cols_a, cols_b, ring1, ring2, p in self.streams:
                ring1.finish()
                ring2.start()
                self.pass_on(h, 0, rows64(p), cols)
        elif k == 3:
            for h, row, cols, cols_a, cols_b, ring1, ring2, p in self.streams:
                ring2.forward()
                self.pass_on(h, 1, rows64(lax.rem(p + 3, 4)), cols)
                self.pass_on(h, 2, rows64(lax.rem(p + 1, 4)), cols)
        elif k == 4:
            for h, row, cols, cols_a, cols_b, ring1, ring2, p in self.streams:
                ring2.finish()
                self.pass_on(h, 3, rows64(lax.rem(p + 2, 4)), cols)
        else:
            self.local.wait()
            self.own.wait_send()
            got = self.dst.at[self.sib_shard]
            remote(got, got, self.os, self.orr, self.sibling).wait_recv()
            for h, row, cols, cols_a, cols_b, ring1, ring2, p in self.streams:
                for j, shift in enumerate((0, 3, 1, 2)):
                    got = self.dst.at[self.far_sib].at[:, rows64(lax.rem(p + shift, 4)), cols]
                    remote(
                        got, got, self.fs.at[self.n, h, j], self.fr.at[self.n, h, j], self.sibling
                    ).wait_recv()
            for copy in self.sent:
                copy.wait_send()

    def share_own(self):
        self.local = pltpu.make_async_copy(self.src, self.dst.at[self.s], self.ls)
        self.local.start()
        self.own = send(self.src, self.dst.at[self.s], self.os, self.orr, self.sibling)

    def pass_on(self, h, j, rows, cols):
        part = self.dst.at[self.far].at[:, rows, cols]
        self.sent.append(
            send(part, part, self.fs.at[self.n, h, j], self.fr.at[self.n, h, j], self.sibling)
        )


def weight_sems(count):
    dma = pltpu.SemaphoreType.DMA
    return [
        dma((count,)), dma((count,)), dma((count,)), dma((count, 2)), dma((count, 2)),
        dma((count, 2, 2, 4)), dma((count, 2, 2, 4)), dma((count, 2, 4)), dma((count, 2, 4)),
    ]


def group_ids():
    c = lax.axis_index("ctx")
    s = lax.axis_index("shard")
    core = lax.rem(s, 2)
    other = 2 - 2 * lax.div(s, 2)
    sibling = s + 1 - 2 * core
    cross_c = lax.rem(c + NC // 2, NC)
    return ((c, sibling), (cross_c, other + core), (cross_c, other + 1 - core))


def mesh_id(pair):
    return {"ctx": pair[0], "shard": pair[1]}


QB = 128


def widen(a):
    return a.astype(jnp.float32)


class RingReduce:
    def __init__(self, part, total, bufs, ring, ssem, rsem):
        self.part, self.total, self.bufs = part, total, bufs
        self.p, self.up, unused, self.down = ring
        self.ssem, self.rsem = ssem, rsem

    def at(self, k):
        return lax.rem(self.p + k, 4)

    def start(self):
        ra, rb, sa, sb, from_down, from_up = self.bufs
        part, at, ssem, rsem = self.part, self.at, self.ssem, self.rsem
        up, down = self.up, self.down
        self.sent = [
            send(part(at(2), 0), ra, ssem(0), rsem(0), up),
            send(part(at(2), 1), rb, ssem(1), rsem(1), down),
            send(part(at(1), 1), from_down.at[2:4], ssem(2), rsem(2), up),
            send(part(at(3), 0), from_up.at[0:2], ssem(3), rsem(3), down),
        ]

    def middle(self):
        ra, rb, sa, sb, from_down, from_up = self.bufs
        part, at, ssem, rsem = self.part, self.at, self.ssem, self.rsem
        up, down = self.up, self.down
        self.sent[0].wait_recv()
        sa[...] = (widen(part(at(1), 0)[...]) + widen(ra[...])).astype(jnp.bfloat16)
        self.sent.append(send(sa, from_down.at[0:2], ssem(4), rsem(4), up))
        self.sent[1].wait_recv()
        sb[...] = (widen(part(at(3), 1)[...]) + widen(rb[...])).astype(jnp.bfloat16)
        self.sent.append(send(sb, from_up.at[2:4], ssem(5), rsem(5), down))

    def finish(self):
        from_down, from_up = self.bufs[4:]
        for copy in self.sent[2:]:
            copy.wait_recv()
        for k in range(2):
            half = pl.ds(2 * k, 2)
            self.total[half] = (
                widen(self.part(self.p, k)[...]) + widen(from_down[half]) + widen(from_up[half])
            ).astype(jnp.bfloat16)
        for copy in self.sent:
            copy.wait_send()


class DirectReduce:
    def __init__(self, part, total, landed, ring, ssem, rsem):
        self.part, self.total, self.landed, self.ring = part, total, landed, ring
        self.ssem, self.rsem = ssem, rsem

    def start(self):
        self.sent = [
            send(
                self.part(lax.rem(self.ring[0] + j, 4)), self.landed.at[j - 1], self.ssem(j),
                self.rsem(j), self.ring[j],
            )
            for j in range(1, 4)
        ]

    def finish(self):
        total = widen(self.part(self.ring[0])[...])
        for j, copy in enumerate(self.sent):
            copy.wait()
            total = total + widen(self.landed[j])
        self.total[...] = total.astype(jnp.bfloat16)


class SmallSums:
    STEPS = 4

    def __init__(self, parts, totals, landed, out, send_sem, recv_sem):
        c, unused_s, y, z, x = place()
        self.parts, self.totals, self.landed, self.out = parts, totals, landed, out
        self.ss, self.rs = send_sem, recv_sem
        self.targets = (
            [{"ctx": c - x + lax.rem(x + j, 4)} for j in range(1, 4)],
            [{"ctx": y * 16 + lax.rem(z + j, 4) * 4 + x} for j in range(1, 4)],
            [{"ctx": lax.rem(c + 16, 32)}],
        )

    def spread(self, k):
        self.sent = [
            send(
                self.totals.at[k], self.landed.at[k, j], self.ss.at[k, j], self.rs.at[k, j], target
            )
            for j, target in enumerate(self.targets[k])
        ]

    def step(self, k):
        if k == 0:
            self.totals[0] = self.parts[0] + self.parts[1] + self.parts[2] + self.parts[3]
            self.spread(0)
            return
        total = self.totals[k - 1]
        for j, copy in enumerate(self.sent):
            copy.wait()
            total = total + self.landed[k - 1, j]
        if k < 3:
            self.totals[k] = total
            self.spread(k)
        else:
            self.out[...] = total


class Stream:
    STEPS = 9

    def __init__(self, grad, out, m, h, scratch, dsems):
        (room, landed, t2, ybuf, u, v) = scratch
        (p1s, p1r, p2s, p2r, ys, yr, ts, tr, ms, g1s, g1r, g2s, g2r) = dsems
        c, s, y, z, x = place()
        along_x, along_z = rings()
        one, two = (along_x, along_z) if h == 0 else (along_z, along_x)
        n = 2 * m + h
        self.s = s
        self.pair = {"ctx": lax.rem(c + 16, 32)}
        self.t1, self.t2, self.u, self.v = room(24 + n), t2.at[n], u.at[n], v.at[n]
        down, up, first, second = (room(4 * n + k) for k in range(4))
        big = (first.at[0:2], first.at[2:4], second.at[0:2], second.at[2:4], down, up)
        self.ybuf = ybuf.at[n]
        self.ys, self.yr, self.ts, self.tr = ys.at[n], yr.at[n], ts.at[n], tr.at[n]
        self.ms = ms.at[n]
        cols = pl.ds(h * 512, 512)
        self.reduce1 = RingReduce(
            lambda p, k: grad.at[pl.ds(2 * k, 2), rows64(p), cols], self.t1,
            big, one, sems(p1s, n), sems(p1r, n),
        )
        self.reduce2 = DirectReduce(
            lambda p: self.t1.at[:, rows16(p)], self.t2, landed.at[n], two,
            sems(p2s, n), sems(p2r, n),
        )
        self.mine = out.at[:, rows16(one[0] * 4 + two[0]), cols]

        def small_block(p):
            return out.at[:, rows16(one[0] * 4 + p), cols]

        def big_block(p, lead=pl.ds(0, 4)):
            return out.at[lead, rows64(p), cols]

        def half_of(k):
            return lambda p: big_block(p, lead=pl.ds(2 * k, 2))

        self.gather1 = DirectGather(small_block, two, sems(g1s, n), sems(g1r, n))
        self.gather2 = RingGather(
            big_block, half_of(0), half_of(1), one, sems(g2s, n), sems(g2r, n)
        )

    def step(self, k):
        if k == 0:
            self.reduce1.start()
        elif k == 1:
            self.reduce1.middle()
        elif k == 2:
            self.reduce1.finish()
            self.reduce2.start()
        elif k == 3:
            self.reduce2.finish()
            self.sent_y = send(self.t2, self.ybuf, self.ys, self.yr, self.pair)
        elif k == 4:
            self.sent_y.wait()
            total = (widen(self.t2[...]) + widen(self.ybuf[...])).astype(jnp.bfloat16)
            self.u[...] = total
            self.turned = []
            for j in range(1, 4):
                owner = lax.rem(self.s + j, 4)
                self.turned.append(
                    send(
                        self.u.at[owner], self.v.at[self.s], self.ts.at[j], self.tr.at[j],
                        {"shard": owner},
                    )
                )
            self.v[self.s] = self.u[self.s]
        elif k == 5:
            for j in range(1, 4):
                source = lax.rem(self.s + 4 - j, 4)
                got = self.v.at[source]
                remote(got, got, self.ts.at[j], self.tr.at[j], {"shard": source}).wait_recv()
                self.turned[j - 1].wait_send()
            kept = pltpu.make_async_copy(self.v, self.mine, self.ms)
            kept.start()
            kept.wait()
            self.gather1.start()
        elif k == 6:
            self.gather1.finish()
            self.gather2.start()
        elif k == 7:
            self.gather2.forward()
        else:
            self.gather2.finish()


class PairFirst:
    def __init__(self, grad, out, h, scratch, landed, dsems, pass_s, pass_r):
        (room, landed2, t2, unused_y, unused_u, unused_v) = scratch
        (p1s, p1r, p2s, p2r, ys, yr, ts, tr, ms, g1s, g1r, g2s, g2r) = dsems
        c, s, y, z, x = place()
        along_x, along_z = rings()
        one, two = (along_x, along_z) if h == 0 else (along_z, along_x)
        self.p = one[0]
        self.grad, self.out, self.landed = grad, out, landed.at[h]
        self.pair = {"ctx": lax.rem(c + 16, 32)}
        self.own = pl.ds(pl.multiple_of(h * 512 + y * 256, 256), 256)
        self.other = pl.ds(pl.multiple_of(h * 512 + 256 - y * 256, 256), 256)
        own, other = self.own, self.other
        left = pl.ds(0, 256)
        self.t2 = t2.at[h, :, :, left]
        self.ys, self.yr, self.ms = ys.at[h], yr.at[h], ms.at[h]
        self.pass_s, self.pass_r = pass_s, pass_r
        self.h = h
        t1 = room(24 + h).at[:, :, left]
        down, up, first, second = (room(4 * h + k).at[:, :, left] for k in range(4))
        self.reduce1 = RingReduce(
            lambda p, k: grad.at[pl.ds(2 * k, 2), rows64(p), own], t1,
            (first.at[0:2], first.at[2:4], second.at[0:2], second.at[2:4], down, up),
            one, sems(p1s, h), sems(p1r, h),
        )
        self.reduce2 = DirectReduce(
            lambda p: t1.at[:, rows16(p)], self.t2, landed2.at[h, :, :, :, left], two,
            sems(p2s, h), sems(p2r, h),
        )
        self.mine = out.at[:, rows16(one[0] * 4 + two[0]), own]

        def big_block(p, lead=pl.ds(0, 4)):
            return out.at[lead, rows64(p), own]

        self.gather1 = DirectGather(
            lambda p: out.at[:, rows16(one[0] * 4 + p), own], two, sems(g1s, h), sems(g1r, h)
        )
        self.gather2 = RingGather(
            big_block, lambda p: big_block(p, lead=pl.ds(0, 2)),
            lambda p: big_block(p, lead=pl.ds(2, 2)), one, sems(g2s, h), sems(g2r, h),
        )
        self.passed = []

    def pass_on(self, j, shift):
        part = self.out.at[:, rows64(lax.rem(self.p + shift, 4)), self.own]
        self.passed.append(
            send(part, part, self.pass_s.at[self.h, j], self.pass_r.at[self.h, j], self.pair)
        )

    def step(self, k):
        if k == 0:
            self.sent_y = send(
                self.grad.at[:, :, self.other], self.landed, self.ys, self.yr, self.pair
            )
        elif k == 1:
            self.sent_y.wait()
            for q in range(4):
                total = widen(self.grad[q, :, self.own]) + widen(self.landed[q])
                self.grad[q, :, self.own] = total.astype(jnp.bfloat16)
            self.reduce1.start()
        elif k == 2:
            self.reduce1.middle()
        elif k == 3:
            self.reduce1.finish()
            self.reduce2.start()
        elif k == 4:
            self.reduce2.finish()
            kept = pltpu.make_async_copy(self.t2, self.mine, self.ms)
            kept.start()
            kept.wait()
            self.gather1.start()
        elif k == 5:
            self.gather1.finish()
            self.gather2.start()
            self.pass_on(0, 0)
        elif k == 6:
            self.gather2.forward()
            self.pass_on(1, 3)
            self.pass_on(2, 1)
        elif k == 7:
            self.gather2.finish()
            self.pass_on(3, 2)
        else:
            for j, shift in enumerate((0, 3, 1, 2)):
                got = self.out.at[:, rows64(lax.rem(self.p + shift, 4)), self.other]
                sems_at = self.pass_s.at[self.h, j], self.pass_r.at[self.h, j]
                remote(got, got, *sems_at, self.pair).wait_recv()
                self.passed[j].wait_send()


def normalized(values):
    centered = values - jnp.mean(values, axis=-1, keepdims=True)
    scale = lax.rsqrt(jnp.mean(centered * centered, axis=-1, keepdims=True) + NORM_EPS)
    return centered * scale, scale


def norm_back(upstream, unit, scale):
    mean = jnp.mean(upstream, axis=-1, keepdims=True)
    along = jnp.mean(upstream * unit, axis=-1, keepdims=True)
    return scale * (upstream - mean - unit * along)


def layer_kernel(
    x, cot, b_qv, b_out, g_one, s_one, b_ff, g_two, s_two, b_in, w_qkv, w_out, w_in, w_ff,
    result, d_inputs, ff_out, in_out, qo_out, small_out,
    dproj_g, act_g, dpre_g, datt_g, hid_g, dbr_g, ctx_g, x_g, small_g,
    wq, wo, wi, wf, params, params_all, proj, q_send, q_recv, c_send, c_recv, g_send, g_recv,
    p_send, p_recv, keys, vt, kt, vals, dk, dv, o_s, lse_s, act, gelu_d, dpre, datt, dctx, dproj,
    hidden, unit_one, d_first, small, small_totals, small_landed,
    landed1, landed2, t2, ybuf, u, v, pass_s, pass_r,
    qss, qrs, css, crs, gss, grs, pss, prs, xs, xr, fs, fr, ls, es, er, els, ms, mr, sss, srs, *more
):
    bf, f32 = jnp.bfloat16, jnp.float32
    wsems, dsems = more[:9], more[9:]
    me = lax.axis_index("ctx")
    shard = lax.axis_index("shard")
    peers = group_ids()
    barrier = pltpu.get_barrier_semaphore()
    signal_ctx_peers(barrier, me)
    for peer in peers:
        pl.semaphore_signal(barrier, inc=1, device_id=mesh_id(peer), device_id_type=MESH)
    for peer in peers[1:]:
        pl.semaphore_signal(
            barrier, inc=1, device_id=mesh_id((me, peer[1])), device_id_type=MESH
        )
    x_g[0] = x[...]
    for n, ref in enumerate((b_out, g_one, s_one, b_ff, g_two, s_two)):
        params[2 * n : 2 * n + 2, :] = widen(ref[...])
    params[12:20, :] = widen(b_in[...])
    for n in range(2):
        for k in range(2):
            row = 20 + 2 * n + k
            params[row : row + 1, :] = widen(b_qv[n : n + 1, 128 * k : 128 * k + 128])
    params_all[shard] = params[...]
    pl.semaphore_wait(barrier, NC + 4)

    gather_q, *gathers = [
        WeightGather(w, out, n, *wsems)
        for n, (w, out) in enumerate(((w_qkv, wq), (w_out, wo), (w_in, wi), (w_ff, wf)))
    ]
    early, late = gathers[:2], gathers[2:]

    def advance(group, k):
        for gather in group:
            gather.step(k)

    def to_peer(src, dst, send_sem, recv_sem, peer):
        return send(src, dst, send_sem, recv_sem, mesh_id(peer))

    pending, arriving = {}, {}

    def share_whole(n, ref):
        pending[n] = [to_peer(ref.at[0], ref.at[1], xs.at[n, 0], xr.at[n, 0], peers[0])]
        arriving[n] = to_peer(ref.at[0], ref.at[2], xs.at[n, 1], xr.at[n, 1], peers[1])

    def pass_on(n, ref):
        arriving[n].wait()
        pending[n].append(to_peer(ref.at[2], ref.at[3], fs.at[n], fr.at[n], peers[0]))

    def share_slices(n, src, dst, width):
        cols = pl.ds(pl.multiple_of(shard * width, width), width)
        own = pltpu.make_async_copy(src.at[:, cols], dst.at[0], ls.at[n - 4])
        own.start()
        pending[n] = [own]
        for k, peer in enumerate(peers):
            cols = pl.ds(pl.multiple_of(peer[1] * width, 256), width)
            pending[n].append(
                to_peer(src.at[:, cols], dst.at[k + 1], xs.at[n, k], xr.at[n, k], peer)
            )

    def arrived(*which):
        for n in which:
            for copy in pending[n]:
                copy.wait()

    gather_q.step(0)
    gather_q.share_own()
    sent_params = [
        to_peer(params, params_all.at[shard], ms.at[k], mr.at[k], peer)
        for k, peer in enumerate(peers)
    ]
    advance(gathers, 0)
    for k in range(1, 5):
        gather_q.step(k)
    advance(gathers, 1)
    gather_q.step(5)
    for gather in gathers:
        gather.share_own()
    share_whole(3, x_g)
    advance(early, 2)
    for k, peer in enumerate(peers):
        sent_params[k].wait_send()
        got = params_all.at[peer[1]]
        remote(got, got, ms.at[k], mr.at[k], mesh_id(peer)).wait_recv()

    def vector(n):
        return jnp.concatenate(
            [params_all[k // 2, 2 * n + k % 2 : 2 * n + k % 2 + 1, :] for k in range(8)], axis=1
        )

    def cols_of(j):
        return pl.ds(pl.multiple_of(j * D, D), D)

    def project(j, carry):
        part = jnp.where(j == 0, 1.0, 0.0) * vector(10) + jnp.where(j == 2, 1.0, 0.0) * vector(11)
        weight = wq[:, 0, :, cols_of(j)].reshape(D, D)
        proj[:, cols_of(j)] = (dot_nn(x[...], weight) + part).astype(bf)
        return carry

    lax.fori_loop(0, 3, project, 0)
    pack_tokens(proj, q_send, 3)
    a2a_start(q_send, q_recv, qss, qrs, me)
    q_recv[me] = q_send[me]
    a2a_wait(q_send, q_recv, qss, qrs, me)
    advance(early, 3)
    advance(late, 2)
    keys[...] = halves(q_recv[:, 32:64, :].reshape(1024, 128))
    vals[...] = halves(q_recv[:, 64:96, :].reshape(1024, 128))
    vp = widen(q_recv[:, 64:96, :].reshape(1024, 128)).T.astype(bf)
    vt[...] = jnp.concatenate([vp[:64], vp[64:]], axis=1)
    kp = widen(q_recv[:, 32:64, :].reshape(1024, 128)).T.astype(bf)
    kt[...] = jnp.concatenate([kp[:64], kp[64:]], axis=1)
    steps = 1024 // QB
    blocks_of = QB // 32

    def attend(i, carry):
        blocks = pl.ds(i * blocks_of, blocks_of)
        qb = halves(q_recv[blocks, 0:32, :].reshape(QB, 128) * bf(SCALE))
        s = dot_nt(keys[...], qb)
        m = jnp.max(s, axis=0, keepdims=True)
        p = jnp.exp(s - m)
        total = jnp.sum(p, axis=0, keepdims=True)
        ot = dot_nn(vt[...], p.astype(bf)) / total
        o = jnp.concatenate([ot[:, :QB], ot[:, QB:]], axis=0).T
        o_s[pl.ds(pl.multiple_of(i * QB, QB), QB), :] = o
        lse_s[i] = m + jnp.log(total)
        c_send[blocks] = o.astype(bf).reshape(blocks_of, 32, 128)
        return carry

    lax.fori_loop(0, steps // 2, attend, 0)
    advance(early, 4)
    advance(late, 3)
    lax.fori_loop(steps // 2, steps, attend, 0)
    a2a_start(c_send, c_recv, css, crs, me)
    c_recv[me] = c_send[me]
    a2a_wait(c_send, c_recv, css, crs, me)
    unpack_tokens(c_recv, ctx_g.at[0], 1)
    share_whole(2, ctx_g)
    advance(early, 5)

    w_out_whole = wo[...].reshape(D, D)
    first_sum = widen(x[...]) + (dot_nn(ctx_g[0], w_out_whole) + vector(0))
    unit, scale_one = normalized(first_sum)
    unit_one[...] = unit
    hidden[...] = unit * vector(1) + vector(2)
    hid_g[0] = hidden[...].astype(bf)
    share_whole(0, hid_g)
    pass_on(3, x_g)

    def feed(j, carry):
        bias = jnp.concatenate([params_all[j, 12 + k : 13 + k, :] for k in range(8)], axis=1)
        pre = dot_nn(hid_g[0], wi[:, 0, :, cols_of(j)].reshape(D, D)) + bias
        grown = 0.5 * (1.0 + lax.erf(pre * 0.7071067811865476))
        act[:, cols_of(j)] = (pre * grown).astype(bf)
        gelu_d[:, cols_of(j)] = grown + pre * (0.3989422804014327 * jnp.exp(-0.5 * pre * pre))
        return carry

    lax.fori_loop(0, 4, feed, 0)
    share_slices(4, act, act_g, 1024)
    advance(late, 4)
    advance(late, 5)

    def feed_out(j, total):
        return total + dot_nn(act[:, cols_of(j)], wf[j].reshape(D, D))

    branch = lax.fori_loop(0, 4, feed_out, jnp.zeros((128, D), f32))
    unit_two, scale_two = normalized(hidden[...] + (branch + vector(3)))
    result[...] = (unit_two * vector(4) + vector(5)).astype(bf)

    def put_sums(n, values):
        sums = jnp.sum(values, axis=0, keepdims=True)
        for k in range(8):
            row = 2 * n + k % 2
            small[k // 2, row : row + 1, :] = sums[:, 128 * k : 128 * k + 128]

    upstream = widen(cot[...])
    put_sums(4, upstream * unit_two)
    put_sums(5, upstream)
    d_second = norm_back(upstream * vector(4), unit_two, scale_two)
    dbr_g[0] = d_second.astype(bf)
    share_whole(1, dbr_g)
    put_sums(3, widen(dbr_g[0]))

    def feed_back(j, total):
        d_act = dot_nt(dbr_g[0], wf[j].reshape(D, D))
        part = (d_act * gelu_d[:, cols_of(j)]).astype(bf)
        dpre[:, cols_of(j)] = part
        sums = jnp.sum(widen(part), axis=0, keepdims=True)
        for k in range(8):
            small[j, 12 + k : 13 + k, :] = sums[:, 128 * k : 128 * k + 128]
        return total + dot_nt(part, wi[:, 0, :, cols_of(j)].reshape(D, D))

    d_hidden = lax.fori_loop(0, 4, feed_back, d_second)
    share_slices(5, dpre, dpre_g, 1024)
    put_sums(1, d_hidden * unit_one[...])
    put_sums(2, d_hidden)
    d_first[...] = norm_back(d_hidden * vector(1), unit_one[...], scale_one)
    datt[...] = d_first[...].astype(bf)
    put_sums(0, widen(datt[...]))
    dctx[...] = dot_nt(datt[...], wo[...].reshape(D, D)).astype(bf)
    pack_tokens(dctx, g_send, 1)
    a2a_start(g_send, g_recv, gss, grs, me)
    share_slices(6, datt, datt_g, 256)
    g_recv[me] = g_send[me]
    dk[...] = jnp.zeros_like(dk)
    dv[...] = jnp.zeros_like(dv)
    pass_on(2, ctx_g)
    pass_on(0, hid_g)
    a2a_wait(g_send, g_recv, gss, grs, me)

    def room(k):
        return wi.at[:, 0, pl.ds(64 * (k % 4), 64), pl.ds(512 * (k // 4), 512)]

    scratch = (room, landed2, t2, ybuf, u, v)

    def product(m, left, right, at):
        width = right.shape[-1]

        def block(q, carry):
            part = left[:, :, pl.ds(pl.multiple_of(q * 256, 256), 256)].reshape(512, 256)
            wf[m, q, :, at : at + width] = lax.dot_general(
                part, right[...].reshape(512, width), (((0,), (0,)), ((), ())),
                preferred_element_type=f32,
            ).astype(bf)
            return carry

        lax.fori_loop(0, 4, block, 0)

    def streams_of(m, out):
        if m == 0:
            streams = [
                PairFirst(wf.at[m], out, h, scratch, landed1, dsems, pass_s, pass_r)
                for h in range(2)
            ]
        else:
            streams = [Stream(wf.at[m], out, m, h, scratch, dsems) for h in range(2)]
        for stream in streams:
            stream.step(0)
        return streams

    def attend_back(i, carry):
        blocks = pl.ds(i * blocks_of, blocks_of)
        qb = halves(q_recv[blocks, 0:32, :].reshape(QB, 128) * bf(SCALE))
        dop = g_recv[blocks].reshape(QB, 128)
        o = o_s[pl.ds(pl.multiple_of(i * QB, QB), QB), :]
        prod = (widen(dop) * o).T
        delta = jnp.concatenate(
            [
                jnp.sum(prod[:64], axis=0, keepdims=True),
                jnp.sum(prod[64:], axis=0, keepdims=True),
            ],
            axis=1,
        )
        dob = halves(dop)
        probs = jnp.exp(dot_nt(keys[...], qb) - lse_s[i])
        dv[...] += dot_nn(probs.astype(bf), dob)
        ds = (probs * (dot_nt(vals[...], dob) - delta)).astype(bf)
        dk[...] += dot_nn(ds, qb)
        dqt = dot_nn(kt[...], ds) * SCALE
        dq = jnp.concatenate([dqt[:, :QB], dqt[:, QB:]], axis=0).T
        p_send[blocks, 0:32, :] = dq.astype(bf).reshape(blocks_of, 32, 128)
        return carry

    def proceed(streams, k):
        for stream in streams:
            stream.step(k)

    lax.fori_loop(0, steps // 4, attend_back, 0)
    pass_on(1, dbr_g)
    arrived(4, 1)
    product(0, act_g, dbr_g, 0)
    ff_streams = streams_of(0, ff_out)
    lax.fori_loop(steps // 4, steps // 2, attend_back, 0)
    proceed(ff_streams, 1)
    lax.fori_loop(steps // 2, steps // 4 * 3, attend_back, 0)
    proceed(ff_streams, 2)
    lax.fori_loop(steps // 4 * 3, steps, attend_back, 0)
    proceed(ff_streams, 3)
    for n, total in enumerate((dk, dv)):
        packed = jnp.concatenate([total[0:1024, :], total[1024:2048, :]], axis=1)
        p_send[:, 32 + 32 * n : 64 + 32 * n, :] = packed.astype(bf).reshape(NC, 32, 128)
    a2a_start(p_send, p_recv, pss, prs, me)
    p_recv[me] = p_send[me]
    proceed(ff_streams, 4)
    arrived(0, 5)
    product(1, hid_g, dpre_g, 0)
    in_streams = streams_of(1, in_out)
    proceed(ff_streams, 5)
    a2a_wait(p_send, p_recv, pss, prs, me)
    unpack_tokens(p_recv, dproj, 3)
    cols = pl.ds(pl.multiple_of(shard * 768, 256), 768)
    own = pltpu.make_async_copy(dproj.at[:, cols], dproj_g.at[0], els.at[0])
    own.start()
    pending[7] = [own]
    for k, peer in enumerate(peers):
        cols = pl.ds(pl.multiple_of(peer[1] * 768, 256), 768)
        pending[7].append(to_peer(dproj.at[:, cols], dproj_g.at[k + 1], es.at[k], er.at[k], peer))
    proceed(in_streams, 1)
    proceed(ff_streams, 6)
    put_sums(10, widen(dproj[:, 0:D]))
    put_sums(11, widen(dproj[:, 2 * D : 3 * D]))
    small_g[0] = small[shard]
    pending[8] = [
        to_peer(small.at[peer[1]], small_g.at[k + 1], es.at[3 + k], er.at[3 + k], peer)
        for k, peer in enumerate(peers)
    ]

    def back_in(j, total):
        weight = wq[:, 0, :, cols_of(j)].reshape(D, D)
        return total + dot_nt(dproj[:, cols_of(j)], weight)

    d_inputs[...] = lax.fori_loop(0, 3, back_in, d_first[...])
    proceed(in_streams, 2)
    proceed(ff_streams, 7)
    arrived(2, 3, 6)
    product(2, ctx_g, datt_g, 768)
    proceed(in_streams, 3)
    arrived(7)
    product(2, x_g, dproj_g, 0)
    qo_streams = streams_of(2, qo_out)
    proceed(in_streams, 4)
    arrived(8)
    sums = SmallSums(small_g, small_totals, small_landed, small_out, sss, srs)
    sums.step(0)
    proceed(qo_streams, 1)
    proceed(in_streams, 5)
    proceed(ff_streams, 8)
    proceed(qo_streams, 2)
    sums.step(1)
    proceed(in_streams, 6)
    proceed(qo_streams, 3)
    sums.step(2)
    proceed(qo_streams, 4)
    proceed(in_streams, 7)
    proceed(qo_streams, 5)
    sums.step(3)
    proceed(qo_streams, 6)
    proceed(in_streams, 8)
    proceed(qo_streams, 7)
    proceed(qo_streams, 8)


def layer(x, cot, smalls, weights):
    bf, f32 = jnp.bfloat16, jnp.float32
    sds = jax.ShapeDtypeStruct
    dma = pltpu.SemaphoreType.DMA
    vm = pltpu.VMEM
    rows = (128, D)
    return pl.pallas_call(
        layer_kernel,
        out_shape=(
            sds(rows, bf), sds(rows, f32), sds((4, 256, 1024), bf), sds((4, 256, 1024), bf),
            sds((4, 256, 1024), bf), sds((24, 128), f32),
        ),
        in_specs=[VM] * 10 + [ANY] * 4,
        out_specs=(VM,) * 6,
        scratch_shapes=[
            vm((4, 128, 768), bf), vm((4, *rows), bf), vm((4, *rows), bf), vm((4, 128, 256), bf),
            vm((4, *rows), bf), vm((4, *rows), bf), vm((4, *rows), bf), vm((4, *rows), bf),
            vm((4, 24, 128), f32),
        ]
        + [vm((4, *w.shape), bf) for w in weights]
        + [
            vm((24, 128), f32), vm((4, 24, 128), f32), vm((128, 3 * D), bf),
            vm((NC, 96, 128), bf), vm((NC, 96, 128), bf), vm((NC, 32, 128), bf),
            vm((NC, 32, 128), bf), vm((NC, 32, 128), bf), vm((NC, 32, 128), bf),
            vm((NC, 96, 128), bf), vm((NC, 96, 128), bf), vm((2048, DH), bf),
            vm((DH, 2048), bf), vm((DH, 2048), bf), vm((2048, DH), bf), vm((2048, DH), f32),
            vm((2048, DH), f32), vm((1024, 128), f32), vm((1024 // QB, 1, 2 * QB), f32),
            vm((128, FF), bf), vm((128, FF), f32), vm((128, FF), bf), vm(rows, bf), vm(rows, bf),
            vm((128, 3 * D), bf), vm(rows, f32), vm(rows, f32), vm(rows, f32),
            vm((4, 24, 128), f32), vm((3, 24, 128), f32), vm((3, 3, 24, 128), f32),
        ]
        + [vm((2, 4, 256, 256), bf), vm((6, 3, 4, 16, 512), bf)]
        + [vm((6, 4, 16, 512), bf)] * 4
        + [dma((2, 4)), dma((2, 4))]
        + [dma] * 8
        + [
            dma((7, 3)), dma((7, 3)), dma((4,)), dma((4,)), dma((3,)),
            dma((6,)), dma((6,)), dma((1,)), dma((3,)), dma((3,)), dma((3, 3)), dma((3, 3)),
        ]
        + weight_sems(4)
        + [
            dma((6, 6)), dma((6, 6)), dma((6, 4)), dma((6, 4)), dma((6,)), dma((6,)),
            dma((6, 4)), dma((6, 4)), dma((6,)), dma((6, 4)), dma((6, 4)), dma((6, 4)),
            dma((6, 4)),
        ],
        compiler_params=pltpu.CompilerParams(
            collective_id=0, has_side_effects=True, vmem_limit_bytes=62 * 1024 * 1024
        ),
    )(x, cot, *smalls, *weights)


def widen_kernel(ff, in_, qo, sums, ff_out, in_out, qkv_out, w_out, b_in, b_qv, *vectors):
    ff_out[...] = widen(ff[0])
    in_out[...] = widen(in_[0])
    qkv_out[...] = widen(qo[0, :, :768])
    w_out[...] = widen(qo[0, :, 768:])
    for n, ref in enumerate(vectors):
        ref[...] = sums[2 * n : 2 * n + 2, :]
    b_in[...] = sums[12:20, :]
    for n in range(2):
        for k in range(2):
            row = 20 + 2 * n + k
            b_qv[n : n + 1, 128 * k : 128 * k + 128] = sums[row : row + 1, :]


def widen_grads(ff, in_, qo, sums):
    sds = jax.ShapeDtypeStruct
    f32 = jnp.float32
    block = pl.BlockSpec((1, 256, 1024), lambda q: (q, 0, 0))

    def whole(shape):
        return pl.BlockSpec(shape, lambda q: (0, 0))

    return pl.pallas_call(
        widen_kernel,
        grid=(4,),
        out_shape=(
            sds((1024, 1024), f32), sds((256, 4096), f32), sds((256, 3072), f32),
            sds((256, 1024), f32), sds((8, 128), f32), sds((2, 256), f32),
        )
        + (sds((2, 128), f32),) * 6,
        in_specs=[block] * 3 + [whole((24, 128))],
        out_specs=(
            pl.BlockSpec((256, 1024), lambda q: (q, 0)),
            pl.BlockSpec((256, 1024), lambda q: (0, q)),
            pl.BlockSpec((256, 768), lambda q: (0, q)),
            pl.BlockSpec((256, 256), lambda q: (0, q)),
            whole((8, 128)),
            whole((2, 256)),
        )
        + (whole((2, 128)),) * 6,
        compiler_params=pltpu.CompilerParams(vmem_limit_bytes=VMEM_LIMIT),
    )(ff, in_, qo, sums)


def local(
    inputs, cotangent, w_qkv, bias_qv, w_out, bias_out, ln1_gain, ln1_bias, w_in, bias_in,
    w_ff_out, bias_ff_out, ln2_gain, ln2_bias,
):
    smalls = (bias_out, ln1_gain, ln1_bias, bias_ff_out, ln2_gain, ln2_bias)
    result, d_inputs, red_ff, red_in, red_qo, sums = layer(
        inputs.reshape(128, D),
        cotangent.reshape(128, D),
        (bias_qv, *(a.reshape(2, 128) for a in smalls), bias_in.reshape(8, 128)),
        (
            w_qkv.reshape(1, 256, 3 * D), w_out.reshape(1, 256, D), w_in.reshape(1, 256, FF),
            w_ff_out.reshape(4, 256, D),
        ),
    )
    own_ff, own_in, own_qkv, own_out, own_b_in, own_b_qv, *own = widen_grads(
        red_ff, red_in, red_qo, sums
    )
    own = [a.reshape(256) for a in own]
    return (
        result.reshape(inputs.shape),
        d_inputs.reshape(inputs.shape),
        own_qkv,
        own_b_qv,
        own_out,
        own[0],
        own[1],
        own[2],
        own_in,
        own_b_in.reshape(1024),
        own_ff,
        own[3],
        own[4],
        own[5],
    )


def solution(mesh):
    specs = (
        P("shard", "ctx", None),
        P("shard", "ctx", None),
        P("shard", None),
        P(None, "shard"),
        P("shard", None),
        P("shard"),
        P("shard"),
        P("shard"),
        P("shard", None),
        P("shard"),
        P("shard", None),
        P("shard"),
        P("shard"),
        P("shard"),
    )
    return jax.shard_map(local, mesh=mesh, in_specs=specs, out_specs=specs, check_vma=False)
```
